32 devices in a mesh: dp: 32 (over z, y, x, core).
Axes of the slice: x: 2, y: 2, z: 4, core: 2. Of those that a mesh axis runs over, the one named last changes fastest.
Arguments:
- tokens: bfloat16 [64, 320, 768], P('dp'), may hold values from -6 to 6
- lengths: int32 [64], P('dp'), may hold values from 157 to 314, as said below
- source: int32 [64], P('dp'), may hold values from 0 to 1, as said below
- cotangent: bfloat16 [64, 320, 768], P('dp'), may hold values from -6 to 6
- w_qkv: bfloat16 [768, 2304], P('dp'), may hold values from -0.21875 to 0.21875
- w_out: bfloat16 [768, 768], P(None, 'dp'), may hold values from -0.875 to 0.875
- w_up: bfloat16 [768, 3072], P('dp'), may hold values from -0.21875 to 0.21875
- w_down: bfloat16 [3072, 768], P(None, 'dp'), may hold values from -0.109375 to 0.109375
- gain_one: bfloat16 [768], P('dp'), may hold values from 0.25 to 1.75
- shift_one: bfloat16 [768], P('dp'), may hold values from -3 to 3
- bias_query: bfloat16 [768], P('dp'), may hold values from -2 to 2
- bias_value: bfloat16 [768], P('dp'), may hold values from -2 to 2
- bias_out: bfloat16 [768], P('dp'), may hold values from -2 to 2
- gain_two: bfloat16 [768], P('dp'), may hold values from 0.25 to 1.75
- shift_two: bfloat16 [768], P('dp'), may hold values from -3 to 3
- bias_up: bfloat16 [3072], P('dp'), may hold values from -2 to 2
- bias_down: bfloat16 [768], P('dp'), may hold values from -2 to 2
Outputs:
- mixed: bfloat16 [64, 320, 768], P('dp')
- grad_tokens: bfloat16 [64, 320, 768], P('dp')
- grad_qkv: float32 [768, 2304], P('dp')
- grad_out: float32 [768, 768], P(None, 'dp')
- grad_up: float32 [768, 3072], P('dp')
- grad_down: float32 [3072, 768], P(None, 'dp')
- grad_gain_one: float32 [768], P('dp')
- grad_shift_one: float32 [768], P('dp')
- grad_bias_query: float32 [768], P('dp')
- grad_bias_value: float32 [768], P('dp')
- grad_bias_out: float32 [768], P('dp')
- grad_gain_two: float32 [768], P('dp')
- grad_shift_two: float32 [768], P('dp')
- grad_bias_up: float32 [3072], P('dp')
- grad_bias_down: float32 [768], P('dp')
The draws below stay inside these ranges and needn't reach their ends.
Inputs may be any that keep to these rules, and one draw needn't show every extreme that they name: `lengths`: visible tokens of a video sequence; some video sequence has exactly 314. Grouped by source: images come first, then videos, each a quarter of the sequences or more.
All inputs are finite; a program needn't handle non-finite values.
Results may differ from the reference program's by a relative error of at most 0.012.
Values may be sent and summed in bfloat16 or wider, within the bound.
No kernel may reach another device: no remote copies, remote signals or barrier semaphores. Data moves between devices by JAX's collectives and lax.ppermute only.
A program may use at most 192 MiB of HBM per device.

```python
import jax
import jax.numpy as jnp
from jax import lax

HEADS = 12
HEAD_DIM = 64
D = 768
FF = 3072
IMG_LEN = 196
VID_MAX = 314
PAD = 320
SEQS = 64


def draw_lengths(key, part):
    key = jax.random.fold_in(key, 11)
    key_draw, key_peak = jax.random.split(key)
    drawn_lengths = jax.random.randint(key_draw, (SEQS,), VID_MAX // 2, VID_MAX + 1)
    peak_index = jax.random.randint(key_peak, (), 3 * SEQS // 4, SEQS)
    return jnp.where(jnp.arange(SEQS) == peak_index, VID_MAX, drawn_lengths).astype(jnp.int32)


def draw_source(key, part):
    key = jax.random.fold_in(key, 23)
    border = jax.random.randint(key, (), SEQS // 4, 3 * SEQS // 4 + 1)
    return (jnp.arange(SEQS) >= border).astype(jnp.int32)


def spiked(array, stream_key, source, target, shards_of, factor):
    owner, partner = [(jnp.arange(array.shape[axis_at]) // (array.shape[axis_at] // shards_of)).reshape([-1 if axis == axis_at else 1 for axis in range(array.ndim)]) for axis_at in (source, target)]
    chosen = jax.random.permutation(stream_key, shards_of)[partner]
    strong = (owner == chosen) | (owner == (partner + shards_of // 2) % shards_of)
    return jnp.where(strong, factor * array, array)


def steps_of(stream_key, dims, pieces, least, largest):
    def one(axis_at, blocks):
        steps = jax.random.uniform(jax.random.fold_in(jax.random.fold_in(stream_key, 6), axis_at), (blocks,), jnp.float32, least / len(pieces), largest / len(pieces))
        return jnp.repeat(jnp.exp(steps), dims[axis_at] // blocks).reshape((-1,) + (1,) * (len(dims) - axis_at - 1))

    gain = one(*pieces[0])
    for cut in pieces[1:]:
        gain = gain * one(*cut)
    return gain


def bell_draw(rng, extent, deviation, reach, cuts=(), kind=jnp.bfloat16):
    values = jax.random.normal(rng, extent, jnp.float32) * deviation
    if len(cuts) > 0:
        values = steps_of(rng, extent, cuts, -0.22, 0.18) * values
    return jnp.clip(values, min=-reach, max=reach).astype(kind)


def noise_with(own_key, dims, width, reach, cuts, heavy, held_as=jnp.bfloat16):
    drawn = width * jax.random.normal(own_key, dims, jnp.float32)
    if cuts:
        drawn = drawn * steps_of(own_key, dims, cuts, -0.22, 0.18)
    return jnp.clip(spiked(drawn, jax.random.fold_in(own_key, 3), *heavy), -reach, reach).astype(held_as)


def setup_inputs(seed: int = 0) -> dict:
    splits = jax.random.split(jax.random.key(seed), 18)
    return {
        "tokens": bell_draw(splits[0], (SEQS, PAD, D), 1.0, 6.0, ((0, 32),)),
        "lengths": draw_lengths(jax.random.fold_in(splits[17], 71), 0),
        "source": draw_source(jax.random.fold_in(splits[17], 71), 0),
        "cotangent": noise_with(splits[3], (SEQS, PAD, D), 1.0, 6.0, ((0, 32),), (0, 2, 32, 2.75)),
        "w_qkv": bell_draw(splits[4], (D, 3 * D), D ** -0.5, 0.21875, ((0, 32),)),
        "w_out": bell_draw(splits[5], (D, D), (D // 16) ** -0.5, 0.875, ((1, 32),)),
        "w_up": bell_draw(splits[6], (D, FF), D ** -0.5, 0.21875, ((0, 32),)),
        "w_down": bell_draw(splits[7], (FF, D), FF ** -0.5, 0.109375, ((1, 32),)),
        "gain_one": jnp.clip(1.0 + 0.15 * jax.random.normal(splits[8], (D,), jnp.float32), 0.25, 1.75).astype(jnp.bfloat16),
        "shift_one": bell_draw(splits[9], (D,), 0.5, 3.0, ((0, 32),)),
        "bias_query": bell_draw(splits[10], (D,), 0.3, 2.0, ((0, 32),)),
        "bias_value": bell_draw(splits[11], (D,), 0.3, 2.0, ((0, 32),)),
        "bias_out": bell_draw(splits[12], (D,), 0.3, 2.0, ((0, 32),)),
        "gain_two": jnp.clip(1.0 + 0.15 * jax.random.normal(splits[13], (D,), jnp.float32), 0.25, 1.75).astype(jnp.bfloat16),
        "shift_two": bell_draw(splits[14], (D,), 0.5, 3.0, ((0, 32),)),
        "bias_up": bell_draw(splits[15], (FF,), 0.3, 2.0, ((0, 32),)),
        "bias_down": bell_draw(splits[16], (D,), 0.3, 2.0, ((0, 32),)),
    }


@jax.custom_vjp
def low(v):
    return lax.optimization_barrier(v.astype(jnp.bfloat16)).astype(jnp.float32)

@jax.custom_vjp
def low_back(v):
    return v

def low_keep(v):
    return (low(v), None)

def low_pass(kept, grad):
    return (grad,)

def back_keep(v):
    return (v, None)

def back_low(kept, grad):
    return (low(grad),)
low.defvjp(low_keep, low_pass)
low_back.defvjp(back_keep, back_low)

def layer_norm(values, gain_vec, shift_vec):
    center = values - lax.optimization_barrier(jnp.mean(values, -1, keepdims=True))
    spread = lax.optimization_barrier(jnp.mean(center * center, -1, keepdims=True))
    return center * lax.rsqrt(spread + 1e-06) * gain_vec + shift_vec

def forward(inputs, key_keep, w_qkv, w_out, w_up, w_down, gain_one, shift_one, bias_query, bias_value, bias_out, gain_two, shift_two, bias_up, bias_down):
    seq_count, slot_count, model_width = inputs.shape
    highest = lax.Precision.HIGHEST
    normed_one = low(layer_norm(inputs, gain_one, shift_one))
    bias_all = jnp.concatenate([bias_query, jnp.zeros_like(bias_query), bias_value])
    triple = low(low_back(jnp.einsum('spd,de->spe', normed_one, w_qkv, precision=highest) + bias_all))
    head_shape = (seq_count, slot_count, HEADS, HEAD_DIM)
    query_rows = triple[:, :, :model_width].reshape(head_shape)
    key_rows = triple[:, :, model_width:2 * model_width].reshape(head_shape)
    value_rows = triple[:, :, 2 * model_width:].reshape(head_shape)
    scores = low_back(jnp.einsum('sqhe,skhe->shqk', query_rows, key_rows, precision=highest) * HEAD_DIM ** (-0.5))
    masked = jnp.where(key_keep[:, None, None, :], scores, -1e+30)
    weights_soft = low(jax.nn.softmax(masked, axis=-1))
    mixed_rows = low(low_back(jnp.einsum('shqk,skhe->sqhe', weights_soft, value_rows, precision=highest)))
    mixed_rows = mixed_rows.reshape(seq_count, slot_count, model_width)
    hidden = inputs + low_back(jnp.einsum('spd,de->spe', mixed_rows, w_out, precision=highest) + bias_out)
    normed_two = low(layer_norm(hidden, gain_two, shift_two))
    raised = low_back(jnp.einsum('spd,de->spe', normed_two, w_up, precision=highest) + bias_up)
    gated_rows = low(jax.nn.gelu(raised, approximate=True))
    return hidden + low_back(jnp.einsum('spd,de->spe', gated_rows, w_down, precision=highest) + bias_down)

def reference(tokens, lengths, source, cotangent, w_qkv, w_out, w_up, w_down, gain_one, shift_one, bias_query, bias_value, bias_out, gain_two, shift_two, bias_up, bias_down):
    visible = jnp.where(source == 1, lengths, IMG_LEN)
    key_keep = jnp.arange(PAD, dtype=jnp.int32)[None, :] < visible[:, None]
    group_size = 1
    for candidate in range(1, SEQS + 1):
        if SEQS % candidate == 0 and candidate * PAD <= 4096:
            group_size = candidate
    group_count = SEQS // group_size
    params = tuple((matrix.astype(jnp.float32) for matrix in (w_qkv, w_out, w_up, w_down, gain_one, shift_one, bias_query, bias_value, bias_out, gain_two, shift_two, bias_up, bias_down)))
    inputs_all = tokens.astype(jnp.float32).reshape(group_count, group_size, PAD, D)
    keep_all = key_keep.reshape(group_count, group_size, PAD)
    grads_all = (cotangent.astype(jnp.float32) * key_keep[:, :, None].astype(jnp.float32)).reshape(group_count, group_size, PAD, D)

    def step(totals, group):
        inputs, keep_rows, grad_rows = group

        def apply(group_inputs, *weights):
            return forward(group_inputs, keep_rows, *weights)
        output, pullback = jax.vjp(apply, inputs, *params)
        grads = pullback(grad_rows)
        new_totals = tuple((total + grad for total, grad in zip(totals, grads[1:])))
        return (new_totals, (output.astype(jnp.bfloat16), grads[0].astype(jnp.bfloat16)))
    zeros = tuple((jnp.zeros_like(matrix) for matrix in params))
    totals, (outputs, grad_inputs) = lax.scan(step, zeros, (inputs_all, keep_all, grads_all))
    mixed = outputs.reshape(SEQS, PAD, D)
    grad_tokens = grad_inputs.reshape(SEQS, PAD, D)
    return (mixed, grad_tokens, totals[0], totals[1], totals[2], totals[3], totals[4], totals[5], totals[6], totals[7], totals[8], totals[9], totals[10], totals[11], totals[12])
```

```python
import functools
import jax
import jax.numpy as jnp
from jax import lax
from jax.experimental import pallas as pl
from jax.experimental.pallas import tpu as pltpu
from jax.sharding import PartitionSpec as P

HEADS = 12
HEAD_DIM = 64
IMG_LEN = 196
EPS = 1e-06
D = 768
FF = 3072
HALF = D // 2
WIDE = FF // 2
LOW = jnp.bfloat16
F32 = jnp.float32
STEP = 384
ROWS = 64
SCALE = HEAD_DIM ** (-0.5)
CHUNKS = ((3 * HALF + 128, 640), (HALF + WIDE, 1024))
Z_CODES = (0, 4, 8, 12)
SMEM = pl.BlockSpec(memory_space=pltpu.SMEM)
ANY = pl.BlockSpec(memory_space=pl.ANY)
VMEM = pl.BlockSpec(memory_space=pltpu.VMEM)


def shape(dims, kind=LOW):
    return jax.ShapeDtypeStruct(dims, kind)


def whole(array):
    zeros = (0,) * len(array.shape)
    return pl.BlockSpec(tuple(array.shape), lambda *i: zeros)


def cols(array, width, offset=0):
    return pl.BlockSpec((array.shape[0], width), lambda *i: (0, offset + i[0]))


def fixed(array, width, index=0):
    return pl.BlockSpec((array.shape[0], width), lambda *i: (0, index))


class Chain:
    def __init__(self):
        self.last = None

    def __call__(
        self, body, outs, ins, *, info=None, grid=(1,), in_specs=None, out_specs=None, scratch=(), us=1.0
    ):
        head = [] if info is None else [info]
        ins = list(ins)
        count = len(head) + len(ins)
        in_specs = list(in_specs or [whole(a) for a in ins])
        out_specs = tuple(out_specs or [whole(o) for o in outs])
        if self.last is not None:
            ins.append(self.last)
            in_specs.append(ANY)
        total = len(head) + len(ins)

        def run(*refs):
            body(*refs[:count], *refs[total:])

        size = sum(a.size * a.dtype.itemsize for a in ins)
        size += sum(o.size * jnp.dtype(o.dtype).itemsize for o in outs)
        results = pl.pallas_call(
            run,
            out_shape=tuple(outs),
            grid_spec=pltpu.PrefetchScalarGridSpec(
                num_scalar_prefetch=len(head),
                grid=grid,
                in_specs=in_specs,
                out_specs=out_specs,
                scratch_shapes=list(scratch),
            ),
            compiler_params=pltpu.CompilerParams(
                vmem_limit_bytes=min(48, 12 + 2 * size // 2**20) * 2**20
            ),
            cost_estimate=pl.CostEstimate(
                flops=int(us * 1.1e9), bytes_accessed=size, transcendentals=0
            ),
        )(*head, *ins)
        self.last = min(results, key=lambda r: r.size * r.dtype.itemsize)
        return results


def dot(left, right, left_dim=1, right_dim=0):
    return lax.dot_general(
        left, right, (((left_dim,), (right_dim,)), ((), ())), preferred_element_type=F32
    )


def standardize(values):
    center = values - jnp.mean(values, -1, keepdims=True)
    scale = lax.rsqrt(jnp.mean(center * center, -1, keepdims=True) + EPS)
    return center * scale, scale


def row_loop(rows, body, init=0):
    def step(i, carry):
        return body(pl.ds(pl.multiple_of(i * ROWS, ROWS), ROWS), carry)

    return lax.fori_loop(0, rows // ROWS, step, init)


def swap(value, bit):
    pairs = [(i, i ^ bit) for i in range(32)]
    return lax.ppermute(value, "dp", pairs)


def pack_body(info, small, *refs):
    weights, (mine, other), (rows, *held, sem) = refs[:3], refs[3:5], refs[5:]
    copies = [pltpu.make_async_copy(w, v, sem) for w, v in zip(weights, held)]
    for copy in copies:
        copy.start()
    w_qkv, w_out, w_up = held
    rows[...] = jnp.zeros_like(rows)
    share = w_qkv.shape[0]
    rows[: small.shape[0], :share] = small[...].astype(F32)
    block = rows[...].T[:share, :].astype(LOW)
    for copy in copies:
        copy.wait()
    for flip, out in enumerate((mine, other)):
        h = info[1] ^ flip

        def half(weight, width, start=0):
            return weight[:, pl.ds(pl.multiple_of(start + h * width, 128), width)]

        for i in range(3):
            out[:, i * HALF : (i + 1) * HALF] = half(w_qkv, HALF, i * D)
        out[:, 3 * HALF : 3 * HALF + 128] = block
        at = CHUNKS[0][0]
        out[:, at : at + HALF] = half(w_out, HALF)
        out[:, at + HALF :] = half(w_up, WIDE)


def unit_body(info, mine, other, unit_one, unit_two, unit_a, unit_b):
    a, b = mine[...].astype(F32), other[...].astype(F32)
    unit = jnp.where(
        info[1] == 0, jnp.concatenate([a, b], 0), jnp.concatenate([b, a], 0)
    ).astype(LOW)
    start = at_a = at_b = 0
    for (width, cut), out in zip(CHUNKS, (unit_one, unit_two)):
        part = unit[:, start : start + width]
        out[...] = part
        unit_a[:, at_a : at_a + cut] = part[:, :cut]
        unit_b[:, at_b : at_b + width - cut] = part[:, cut:]
        start, at_a, at_b = start + width, at_a + cut, at_b + width - cut


def own_body(unit_a, far_a, unit_b, far_b, pair_a, pair_b):
    for pair, unit, far in ((pair_a, unit_a, far_a), (pair_b, unit_b, far_b)):
        pair[0] = unit[...]
        pair[1] = far[...]


def stack_body(cut, z_one, z_two, z_three, stack_a, stack_b):
    for i, piece in enumerate((z_one, z_two, z_three)):
        stack_a[i] = piece[:, :cut]
        stack_b[i] = piece[:, cut:]


def join_body(stack_a, far_a, stack_b, far_b, join_a, join_b):
    for join, stack, far in ((join_a, stack_a, far_a), (join_b, stack_b, far_b)):
        join[0:3] = stack[...]
        join[3:6] = far[...]


def place_body(plan, info, *refs):
    pieces, out, sem = refs[:-2], refs[-2], refs[-1]
    copies = []
    for piece, (codes, source, target, width) in zip(pieces, plan):
        for i, code in enumerate(codes):
            row = pl.multiple_of((info[0] ^ code) * 48, 48)
            copies.append(
                pltpu.make_async_copy(
                    piece.at[i, :, pl.ds(source, width)],
                    out.at[pl.ds(row, 48), pl.ds(target, width)],
                    sem,
                )
            )
    for copy in copies:
        copy.start()
    for copy in copies:
        copy.wait()


KEEP_A = tuple(c ^ y for y in (0, 2) for c in Z_CODES)
KEEP_B = tuple(c ^ x for x in (0, 1) for c in Z_CODES)
SEND_A = tuple(c ^ 1 for c in KEEP_A)
SEND_B = tuple(c ^ 2 for c in KEEP_B)


def spread(chip, grad, send, keep, send_codes, keep_codes):
    for out, codes in ((send, send_codes), (keep, keep_codes)):
        for i, code in enumerate(codes):
            row = pl.multiple_of((chip ^ code) * 48, 48)
            out[i] = grad[pl.ds(row, 48), :].astype(LOW)


def add(left, right):
    return (left.astype(F32) + right.astype(F32)).astype(LOW)


def first_sum_body(far_a, keep_a, far_b, keep_b, send_a, own_a, send_b, own_b):
    for far, keep, send, own in ((far_a, keep_a, send_a, own_a), (far_b, keep_b, send_b, own_b)):
        for i in range(4):
            send[i] = add(far[4 + i], keep[4 + i])
            own[i] = add(far[i], keep[i])


def second_sum_body(far_a, keep_a, far_b, keep_b, *outs):
    cut = keep_a.shape[2]
    for i, out in enumerate(outs):
        out[:, :cut] = add(far_a[i], keep_a[i])
        out[:, cut:] = add(far_b[i], keep_b[i])


def last_sum_body(info, own, z_one, z_two, z_three, mine, other, total):
    value = own[...].astype(F32)
    for piece in (z_one, z_two, z_three):
        value = value + piece[...].astype(F32)
    total[...] = value
    rows = mine.shape[0]
    mine[...] = total[pl.ds(pl.multiple_of(info[1] * rows, 8), rows), :]
    other[...] = total[pl.ds(pl.multiple_of((1 - info[1]) * rows, 8), rows), :]


def merge(info, mine, other, start, width, out, count=1):
    for flip, part in enumerate((mine, other)):
        h = info[1] ^ flip
        for i in range(count):
            at = pl.multiple_of((2 * i + h) * width, 128)
            out[:, pl.ds(at, width)] = part[:, start + i * width : start + (i + 1) * width]


def merge_down_body(info, mine, other, out):
    merge(info, mine, other, 0, WIDE, out)


def merge_up_body(info, mine, other, out_up, out_out):
    merge(info, mine, other, 0, WIDE, out_up)
    merge(info, mine, other, WIDE, HALF, out_out)


def merge_qkv_body(info, mine, other, out, vec):
    merge(info, mine, other, 0, HALF, out, 3)
    vec[...] = mine[:, 3 * HALF :] + other[:, 3 * HALF :]


def start_body(slots, visible, cot, dy, total):
    rows = cot.shape[0]
    total[...] = jnp.zeros_like(total)
    for s in range(rows // slots):
        live = lax.broadcasted_iota(jnp.int32, (slots, 1), 0) < visible[s]
        part = jnp.where(live, cot[s * slots : (s + 1) * slots, :].astype(F32), 0.0)
        dy[s * slots : (s + 1) * slots, :] = part.astype(LOW)
        total[0:1, :] += jnp.sum(part, 0, keepdims=True)


def qkv_body(info, tokens, own, par, normed, qkv_own, qkv_par, vecs):
    vecs[...] = own[:, 3 * HALF :].astype(F32).T[:16, :]

    def norm(at, carry):
        z, _ = standardize(tokens[at, :].astype(F32))
        normed[at, :] = (z * vecs[0:1, :] + vecs[1:2, :]).astype(LOW)
        return carry

    row_loop(tokens.shape[0], norm)
    for flip, (weight, out) in enumerate(((own, qkv_own), (par, qkv_par))):
        half = half_of(info, flip, HALF)
        for i in range(3):
            at = slice(i * STEP, (i + 1) * STEP)
            value = dot(normed[...], weight[:, at])
            if i != 1:
                value = value + vecs[6 + i // 2 : 7 + i // 2, half]
            out[:, at] = value.astype(LOW)


def soft_of(query, key, live):
    scores = jnp.where(live, dot(query, key, 1, 1) * SCALE, -1e30)
    power = jnp.exp(scores - jnp.max(scores, -1, keepdims=True))
    return power * (1.0 / jnp.sum(power, -1, keepdims=True))


def attend_body(slots, visible, qkv, out):
    rows = qkv.shape[0]
    lane = lax.broadcasted_iota(jnp.int32, (1, 128), 1)
    for s in range(rows // slots):
        at = slice(s * slots, (s + 1) * slots)
        live = lax.broadcasted_iota(jnp.int32, (1, slots), 1) < visible[s]
        for j in range(HALF // 128):
            query, key, value = (
                qkv[at, i * HALF + j * 128 : i * HALF + (j + 1) * 128] for i in range(3)
            )
            mixed = None
            for e in range(2):
                mine = (lane < HEAD_DIM) if e == 0 else (lane >= HEAD_DIM)
                soft = soft_of(jnp.where(mine, query, 0), key, live).astype(LOW)
                part = dot(soft, jnp.where(mine, value, 0))
                mixed = part if mixed is None else mixed + part
            out[at, j * 128 : (j + 1) * 128] = mixed.astype(LOW)


def hidden_body(tokens, vecs, o_own, o_par, own, par, hidden, normed):
    hidden[...] = dot(o_own[...], own[...], 1, 1) + dot(o_par[...], par[...], 1, 1)

    def norm(at, carry):
        value = tokens[at, :].astype(F32) + (hidden[at, :] + vecs[4:5, :])
        hidden[at, :] = value
        z, _ = standardize(value)
        normed[at, :] = (z * vecs[2:3, :] + vecs[3:4, :]).astype(LOW)
        return carry

    row_loop(tokens.shape[0], norm)


GELU_A = 0.7978845608028654
GELU_B = 0.044715


def raise_body(normed, dy, b_own, b_par, own, par, a_own, s_own, s_par, bundle):
    i = pl.program_id(0)

    @pl.when(i == 0)
    def _():
        bundle[:, :D] = dy[...]

    for bias, weight, slope in ((b_own, own, s_own), (b_par, par, s_par)):
        u = dot(normed[...], weight[...]) + bias[...]
        square = u * u
        t = jnp.tanh(u * (GELU_A + (GELU_A * GELU_B) * square))
        gated = u * (0.5 + 0.5 * t)
        curve = GELU_A + (3.0 * GELU_A * GELU_B) * square
        slope[...] = ((0.5 + 0.5 * t) + (gated * (1.0 - t)) * curve).astype(LOW)
        if weight is own:
            a_own[...] = gated.astype(LOW)
        else:
            at = pl.multiple_of(D + i * STEP, 128)
            bundle[:, pl.ds(at, STEP)] = gated.astype(LOW)


def half_of(info, flip, width):
    return pl.ds(pl.multiple_of((info[1] ^ flip) * width, 128), width)


def mix_body(info, hidden, vecs, a_own, bundle, weight, out):
    value = dot(a_own[...], weight[:, half_of(info, 0, WIDE)], 1, 1)
    value += dot(bundle[:, D:], weight[:, half_of(info, 1, WIDE)], 1, 1)
    out[...] = (hidden[...] + (value + vecs[5:6, :])).astype(LOW)


def raise_back_body(info, dy, normed, s_own, s_par, own, par, d_own, t_own, t_par, bundle):
    i = pl.program_id(0)

    @pl.when(i == 0)
    def _():
        bundle[:, :D] = normed[...]

    for slope, weight, total in ((s_own, own, t_own), (s_par, par, t_par)):
        value = (dot(dy[...], weight[...]) * slope[...].astype(F32)).astype(LOW)
        total[...] = jnp.sum(value.astype(F32), 0, keepdims=True)
        if weight is own:
            d_own[...] = value
        else:
            at = pl.multiple_of(D + i * STEP, 128)
            bundle[:, pl.ds(at, STEP)] = value


def norm_back(part, values, gain):
    z, scale = standardize(values)
    e = part * gain
    mean_e = jnp.mean(e, -1, keepdims=True)
    mean_ez = jnp.mean(e * z, -1, keepdims=True)
    return scale * (e - mean_e - z * mean_ez), z


def hidden_back_body(
    steps, dy, hidden, vecs, o_par, d_own, d_par, own, par, dh, bundle, sums, acc
):
    i = pl.program_id(0)
    part = dot(d_own[...], own[...], 1, 1) + dot(d_par[...], par[...], 1, 1)

    @pl.when(i == 0)
    def _():
        acc[...] = part

    @pl.when(i > 0)
    def _():
        acc[...] += part

    @pl.when(i == steps - 1)
    def _():
        bundle[:, D:] = o_par[...]

        def back(at, carry):
            part = acc[at, :]
            value, z = norm_back(part, hidden[at, :], vecs[2:3, :])
            value = dy[at, :].astype(F32) + value
            dh[at, :] = value
            low = value.astype(LOW)
            bundle[at, :D] = low
            gain, shift, bias = carry
            return (
                gain + jnp.sum(part * z, 0, keepdims=True),
                shift + jnp.sum(part, 0, keepdims=True),
                bias + jnp.sum(low.astype(F32), 0, keepdims=True),
            )

        zero = jnp.zeros((1, D), F32)
        totals = row_loop(acc.shape[0], back, (zero, zero, zero))
        for r in range(3):
            sums[r : r + 1, :] = totals[r]


def attend_back_body(slots, start, visible, normed, qkv, dp, out_weight, dqkv, sums, mixed):
    rows = qkv.shape[0]
    if start:
        dqkv[:, :start] = normed[...]
    mixed[...] = dot(dp[...], out_weight[...]).astype(LOW)
    lane = lax.broadcasted_iota(jnp.int32, (1, 128), 1)
    sums[...] = jnp.zeros_like(sums)
    for s in range(rows // slots):
        at = slice(s * slots, (s + 1) * slots)
        live = lax.broadcasted_iota(jnp.int32, (1, slots), 1) < visible[s]
        for j in range(HALF // 128):
            cols = [slice(i * HALF + j * 128, i * HALF + (j + 1) * 128) for i in range(3)]
            query, key, value = (qkv[at, c] for c in cols)
            grad = mixed[at, j * 128 : (j + 1) * 128]
            totals = [None] * 3
            for e in range(2):
                mine = (lane < HEAD_DIM) if e == 0 else (lane >= HEAD_DIM)
                query_e, key_e, grad_e = (jnp.where(mine, v, 0) for v in (query, key, grad))
                soft = soft_of(query_e, key, live)
                grad_soft = dot(grad_e, value, 1, 1)
                inner = jnp.sum(soft * grad_soft, -1, keepdims=True)
                grad_scores = (soft * (grad_soft - inner)).astype(LOW)
                parts = (
                    dot(grad_scores, key_e),
                    dot(grad_scores, query_e, 0, 0),
                    dot(soft.astype(LOW), grad_e, 0, 0),
                )
                totals = [p if t is None else t + p for t, p in zip(totals, parts)]
            for i, factor in enumerate((SCALE, SCALE, 1.0)):
                low = (totals[i] * factor).astype(LOW)
                dqkv[at, start + cols[i].start : start + cols[i].stop] = low
                if i != 1:
                    sums[i : i + 1, j * 128 : (j + 1) * 128] += jnp.sum(
                        low.astype(F32), 0, keepdims=True
                    )


def token_back_body(
    info, tokens, dh, vecs, sums_two, dy_sum, up_sum, sums_own, sums_par, d_own, d_par, own, par,
    out, block, acc, sums,
):
    acc[...] = dot(d_own[...], own[...], 1, 1) + dot(d_par[:, D:], par[...], 1, 1)

    def back(at, carry):
        part = acc[at, :]
        value, z = norm_back(part, tokens[at, :].astype(F32), vecs[0:1, :])
        out[at, :] = (dh[at, :] + value).astype(LOW)
        gain, shift = carry
        return (
            gain + jnp.sum(part * z, 0, keepdims=True),
            shift + jnp.sum(part, 0, keepdims=True),
        )

    zero = jnp.zeros((1, D), F32)
    totals = row_loop(acc.shape[0], back, (zero, zero))
    sums[...] = jnp.zeros_like(sums)
    for r in range(2):
        sums[r : r + 1, :] = totals[r]
    sums[2:5, :] = sums_two[0:3, :]
    sums[5:6, :] = dy_sum[0:1, :]
    for flip, part in enumerate((sums_own, sums_par)):
        half = half_of(info, flip, HALF)
        sums[6:7, half] = part[0:1, :]
        sums[7:8, half] = part[2:3, :]
    sums[8:12, :] = up_sum[...]
    block[...] = sums[...].T


def outer(left, left_far, right, right_far):
    return dot(left[...], right[...], 0, 0) + dot(left_far[...], right_far[...], 0, 0)


def down_grad_body(
    cut, chip_ref, left, left_far, right, right_far, send_a, keep_a, send_b, keep_b, grad
):
    i = pl.program_id(0)
    chip = chip_ref[0]
    grad[...] = outer(left, left_far, right, right_far)

    @pl.when(i < cut)
    def _():
        spread(chip, grad, send_a, keep_a, SEND_A, KEEP_A)

    @pl.when(i >= cut)
    def _():
        spread(chip, grad, send_b, keep_b, SEND_B, KEEP_B)


def up_grad_body(
    chip_ref, norm, norm_far, du, du_far, dp, dp_far, o, o_far, send_a, keep_a, send_b, keep_b, grad
):
    i = pl.program_id(0)
    chip = chip_ref[0]

    @pl.when(i < 4)
    def _():
        grad[...] = outer(norm, norm_far, du, du_far)

    @pl.when(i == 4)
    def _():
        grad[...] = outer(dp, dp_far, o, o_far)

    @pl.when(i < 2)
    def _():
        spread(chip, grad, send_a, keep_a, SEND_A, KEEP_A)

    @pl.when(i >= 2)
    def _():
        spread(chip, grad, send_b, keep_b, SEND_B, KEEP_B)


def qkv_grad_body(
    chip_ref, norm, dqkv, bundle, vecs, send_a, keep_a, send_b, keep_b, grad
):
    chip = chip_ref[0]
    for i in range(3):
        at = slice(i * STEP, (i + 1) * STEP)
        far = slice(D + i * STEP, D + (i + 1) * STEP)
        grad[...] = outer(norm, bundle.at[:, :D], dqkv.at[:, at], bundle.at[:, far])
        if i < 2:
            spread(chip, grad, send_a.at[:, :, at], keep_a.at[:, :, at], SEND_A, KEEP_A)
        else:
            cols = slice(0, STEP)
            spread(chip, grad, send_b.at[:, :, cols], keep_b.at[:, :, cols], SEND_B, KEEP_B)
    grad[:, 0:128] = vecs[...]
    cols = slice(STEP, STEP + 128)
    spread(
        chip, grad.at[:, 0:128], send_b.at[:, :, cols], keep_b.at[:, :, cols], SEND_B, KEEP_B
    )


def pick(flag, left, right):
    return jnp.where(flag, left, right)


def half_major(matrix):
    rows = matrix.shape[0]
    return matrix.reshape(rows, 3, 2, HALF).transpose(0, 2, 1, 3).reshape(rows, 3 * D)


def third_major(matrix):
    rows = matrix.shape[0]
    return matrix.reshape(rows, 2, 3, HALF).transpose(0, 2, 1, 3).reshape(rows, 3 * D)


class WholeComm:
    def __init__(self, count):
        self.info = jnp.zeros((2,), jnp.int32)

    def order(self, low, high):
        return low, high

    def weights(self, call, small, w_qkv, w_out, w_up, w_down):
        def gather(value):
            return lax.all_gather(value, "dp", axis=0, tiled=True)

        def half(matrix, h):
            width = matrix.shape[1] // 2
            return matrix[:, h * width : (h + 1) * width]

        block = gather(jnp.pad(small.T, ((0, 0), (0, 128 - small.shape[0]))))
        qkv, out, up = (gather(w) for w in (half_major(w_qkv), w_out, w_up))
        self.first = [jnp.concatenate([half(qkv, h), block], 1) for h in range(2)]
        self.second = [jnp.concatenate([half(out, h), half(up, h)], 1) for h in range(2)]
        return gather(w_down)

    def step(self, call):
        pass

    def first_weights(self, call):
        return self.first

    def middle(self, call):
        pass

    def second_weights(self, call):
        return self.second

    def pump(self, call):
        pass

    def reduce(self, value):
        return lax.psum_scatter(value, "dp", scatter_dimension=0, tiled=True)

    def reduce_down(self, call, dy, gated, bundle):
        self.down = self.reduce(dot(dy, jnp.concatenate([gated, bundle[:, D:]], 1), 0, 0))

    def reduce_up(self, call, normed, raised, up_bundle, mixed, out_bundle):
        raised = jnp.concatenate([raised, up_bundle[:, D:]], 1)
        mixed = jnp.concatenate([mixed, out_bundle[:, D:]], 1)
        self.up = (
            self.reduce(dot(normed, raised, 0, 0)),
            self.reduce(dot(out_bundle[:, :D], mixed, 0, 0)),
        )

    def reduce_qkv(self, call, normed, triple, bundle, block):
        triple = jnp.concatenate([triple, bundle[:, D:]], 1)
        self.qkv = third_major(self.reduce(dot(normed, triple, 0, 0))), self.reduce(block)

    def results(self, call):
        return self.down, *self.up, *self.qkv


class GridComm:
    def __init__(self):
        index = lax.axis_index("dp")
        self.info = jnp.stack([index >> 1, index & 1]).astype(jnp.int32)
        self.is_first = (index & 1) == 0
        self.jobs = []

    def order(self, low, high):
        return pick(self.is_first, low, high), pick(self.is_first, high, low)

    def weights(self, call, small, w_qkv, w_out, w_up, w_down):
        down = lax.all_gather(w_down, "dp", axis=0, tiled=True)
        rows = w_qkv.shape[0]
        total = sum(width for width, _ in CHUNKS)
        total_a = sum(cut for _, cut in CHUNKS)
        mine, other = call(
            pack_body,
            [shape((rows, total))] * 2,
            [small, w_qkv, w_out, w_up],
            info=self.info,
            in_specs=[whole(small)] + [ANY] * 3,
            scratch=[pltpu.VMEM((128, 128), F32)]
            + [pltpu.VMEM(w.shape, LOW) for w in (w_qkv, w_out, w_up)]
            + [pltpu.SemaphoreType.DMA],
        )
        *self.units, unit_a, unit_b = call(
            unit_body,
            [shape((48, w)) for w in [*(c[0] for c in CHUNKS), total_a, total - total_a]],
            [mine, swap(other, 1)],
            info=self.info,
        )
        self.own = [unit_a, swap(unit_a, 4), unit_b, swap(unit_b, 2)]
        self.lines = [[swap(self.units[0], bit) for bit in (8, 16, 24)]]
        return down

    def step(self, call):
        outs = [shape((2, *a.shape)) for a in self.own[::2]]
        self.pair_a, self.pair_b = call(own_body, outs, self.own)
        self.far_a, self.far_b = swap(self.pair_a, 2), swap(self.pair_b, 4)

    def stack(self, call, index):
        width, cut = CHUNKS[index]
        a, b = call(
            functools.partial(stack_body, cut),
            [shape((3, 48, cut)), shape((3, 48, width - cut))],
            self.lines[index],
        )
        return a, swap(a, 4), b, swap(b, 2)

    def join(self, call, index, stacked):
        width, cut = CHUNKS[index]
        a, b = call(
            join_body, [shape((6, 48, cut)), shape((6, 48, width - cut))], stacked
        )
        return a, swap(a, 2), b, swap(b, 4)

    def finish(self, call, index, joined):
        width, cut = CHUNKS[index]
        at_a = sum(c for _, c in CHUNKS[:index])
        at_b = sum(w - c for w, c in CHUNKS[:index])
        z = Z_CODES[1:]
        codes_a = z + tuple(c ^ 2 for c in z)
        codes_b = z + tuple(c ^ 1 for c in z)
        plan = [
            (codes_a, 0, 0, cut),
            (tuple(c ^ 1 for c in codes_a), 0, 0, cut),
            (codes_b, 0, cut, width - cut),
            (tuple(c ^ 2 for c in codes_b), 0, cut, width - cut),
            ((0, 2), at_a, 0, cut),
            ((1, 3), at_a, 0, cut),
            ((0, 1), at_b, cut, width - cut),
            ((2, 3), at_b, cut, width - cut),
        ]
        (own,) = call(
            functools.partial(place_body, plan),
            [shape((D, width))],
            [*joined, self.pair_a, self.far_a, self.pair_b, self.far_b],
            info=self.info,
            in_specs=[ANY] * 8,
            scratch=[pltpu.SemaphoreType.DMA],
        )
        return own, swap(own, 1)

    def first_weights(self, call):
        stacked = self.stack(call, 0)
        joined = self.join(call, 0, stacked)
        self.lines.append([swap(self.units[1], bit) for bit in (8, 16, 24)])
        first = self.finish(call, 0, joined)
        self.stacked = self.stack(call, 1)
        return first

    def middle(self, call):
        self.joined = self.join(call, 1, self.stacked)

    def second_weights(self, call):
        return self.finish(call, 1, self.joined)

    def pieces(self, width_a, width_b):
        return [shape((8, 48, w)) for w in (width_a, width_a, width_b, width_b)]

    def job(self, call, parts, body, outs):
        send_a, keep_a, send_b, keep_b = parts
        width_a, width_b = keep_a.shape[2], keep_b.shape[2]
        width = width_a + width_b
        far_a, far_b = swap(send_a, 2), swap(send_b, 4)
        yield
        send_a, keep_a, send_b, keep_b = call(
            first_sum_body,
            [shape((4, 48, w)) for w in (width_a, width_a, width_b, width_b)],
            [far_a, keep_a, far_b, keep_b],
        )
        far_a, far_b = swap(send_a, 4), swap(send_b, 2)
        yield
        own, *lines = call(
            second_sum_body, [shape((48, width))] * 4, [far_a, keep_a, far_b, keep_b]
        )
        lines = [swap(line, bit) for line, bit in zip(lines, (8, 16, 24))]
        yield
        mine, other = call(
            last_sum_body,
            [shape((24, width), F32)] * 2,
            [own, *lines],
            info=self.info,
            scratch=[pltpu.VMEM((48, width), F32)],
        )
        other = swap(other, 1)
        yield
        self.outs.append(
            call(body, outs, [mine, other], info=self.info)
        )

    def begin(self, call, parts, body, outs):
        job = self.job(call, parts, body, outs)
        next(job)
        self.jobs.append(job)

    def pump(self, call):
        self.jobs = [job for job in self.jobs if next(job, self) is not self]

    def results(self, call):
        while self.jobs:
            self.pump(call)
        (down,), (up, out), (qkv, vec) = self.outs
        return down, up, out, qkv, vec

    def reduce_down(self, call, dy, gated, bundle):
        self.outs = []
        far = swap(bundle, 1)
        out_a = pl.BlockSpec((8, 48, STEP), lambda i, _: (0, 0, jnp.minimum(i, 1)))
        out_b = pl.BlockSpec((8, 48, STEP), lambda i, _: (0, 0, jnp.maximum(i - 2, 0)))
        parts = call(
            functools.partial(down_grad_body, 2),
            self.pieces(768, 768),
            [dy, far, gated, far],
            info=self.info,
            grid=(4,),
            in_specs=[whole(dy), fixed(far, D), cols(gated, STEP), cols(far, STEP, 2)],
            out_specs=[out_a, out_a, out_b, out_b],
            scratch=[pltpu.VMEM((D, STEP), F32)],
            us=7,
        )
        self.begin(call, parts, merge_down_body, [shape((24, FF), F32)])

    def reduce_up(self, call, normed, raised, up_bundle, mixed, out_bundle):
        up_far, out_far = swap(up_bundle, 1), swap(out_bundle, 1)

        def part(array, offset=0):
            return pl.BlockSpec(
                (array.shape[0], STEP), lambda i, _: (0, offset + jnp.minimum(i, 3))
            )

        out_a = pl.BlockSpec((8, 48, STEP), lambda i, _: (0, 0, jnp.minimum(i, 1)))
        out_b = pl.BlockSpec((8, 48, STEP), lambda i, _: (0, 0, jnp.maximum(i - 2, 0)))
        parts = call(
            up_grad_body,
            self.pieces(768, 1152),
            [normed, up_far, raised, up_far, out_bundle, out_far, mixed, out_far],
            info=self.info,
            grid=(5,),
            in_specs=[
                whole(normed), fixed(up_far, D), part(raised), part(up_far, 2),
                fixed(out_bundle, D), fixed(out_far, D), whole(mixed), fixed(out_far, HALF, 2),
            ],
            out_specs=[out_a, out_a, out_b, out_b],
            scratch=[pltpu.VMEM((D, STEP), F32)],
            us=10,
        )
        self.begin(
            call, parts, merge_up_body, [shape((24, FF), F32), shape((24, D), F32)]
        )

    def reduce_qkv(self, call, normed, triple, bundle, block):
        parts = call(
            qkv_grad_body,
            self.pieces(768, 512),
            [normed, triple, swap(bundle, 1), block],
            info=self.info,
            scratch=[pltpu.VMEM((D, STEP), F32)],
            us=6.2,
        )
        self.begin(
            call, parts, merge_qkv_body, [shape((24, 3 * D), F32), shape((24, 128), F32)]
        )


def shards(count, tokens, lengths, source, cotangent, w_qkv, w_out, w_up, w_down, *small):
    (
        gain_one, shift_one, bias_query, bias_value, bias_out, gain_two, shift_two,
        bias_up, bias_down,
    ) = small
    seqs, slots = tokens.shape[:2]
    rows = seqs * slots
    share = gain_one.shape[0]
    call = Chain()
    comm = GridComm() if count == 32 else WholeComm(count)
    visible = jnp.where(source == 1, lengths, IMG_LEN)
    tokens = tokens.reshape(rows, D)

    act = shape((rows, D))
    act_f = shape((rows, D), F32)
    half = shape((rows, HALF))
    triple = shape((rows, 3 * HALF))
    wide = shape((rows, WIDE))
    bundle = shape((rows, D + WIDE))

    small = jnp.stack(
        [gain_one, shift_one, gain_two, shift_two, bias_out, bias_down, bias_query, bias_value]
    )
    small = jnp.concatenate([small, bias_up.reshape(4, share)])
    down = comm.weights(call, small, w_qkv, w_out.T, w_up, w_down.T)
    dy, dy_sum = call(
        functools.partial(start_body, slots),
        [act, shape((8, D), F32)],
        [cotangent.reshape(rows, D)],
        info=visible,
    )
    comm.step(call)
    first = comm.first_weights(call)
    normed_one, *qkv, vecs = call(
        qkv_body,
        [act, triple, triple, shape((16, D), F32)],
        [tokens, *first],
        info=comm.info,
        us=6.5,
    )
    comm.middle(call)
    bias_up = vecs[8:12].reshape(4, count, share).transpose(1, 0, 2).reshape(2, 1, WIDE)
    up_own, up_par = comm.order(bias_up[0], bias_up[1])
    o_own, o_par = [
        call(functools.partial(attend_body, slots), [half], [part], info=visible, us=4.3)[0]
        for part in qkv
    ]
    second = comm.second_weights(call)
    out_specs = [fixed(w, HALF) for w in second]
    hidden, normed_two = call(
        hidden_body,
        [act_f, act],
        [tokens, vecs, o_own, o_par, *second],
        in_specs=[whole(a) for a in (tokens, vecs, o_own, o_par)] + out_specs,
        us=4.4,
    )
    steps = WIDE // STEP
    up_specs = [cols(w, STEP, 1) for w in second]
    gate, step = cols(wide, STEP), cols(up_own, STEP)
    gated, *slope, down_bundle = call(
        raise_body,
        [wide] * 3 + [bundle],
        [normed_two, dy, up_own, up_par, *second],
        grid=(steps,),
        in_specs=[whole(act)] * 2 + [step] * 2 + up_specs,
        out_specs=[gate] * 3 + [whole(bundle)],
        us=11.3,
    )
    comm.reduce_down(call, dy, gated, down_bundle)
    down_specs = [
        pl.BlockSpec((D, STEP), lambda i, info: (0, info[1] * steps + i)),
        pl.BlockSpec((D, STEP), lambda i, info: (0, (1 - info[1]) * steps + i)),
    ]
    raised, up_sum_own, up_sum_par, up_bundle = call(
        raise_back_body,
        [wide] + [shape((1, WIDE), F32)] * 2 + [bundle],
        [dy, normed_two, *slope, down, down],
        info=comm.info,
        grid=(steps,),
        in_specs=[whole(act)] * 2 + [gate] * 2 + down_specs,
        out_specs=[gate, step, step, whole(bundle)],
        us=9,
    )
    comm.pump(call)
    out_bundle = shape((rows, D + HALF))
    grad_hidden, out_bundle, sums_two = call(
        functools.partial(hidden_back_body, steps),
        [act_f, out_bundle, shape((8, D), F32)],
        [dy, hidden, vecs, o_par, raised, up_bundle, *second],
        grid=(steps,),
        in_specs=[whole(act)] * 2
        + [whole(vecs), whole(o_par), gate, cols(up_bundle, STEP, 2)]
        + up_specs,
        out_specs=[whole(act), whole(out_bundle), pl.BlockSpec((8, D), lambda i: (0, 0))],
        scratch=[pltpu.VMEM((rows, D), F32)],
        us=10.7,
    )
    comm.pump(call)
    comm.reduce_up(call, normed_two, raised, up_bundle, o_own, out_bundle)
    grads = [None, None]
    for h in (1, 0):
        out = shape((rows, h * D + 3 * HALF))
        grads[h] = call(
            functools.partial(attend_back_body, slots, h * D),
            [out, shape((8, HALF), F32)],
            [normed_one, qkv[h], out_bundle, second[h]],
            info=visible,
            in_specs=[whole(normed_one), whole(triple), fixed(out_bundle, D), out_specs[h]],
            scratch=[pltpu.VMEM((rows, HALF), LOW)],
            us=9.5,
        )
        comm.pump(call)
    grad_own, grad_bundle = grads[0][0], grads[1][0]
    up_sum = jnp.concatenate(comm.order(up_sum_own[0], up_sum_par[0]))
    up_sum = up_sum.reshape(count, 4, share).transpose(1, 0, 2).reshape(4, D)
    grad_tokens, block = call(
        token_back_body,
        [act, shape((D, 128), F32)],
        [
            tokens, grad_hidden, vecs, sums_two, dy_sum, up_sum, grads[0][1], grads[1][1],
            grad_own, grad_bundle, *first,
        ],
        info=comm.info,
        in_specs=[
            whole(a)
            for a in (
                tokens, grad_hidden, vecs, sums_two, dy_sum, up_sum, grads[0][1], grads[1][1],
                grad_own, grad_bundle,
            )
        ]
        + [fixed(w, 3 * HALF) for w in first],
        scratch=[pltpu.VMEM((rows, D), F32), pltpu.VMEM((128, D), F32)],
        us=9.6,
    )
    comm.pump(call)
    comm.reduce_qkv(call, normed_one, grad_own, grad_bundle, block)
    (output,) = call(
        mix_body, [act], [hidden, vecs, gated, down_bundle, down], info=comm.info, us=4.7
    )
    g_down_t, g_up, g_out_t, g_qkv, g_vec = comm.results(call)
    (
        g_gain_one, g_shift_one, g_gain_two, g_shift_two, g_bias_out, g_bias_down, g_query, g_value,
    ) = [g_vec[:, i] for i in range(8)]
    return (
        output.reshape(seqs, slots, D),
        grad_tokens.reshape(seqs, slots, D),
        g_qkv,
        g_out_t.T,
        g_up,
        g_down_t.T,
        g_gain_one, g_shift_one, g_query, g_value, g_bias_out, g_gain_two, g_shift_two,
        g_vec[:, 8:12].T.reshape(4 * share),
        g_bias_down,
    )


def solution(mesh):
    row, tall, wide, vec = P("dp", None, None), P("dp", None), P(None, "dp"), P("dp")
    in_specs = (row, vec, vec, row, tall, wide, tall, wide) + (vec,) * 9
    out_specs = (row, row, tall, wide, tall, wide) + (vec,) * 9
    body = functools.partial(shards, mesh.shape["dp"])
    return jax.shard_map(
        body, mesh=mesh, in_specs=in_specs, out_specs=out_specs, check_vma=False
    )
```

```python
import functools
import jax
import jax.numpy as jnp
import numpy as np
from jax import lax
from jax.experimental import pallas as pl
from jax.experimental.pallas import tpu as pltpu
from jax.sharding import PartitionSpec as P

HEADS = 12
HEAD_DIM = 64
IMG_LEN = 196
EPS = 1e-06
D = 768
FF = 3072
HALF = D // 2
WIDE = FF // 2
LOW = jnp.bfloat16
F32 = jnp.float32
STEP = 384
ROWS = 64
MARGIN = 10
PACE = 4.0
UP_LANE = 32
SCALE = HEAD_DIM ** (-0.5)
CHUNKS = ((4 * HALF + 128, 896), (WIDE, 768), (WIDE, 768))
Z_CODES = (0, 4, 8, 12)
SMEM = pl.BlockSpec(memory_space=pltpu.SMEM)
ANY = pl.BlockSpec(memory_space=pl.ANY)
VMEM = pl.BlockSpec(memory_space=pltpu.VMEM)


def shape(dims, kind=LOW):
    return jax.ShapeDtypeStruct(dims, kind)


class Chain:
    def __init__(self, loose):
        self.last = None
        self.loose = loose

    def near(self, array):
        if any(array is a for a in self.loose):
            return array
        return pltpu.with_memory_space_constraint(array, pltpu.VMEM)

    def __call__(
        self, body, outs, ins, *, info=None, touch=(), in_hbm=(), scratch=(), us=8.0, last=False
    ):
        head = [] if info is None else [info]
        ins = list(ins)
        count = len(head) + len(ins)
        specs = [SMEM] * len(head) + [ANY if i in in_hbm else VMEM for i in range(len(ins))]
        given = [
            pltpu.with_memory_space_constraint(a, pltpu.HBM) if i in in_hbm else self.near(a)
            for i, a in enumerate(ins)
        ]
        extra = list(touch) + ([] if self.last is None else [self.last])
        total = count + len(extra)

        def run(*refs):
            body(*refs[:count], *refs[total:])

        held = sum(
            int(np.prod(k.shape)) * jnp.dtype(k.dtype).itemsize
            for k in scratch
            if getattr(k, "shape", ())
        )
        size = sum(a.size * a.dtype.itemsize for a in [*ins, *outs])
        results = pl.pallas_call(
            run,
            out_shape=tuple(outs if last else [pltpu.VMEM(o.shape, o.dtype) for o in outs]),
            in_specs=specs + [ANY] * len(extra),
            out_specs=(VMEM,) * len(outs),
            scratch_shapes=list(scratch),
            compiler_params=pltpu.CompilerParams(vmem_limit_bytes=held + MARGIN * 2**20),
            cost_estimate=pl.CostEstimate(
                flops=int(us * PACE * 1.1e9), bytes_accessed=size, transcendentals=0
            ),
        )(*head, *given, *extra)
        self.last = min(results, key=lambda r: r.size * r.dtype.itemsize)
        return results


def dot(left, right, left_dim=1, right_dim=0):
    return lax.dot_general(
        left, right, (((left_dim,), (right_dim,)), ((), ())), preferred_element_type=F32
    )


def standardize(values):
    center = values - jnp.mean(values, -1, keepdims=True)
    scale = lax.rsqrt(jnp.mean(center * center, -1, keepdims=True) + EPS)
    return center * scale, scale


def row_loop(rows, body, init=0):
    def step(i, carry):
        return body(pl.ds(pl.multiple_of(i * ROWS, ROWS), ROWS), carry)

    return lax.fori_loop(0, rows // ROWS, step, init)


def swap(value, bit):
    pairs = [(i, i ^ bit) for i in range(32)]
    return lax.ppermute(value, "dp", pairs)


def pack_body(info, small, bias_up, *refs):
    weights, (mine, other), (rows, *held, sem) = refs[:4], refs[4:6], refs[6:]
    copies = [pltpu.make_async_copy(w, v, sem) for w, v in zip(weights, held)]
    for copy in copies:
        copy.start()
    w_qkv, w_out, w_up, w_down = held
    rows[...] = jnp.zeros_like(rows)
    share = w_qkv.shape[0]
    rows[: small.shape[0], :share] = small[...].astype(F32)
    rows[...] = rows[...].T
    rows[0:1, UP_LANE : UP_LANE + 4 * share] = bias_up[...].astype(F32)
    block = rows[:share, :].astype(LOW)
    for copy in copies:
        copy.wait()
    for flip, out in enumerate((mine, other)):
        h = info[1] ^ flip

        def half(weight, width, start=0):
            return weight[:, pl.ds(pl.multiple_of(start + h * width, 128), width)]

        for i in range(3):
            out[:, i * HALF : (i + 1) * HALF] = half(w_qkv, HALF, i * D)
        out[:, 3 * HALF : 4 * HALF] = half(w_out, HALF)
        at = CHUNKS[0][0]
        out[:, 4 * HALF : at] = block
        out[:, at : at + WIDE] = half(w_up, WIDE)
        out[:, at + WIDE :] = half(w_down, WIDE)


def unit_body(info, mine, other, unit_one, unit_two, unit_three, unit_a, unit_b):
    a, b = mine[...].astype(F32), other[...].astype(F32)
    unit = jnp.where(
        info[1] == 0, jnp.concatenate([a, b], 0), jnp.concatenate([b, a], 0)
    ).astype(LOW)
    start = at_a = at_b = 0
    for (width, cut), out in zip(CHUNKS, (unit_one, unit_two, unit_three)):
        part = unit[:, start : start + width]
        out[...] = part
        unit_a[:, at_a : at_a + cut] = part[:, :cut]
        unit_b[:, at_b : at_b + width - cut] = part[:, cut:]
        start, at_a, at_b = start + width, at_a + cut, at_b + width - cut


def own_body(unit_a, far_a, unit_b, far_b, pair_a, pair_b):
    for pair, unit, far in ((pair_a, unit_a, far_a), (pair_b, unit_b, far_b)):
        width = pair.shape[2]
        pair[0] = unit[:, :width]
        pair[1] = far[:, :width]


def pair_body(unit, far, pair):
    pair[0] = unit[...]
    pair[1] = far[...]


def stack_body(cut, *refs):
    pieces, (stack_a, stack_b) = refs[:-2], refs[-2:]
    at = 0
    for piece in pieces:
        for i in range(piece.shape[0] if len(piece.shape) == 3 else 1):
            part = piece.at[i] if len(piece.shape) == 3 else piece
            stack_a[at] = part[:, :cut]
            stack_b[at] = part[:, cut:]
            at += 1


def join_body(start_a, start_b, *refs):
    stacks, own, (join_a, join_b) = refs[:4], refs[4:-2], refs[-2:]
    for side, join, start in ((0, join_a, start_a), (1, join_b, start_b)):
        width = join.shape[2]
        parts = own[2 * side : 2 * side + 2]
        for i, part in enumerate(parts):
            join[i] = part[:, start : start + width]
        at = len(parts)
        join[at : at + 3] = stacks[2 * side][...]
        join[at + 3 : at + 6] = stacks[2 * side + 1][...]


def place_body(plan, info, *refs):
    pieces, out, sem = refs[:-2], refs[-2], refs[-1]
    copies = []
    for piece, (codes, source, target, width) in zip(pieces, plan):
        for i, code in enumerate(codes):
            row = pl.multiple_of((info[0] ^ code) * 48, 48)
            copies.append(
                pltpu.make_async_copy(
                    piece.at[i, :, pl.ds(source, width)],
                    out.at[pl.ds(row, 48), pl.ds(target, width)],
                    sem,
                )
            )
    for copy in copies:
        copy.start()
    for copy in copies:
        copy.wait()


ORDER = (1, 2, 3, 0, 1, 3, 2, 0, 1, 3, 3, 1, 2, 3, 2)
KEEP_A = tuple(c ^ y for y in (0, 2) for c in Z_CODES)
KEEP_B = tuple(c ^ x for x in (0, 1) for c in Z_CODES)
SEND_A = tuple(c ^ 1 for c in KEEP_A)
SEND_B = tuple(c ^ 2 for c in KEEP_B)


def spread(chip, grad, send, keep, send_codes, keep_codes):
    for out, codes in ((send, send_codes), (keep, keep_codes)):
        for i, code in enumerate(codes):
            row = pl.multiple_of((chip ^ code) * 48, 48)
            out[i] = grad[pl.ds(row, 48), :].astype(out.dtype)


def add(left, right):
    return (left.astype(F32) + right.astype(F32)).astype(LOW)


def first_sum_body(far_a, keep_a, far_b, keep_b, send_a, own_a, send_b, own_b):
    for far, keep, send, own in ((far_a, keep_a, send_a, own_a), (far_b, keep_b, send_b, own_b)):
        for i in range(4):
            send[i] = add(far[4 + i], keep[4 + i])
            own[i] = add(far[i], keep[i])


def second_sum_body(far_a, keep_a, far_b, keep_b, *outs):
    cut = keep_a.shape[2]
    for i in range(4):
        out = outs[i] if len(outs) == 4 else outs[i % 2].at[i // 2]
        out[:, :cut] = add(far_a[i], keep_a[i])
        out[:, cut:] = add(far_b[i], keep_b[i])


def last_sum_body(info, own, z_one, z_two, z_three, mine, other, total):
    value = own[...].astype(F32)
    for piece in (z_one, z_two, z_three):
        value = value + piece[...].astype(F32)
    total[...] = value
    split_rows(info, total, mine, other)


def split_rows(info, total, mine, other):
    rows = mine.shape[0]
    mine[...] = total[pl.ds(pl.multiple_of(info[1] * rows, 8), rows), :]
    other[...] = total[pl.ds(pl.multiple_of((1 - info[1]) * rows, 8), rows), :]


def merge(info, mine, other, start, width, out, count=1):
    for flip, part in enumerate((mine, other)):
        h = info[1] ^ flip
        for i in range(count):
            at = pl.multiple_of((2 * i + h) * width, 128)
            out[:, pl.ds(at, width)] = part[:, start + i * width : start + (i + 1) * width]


def merge_one_body(info, mine, other, out):
    merge(info, mine, other, 0, WIDE, out)


def merge_qkv_body(info, mine, other, out_qkv, out_out):
    merge(info, mine, other, 0, HALF, out_qkv, 3)
    merge(info, mine, other, 3 * HALF, HALF, out_out)


def near_sum_body(own, far, keep, send):
    keep[...] = add(own[0], far[0])
    send[...] = add(own[1], far[1])


def last_near_body(info, keep, far, mine, other, total):
    total[...] = keep[...].astype(F32) + far[...].astype(F32)
    split_rows(info, total, mine, other)


def block_body(info, block, send, keep):
    spread(info[0], block, send, keep, SEND_A, KEEP_A)


def block_sum_body(far, keep, send, own):
    count = keep.shape[0] // 2
    own[...] = far[:count] + keep[:count]
    send[...] = far[count:] + keep[count:]


def block_last_body(info, far, keep, mine, other, total):
    total[...] = far[0] + keep[0]
    split_rows(info, total, mine, other)


def block_end_body(mine, other, out):
    out[...] = mine[...] + other[...]


def start_body(slots, visible, cot, dy, total):
    rows = cot.shape[0]
    total[...] = jnp.zeros_like(total)
    for s in range(rows // slots):
        live = lax.broadcasted_iota(jnp.int32, (slots, 1), 0) < visible[s]
        part = jnp.where(live, cot[s * slots : (s + 1) * slots, :].astype(F32), 0.0)
        dy[s * slots : (s + 1) * slots, :] = part.astype(LOW)
        total[0:1, :] += jnp.sum(part, 0, keepdims=True)


def qkv_body(info, tokens, own, normed, qkv, vecs):
    vecs[...] = own[:, 4 * HALF :].astype(F32).T[:16, :]

    def norm(at, carry):
        z, _ = standardize(tokens[at, :].astype(F32))
        normed[at, :] = (z * vecs[0:1, :] + vecs[1:2, :]).astype(LOW)
        return carry

    row_loop(tokens.shape[0], norm)
    project_qkv(info, 0, normed, own, vecs, qkv)


def project_qkv(info, flip, normed, weight, vecs, out):
    half = half_of(info, flip, HALF)
    for i in range(3):
        at = slice(i * STEP, (i + 1) * STEP)
        value = dot(normed[...], weight[:, at])
        if i != 1:
            value = value + vecs[6 + i // 2 : 7 + i // 2, half]
        out[:, at] = value.astype(LOW)


def qkv_far_body(share, info, normed, own, weight, vecs, qkv, bias_up, again):
    again[...] = normed[...]
    project_qkv(info, 1, normed, weight, vecs, qkv)
    for d in range(D // share):
        row = own[d * share // 16 * 16 : d * share // 16 * 16 + 16, 4 * HALF :].astype(F32)
        at = d * share % 16
        bias_up[0:1, 4 * share * d : 4 * share * (d + 1)] = row[
            at : at + 1, UP_LANE : UP_LANE + 4 * share
        ]


def soft_of(query, key, live):
    scores = jnp.where(live, dot(query, key, 1, 1) * SCALE, -1e30)
    power = jnp.exp(scores - jnp.max(scores, -1, keepdims=True))
    return power * (1.0 / jnp.sum(power, -1, keepdims=True))


def attend_body(slots, visible, qkv, out):
    rows = qkv.shape[0]
    lane = lax.broadcasted_iota(jnp.int32, (1, 128), 1)
    for s in range(rows // slots):
        at = slice(s * slots, (s + 1) * slots)
        live = lax.broadcasted_iota(jnp.int32, (1, slots), 1) < visible[s]
        for j in range(HALF // 128):
            query, key, value = (
                qkv[at, i * HALF + j * 128 : i * HALF + (j + 1) * 128] for i in range(3)
            )
            mixed = None
            for e in range(2):
                mine = (lane < HEAD_DIM) if e == 0 else (lane >= HEAD_DIM)
                soft = soft_of(jnp.where(mine, query, 0), key, live).astype(LOW)
                part = dot(soft, jnp.where(mine, value, 0))
                mixed = part if mixed is None else mixed + part
            out[at, j * 128 : (j + 1) * 128] = mixed.astype(LOW)


def hidden_body(tokens, vecs, o_own, o_par, own, par, hidden, normed):
    hidden[...] = dot(o_own[...], own[:, 3 * HALF : 4 * HALF], 1, 1)
    hidden[...] += dot(o_par[...], par[:, 3 * HALF : 4 * HALF], 1, 1)

    def norm(at, carry):
        value = tokens[at, :].astype(F32) + (hidden[at, :] + vecs[4:5, :])
        hidden[at, :] = value
        z, _ = standardize(value)
        normed[at, :] = (z * vecs[2:3, :] + vecs[3:4, :]).astype(LOW)
        return carry

    row_loop(tokens.shape[0], norm)


GELU_A = 0.7978845608028654
GELU_B = 0.044715


def raise_body(flip, info, normed, bias, weight, gate, slope):
    for i in range(WIDE // STEP):
        at = slice(i * STEP, (i + 1) * STEP)
        start = pl.multiple_of((info[1] ^ flip) * WIDE + i * STEP, 128)
        u = dot(normed[...], weight[:, at]) + bias[:, pl.ds(start, STEP)]
        square = u * u
        t = jnp.tanh(u * (GELU_A + (GELU_A * GELU_B) * square))
        lift = 0.5 + 0.5 * t
        gated = u * lift
        curve = GELU_A + (3.0 * GELU_A * GELU_B) * square
        slope[:, at] = (lift + (gated * (1.0 - t)) * curve).astype(LOW)
        gate[:, at] = gated.astype(LOW)


def half_of(info, flip, width):
    return pl.ds(pl.multiple_of((info[1] ^ flip) * width, 128), width)


def mix_body(hidden, vecs, a_own, a_par, own, par, out):
    value = dot(a_own[...], own[...], 1, 1)
    value += dot(a_par[...], par[...], 1, 1)
    out[...] = (hidden[...] + (value + vecs[5:6, :])).astype(LOW)


def raise_back_body(info, dy, s_own, s_par, own, par, d_own, d_par, total):
    for i in range(WIDE // STEP):
        at = slice(i * STEP, (i + 1) * STEP)
        for h, (slope, weight, out) in enumerate(((s_own, own, d_own), (s_par, par, d_par))):
            value = (dot(dy[...], weight[:, at]) * slope[:, at].astype(F32)).astype(LOW)
            start = pl.multiple_of((info[1] ^ h) * WIDE + i * STEP, 128)
            total[:, pl.ds(start, STEP)] = jnp.sum(value.astype(F32), 0, keepdims=True)
            out[:, at] = value


def norm_back(part, values, gain):
    z, scale = standardize(values)
    e = part * gain
    mean_e = jnp.mean(e, -1, keepdims=True)
    mean_ez = jnp.mean(e * z, -1, keepdims=True)
    return scale * (e - mean_e - z * mean_ez), z


def hidden_back_body(dy, hidden, vecs, d_own, d_par, own, par, dh, dp, sums, acc):
    acc[...] = dot(d_own[...], own[...], 1, 1)
    acc[...] += dot(d_par[...], par[...], 1, 1)

    def back(at, carry):
        part = acc[at, :]
        value, z = norm_back(part, hidden[at, :], vecs[2:3, :])
        value = dy[at, :].astype(F32) + value
        dh[at, :] = value
        low = value.astype(LOW)
        dp[at, :] = low
        gain, shift, bias = carry
        return (
            gain + jnp.sum(part * z, 0, keepdims=True),
            shift + jnp.sum(part, 0, keepdims=True),
            bias + jnp.sum(low.astype(F32), 0, keepdims=True),
        )

    zero = jnp.zeros((1, D), F32)
    totals = row_loop(acc.shape[0], back, (zero, zero, zero))
    for r in range(3):
        sums[r : r + 1, :] = totals[r]


def attend_back_body(slots, visible, qkv, dp, out_weight, dqkv, sums, mixed):
    rows = qkv.shape[0]
    mixed[...] = dot(dp[...], out_weight[:, 3 * HALF : 4 * HALF]).astype(LOW)
    lane = lax.broadcasted_iota(jnp.int32, (1, 128), 1)
    sums[...] = jnp.zeros_like(sums)
    for s in range(rows // slots):
        at = slice(s * slots, (s + 1) * slots)
        live = lax.broadcasted_iota(jnp.int32, (1, slots), 1) < visible[s]
        for j in range(HALF // 128):
            cols = [slice(i * HALF + j * 128, i * HALF + (j + 1) * 128) for i in range(3)]
            query, key, value = (qkv[at, c] for c in cols)
            grad = mixed[at, j * 128 : (j + 1) * 128]
            totals = [None] * 3
            for e in range(2):
                mine = (lane < HEAD_DIM) if e == 0 else (lane >= HEAD_DIM)
                query_e, key_e, grad_e = (jnp.where(mine, v, 0) for v in (query, key, grad))
                soft = soft_of(query_e, key, live)
                grad_soft = dot(grad_e, value, 1, 1)
                inner = jnp.sum(soft * grad_soft, -1, keepdims=True)
                grad_scores = (soft * (grad_soft - inner)).astype(LOW)
                parts = (
                    dot(grad_scores, key_e),
                    dot(grad_scores, query_e, 0, 0),
                    dot(soft.astype(LOW), grad_e, 0, 0),
                )
                totals = [p if t is None else t + p for t, p in zip(totals, parts)]
            for i, factor in enumerate((SCALE, SCALE, 1.0)):
                low = (totals[i] * factor).astype(LOW)
                dqkv[at, cols[i]] = low
                if i != 1:
                    sums[i : i + 1, j * 128 : (j + 1) * 128] += jnp.sum(
                        low.astype(F32), 0, keepdims=True
                    )


def token_back_body(
    share, info, tokens, dh, vecs, sums_two, dy_sum, up_sum, sums_own, sums_par, d_own, d_par, own, par,
    out, block, acc, sums,
):
    acc[...] = dot(d_own[...], own[:, : 3 * HALF], 1, 1)
    acc[...] += dot(d_par[...], par[:, : 3 * HALF], 1, 1)

    def back(at, carry):
        part = acc[at, :]
        value, z = norm_back(part, tokens[at, :].astype(F32), vecs[0:1, :])
        out[at, :] = (dh[at, :] + value).astype(LOW)
        gain, shift = carry
        return (
            gain + jnp.sum(part * z, 0, keepdims=True),
            shift + jnp.sum(part, 0, keepdims=True),
        )

    zero = jnp.zeros((1, D), F32)
    totals = row_loop(acc.shape[0], back, (zero, zero))
    sums[...] = jnp.zeros_like(sums)
    for r in range(2):
        sums[r : r + 1, :] = totals[r]
    sums[2:5, :] = sums_two[0:3, :]
    sums[5:6, :] = dy_sum[0:1, :]
    for flip, part in enumerate((sums_own, sums_par)):
        half = half_of(info, flip, HALF)
        sums[6:7, half] = part[0:1, :]
        sums[7:8, half] = part[2:3, :]
    block[...] = sums[...].T
    for d in range(D // share):
        part = up_sum[0:1, 4 * share * d : 4 * share * (d + 1)]
        block[share * d : share * d + 1, UP_LANE : UP_LANE + 4 * share] = part


def outer(left, left_far, right, right_far):
    return dot(left[...], right[...], 0, 0) + dot(left_far[...], right_far[...], 0, 0)


def pair_grads(info, blocks, sends, grad):
    send_a, keep_a, send_b, keep_b = sends
    width = keep_a.shape[2]
    at = 0
    for left, left_far, right, right_far in blocks:
        grad[...] = outer(left, left_far, right, right_far)
        split = min(max(width - at, 0), STEP)
        if split:
            cols = slice(at, at + split)
            part = grad.at[:, :split]
            spread(info[0], part, send_a.at[:, :, cols], keep_a.at[:, :, cols], SEND_A, KEEP_A)
        if split < STEP:
            cols = slice(at + split - width, at + STEP - width)
            part = grad.at[:, split:]
            spread(info[0], part, send_b.at[:, :, cols], keep_b.at[:, :, cols], SEND_B, KEEP_B)
        at += STEP


def steps_of(near, far, count):
    for i in range(count):
        at = slice(i * STEP, (i + 1) * STEP)
        yield near.at[:, at], far.at[:, at]


def wide_grad_body(info, left, left_far, right, right_far, *rest):
    blocks = [(left, left_far, a, b) for a, b in steps_of(right, right_far, 4)]
    pair_grads(info, blocks, rest[:4], rest[4])


def qkv_grad_body(info, norm, norm_far, dqkv, dqkv_far, dp, dp_far, mixed, mixed_far, *rest):
    blocks = [(norm, norm_far, a, b) for a, b in steps_of(dqkv, dqkv_far, 3)]
    blocks += [(dp, dp_far, a, b) for a, b in steps_of(mixed, mixed_far, 1)]
    pair_grads(info, blocks, rest[:4], rest[4])


def pick(flag, left, right):
    return jnp.where(flag, left, right)


def half_major(matrix):
    rows = matrix.shape[0]
    return matrix.reshape(rows, 3, 2, HALF).transpose(0, 2, 1, 3).reshape(rows, 3 * D)


def third_major(matrix):
    rows = matrix.shape[0]
    return matrix.reshape(rows, 2, 3, HALF).transpose(0, 2, 1, 3).reshape(rows, 3 * D)


class WholeComm:
    touch = ()

    def __init__(self, count):
        self.info = jnp.zeros((2,), jnp.int32)

    def order(self, low, high):
        return low, high

    def weights(self, call, small, bias_up, w_qkv, w_out, w_up, w_down):
        def gather(value):
            return lax.all_gather(value, "dp", axis=0, tiled=True)

        def half(matrix, h):
            width = matrix.shape[1] // 2
            return matrix[:, h * width : (h + 1) * width]

        block = jnp.pad(small.T, ((0, 0), (0, 128 - small.shape[0])))
        block = gather(block.at[0, UP_LANE : UP_LANE + bias_up.shape[1]].set(bias_up[0]))
        qkv, out, up = (gather(w) for w in (half_major(w_qkv), w_out, w_up))
        self.first = [jnp.concatenate([half(qkv, h), half(out, h), block], 1) for h in range(2)]
        self.second = [half(up, h) for h in range(2)]
        down = gather(w_down)
        self.third = [half(down, h) for h in range(2)]

    def step(self, call):
        pass

    def advance(self, call):
        pass

    def pump(self, call, index):
        pass

    def reduce(self, value):
        return lax.psum_scatter(value, "dp", scatter_dimension=0, tiled=True)

    def far(self, array):
        return array

    def reduce_down(self, call, dy, dy_far, gated, gated_far):
        self.down = self.reduce(dot(dy, jnp.concatenate([gated, gated_far], 1), 0, 0))

    def reduce_up(self, call, norm, norm_far, du, du_far):
        self.up = self.reduce(dot(norm, jnp.concatenate([du, du_far], 1), 0, 0))

    def reduce_qkv(self, call, norm, norm_far, triple, triple_far, dp, dp_far, mixed, mixed_far):
        triple = jnp.concatenate([triple, triple_far], 1)
        self.qkv = third_major(self.reduce(dot(norm, triple, 0, 0)))
        self.out = self.reduce(dot(dp, jnp.concatenate([mixed, mixed_far], 1), 0, 0))

    def reduce_block(self, call, block):
        self.vec = self.reduce(block)

    def results(self, call):
        return self.down, self.up, self.out, self.qkv, self.vec


class GridComm:
    def __init__(self):
        index = lax.axis_index("dp")
        self.info = jnp.stack([index >> 1, index & 1]).astype(jnp.int32)
        self.is_first = (index & 1) == 0
        self.jobs = []

    def order(self, low, high):
        return pick(self.is_first, low, high), pick(self.is_first, high, low)

    def weights(self, call, small, bias_up, w_qkv, w_out, w_up, w_down):
        rows = w_qkv.shape[0]
        total = sum(width for width, _ in CHUNKS)
        total_a = sum(cut for _, cut in CHUNKS)
        parts = (w_qkv, w_out, w_up, w_down)
        mine, other = call(
            pack_body,
            [shape((rows, total))] * 2,
            [small, bias_up, *parts],
            info=self.info,
            in_hbm=(2, 3, 4, 5),
            scratch=[pltpu.VMEM((128, 128), F32)]
            + [pltpu.VMEM(w.shape, LOW) for w in parts]
            + [pltpu.SemaphoreType.DMA],
        )
        *self.units, unit_a, unit_b = call(
            unit_body,
            [shape((48, w)) for w in [*(c[0] for c in CHUNKS), total_a, total - total_a]],
            [mine, swap(other, 1)],
            info=self.info,
        )
        self.own = [unit_a, swap(unit_a, 4), unit_b, swap(unit_b, 2)]
        self.lines = [swap(self.units[0], bit) for bit in (8, 16, 24)]
        self.plan = self.schedule(call)

    def advance(self, call):
        next(self.plan)

    def pair(self, call, index, far):
        (pair,) = call(pair_body, [shape((2, 48, CHUNKS[index][0]))], [self.units[index], far])
        return [far, swap(pair, 8)]

    def schedule(self, call):
        width, cut = CHUNKS[0]
        pair_a, pair_b = call(
            own_body, [shape((2, 48, cut)), shape((2, 48, width - cut))], self.own
        )
        pairs = [pair_a, swap(pair_a, 2), pair_b, swap(pair_b, 4)]
        stacked = self.stack(call, 0, self.lines)
        far_one = swap(self.units[1], 16)
        joined = self.join(call, 0, stacked, touch=(far_one,))
        line_one = self.pair(call, 1, far_one)
        far_two = swap(self.units[2], 16)
        own = self.finish(call, 0, joined, pairs)
        self.first = [own, swap(own, 1)]
        yield
        line_two = self.pair(call, 2, far_two)
        yield
        stacked = self.stack(call, 1, line_one)
        yield
        joined = self.join(call, 1, stacked)
        stacked = self.stack(call, 2, line_two)
        yield
        joined_two = self.join(call, 2, stacked)
        yield
        own = self.finish(call, 1, joined)
        self.second = [own, swap(own, 1)]
        yield
        own = self.finish(call, 2, joined_two)
        self.third = [own, swap(own, 1)]
        yield

    def starts(self, index):
        return (
            sum(c for _, c in CHUNKS[:index]),
            sum(w - c for w, c in CHUNKS[:index]),
        )

    def stack(self, call, index, line, touch=()):
        width, cut = CHUNKS[index]
        a, b = call(
            functools.partial(stack_body, cut),
            [shape((3, 48, cut)), shape((3, 48, width - cut))],
            line,
            touch=touch,
        )
        return a, swap(a, 4), b, swap(b, 2)

    def join(self, call, index, stacked, touch=()):
        width, cut = CHUNKS[index]
        count = 6 if index == 0 else 8
        a, b = call(
            functools.partial(join_body, *self.starts(index)),
            [shape((count, 48, cut)), shape((count, 48, width - cut))],
            [*stacked] + ([] if index == 0 else self.own),
            touch=touch,
        )
        return a, swap(a, 2), b, swap(b, 4)

    def finish(self, call, index, joined, pairs=()):
        width, cut = CHUNKS[index]
        z = (8, 4, 12) if index else Z_CODES[1:]
        codes_a = z + tuple(c ^ 2 for c in z)
        codes_b = z + tuple(c ^ 1 for c in z)
        if index:
            codes_a, codes_b = (0, 2) + codes_a, (0, 1) + codes_b
        plan = []
        for codes_a, codes_b in [(codes_a, codes_b)] + ([((0, 2), (0, 1))] if pairs else []):
            plan += [
                (codes_a, 0, 0, cut),
                (tuple(c ^ 1 for c in codes_a), 0, 0, cut),
                (codes_b, 0, cut, width - cut),
                (tuple(c ^ 2 for c in codes_b), 0, cut, width - cut),
            ]
        return call(
            functools.partial(place_body, plan),
            [shape((D, width))],
            [*joined, *pairs],
            info=self.info,
            scratch=[pltpu.SemaphoreType.DMA],
        )[0]

    def pieces(self, width_a, width_b):
        return [shape((8, 48, w)) for w in (width_a, width_a, width_b, width_b)]

    def job(self, call, name, parts, body, outs, direct):
        send_a, keep_a, send_b, keep_b = parts
        width_a, width_b = keep_a.shape[2], keep_b.shape[2]
        width = width_a + width_b
        far_a, far_b = swap(send_a, 2), swap(send_b, 4)
        yield
        send_a, keep_a, send_b, keep_b = call(
            first_sum_body,
            [shape((4, 48, w)) for w in (width_a, width_a, width_b, width_b)],
            [far_a, keep_a, far_b, keep_b],
        )
        far_a, far_b = swap(send_a, 4), swap(send_b, 2)
        yield
        if direct:
            own, *lines = call(
                second_sum_body, [shape((48, width))] * 4, [far_a, keep_a, far_b, keep_b]
            )
            lines = [swap(line, bit) for line, bit in zip(lines, (8, 16, 24))]
            yield
            last_body, lines = last_sum_body, [own, *lines]
        else:
            own, send = call(
                second_sum_body, [shape((2, 48, width))] * 2, [far_a, keep_a, far_b, keep_b]
            )
            far = swap(send, 8)
            yield
            own, send = call(near_sum_body, [shape((48, width))] * 2, [own, far])
            far = swap(send, 16)
            yield
            last_body, lines = last_near_body, [own, far]
        mine, other = call(
            last_body,
            [shape((24, width), F32)] * 2,
            lines,
            info=self.info,
            scratch=[pltpu.VMEM((48, width), F32)],
        )
        other = swap(other, 1)
        yield
        self.outs[name] = call(body, outs, [mine, other], info=self.info, last=True)

    def begin(self, job):
        next(job)
        self.jobs.append(job)

    def pump(self, call, index):
        return next(self.jobs[index], self) is not self

    def block_job(self, call, block):
        send, keep = call(
            block_body, [shape((8, 48, 128), F32)] * 2, [block], info=self.info
        )
        far = swap(send, 2)
        yield
        for bit, count in ((4, 4), (16, 2), (8, 1)):
            send, keep = call(
                block_sum_body, [shape((count, 48, 128), F32)] * 2, [far, keep]
            )
            far = swap(send, bit)
            yield
        mine, other = call(
            block_last_body,
            [shape((24, 128), F32)] * 2,
            [far, keep],
            info=self.info,
            scratch=[pltpu.VMEM((48, 128), F32)],
        )
        other = swap(other, 1)
        yield
        self.vec = call(block_end_body, [shape((24, 128), F32)], [mine, other])[0]

    def results(self, call):
        for index in ORDER:
            self.pump(call, index)
        (down,), (up,), (qkv, out) = [self.outs[k] for k in ("down", "up", "qkv")]
        return down, up, out, qkv, self.vec

    def far(self, array):
        return swap(array, 1)

    def reduce_down(self, call, dy, dy_far, gated, gated_far):
        self.outs = {}
        parts = call(
            wide_grad_body,
            self.pieces(768, 768),
            [dy, dy_far, gated, gated_far],
            info=self.info,
            scratch=[pltpu.VMEM((D, STEP), F32)],
            us=6,
        )
        self.begin(self.job(call, "down", parts, merge_one_body, [shape((24, FF), F32)], False))

    def reduce_up(self, call, *args):
        parts = call(
            wide_grad_body,
            self.pieces(768, 768),
            args,
            info=self.info,
            scratch=[pltpu.VMEM((D, STEP), F32)],
            us=6,
        )
        self.begin(self.job(call, "up", parts, merge_one_body, [shape((24, FF), F32)], False))

    def reduce_qkv(self, call, *args):
        parts = call(
            qkv_grad_body,
            self.pieces(768, 768),
            args,
            info=self.info,
            scratch=[pltpu.VMEM((D, STEP), F32)],
            us=6,
        )
        outs = [shape((24, 3 * D), F32), shape((24, D), F32)]
        self.begin(self.job(call, "qkv", parts, merge_qkv_body, outs, True))

    def reduce_block(self, call, block):
        self.begin(self.block_job(call, block))


def shards(count, tokens, lengths, source, cotangent, w_qkv, w_out, w_up, w_down, *small):
    (
        gain_one, shift_one, bias_query, bias_value, bias_out, gain_two, shift_two,
        bias_up, bias_down,
    ) = small
    seqs, slots = tokens.shape[:2]
    rows = seqs * slots
    share = gain_one.shape[0]
    comm = GridComm() if count == 32 else WholeComm(count)
    visible = jnp.where(source == 1, lengths, IMG_LEN)
    tokens = tokens.reshape(rows, D)
    cotangent = cotangent.reshape(rows, D)
    small = jnp.stack(
        [gain_one, shift_one, gain_two, shift_two, bias_out, bias_down, bias_query, bias_value]
    )
    bias_up = bias_up[None]
    call = Chain([tokens, cotangent, small, bias_up])

    act = shape((rows, D))
    act_f = shape((rows, D), F32)
    half = shape((rows, HALF))
    triple = shape((rows, 3 * HALF))
    wide = shape((rows, WIDE))

    def attend(part, *touch):
        return call(
            functools.partial(attend_body, slots), [half], [part], info=visible, us=4.3, touch=touch
        )[0]

    comm.weights(call, small, bias_up, w_qkv, w_out.T, w_up, w_down.T)
    dy, dy_sum = call(
        functools.partial(start_body, slots),
        [act, shape((8, D), F32)],
        [cotangent],
        info=visible,
    )
    dy_far = comm.far(dy)
    comm.advance(call)
    normed_one, qkv_own, vecs = call(
        qkv_body,
        [act, triple, shape((16, D), F32)],
        [tokens, comm.first[0]],
        info=comm.info,
        touch=(dy_far,),
        us=4.3,
    )
    o_own = attend(qkv_own)
    comm.advance(call)
    comm.advance(call)
    qkv_par, bias_up, normed_again = call(
        functools.partial(qkv_far_body, share),
        [triple, shape((1, FF), F32), act],
        [normed_one, comm.first[0], comm.first[1], vecs],
        info=comm.info,
        us=2.5,
    )
    normed_one_far = comm.far(normed_again)
    comm.advance(call)
    o_par = attend(qkv_par)
    o_far = comm.far(o_par)
    comm.advance(call)
    hidden, normed_two = call(
        hidden_body,
        [act_f, act],
        [tokens, vecs, o_own, o_par, *comm.first],
        touch=(o_far, normed_one_far),
        us=3.6,
    )
    normed_two_far = comm.far(normed_two)
    comm.advance(call)
    second = comm.second

    def raise_half(flip, *touch):
        return call(
            functools.partial(raise_body, flip),
            [wide] * 2,
            [normed_two, bias_up, second[flip]],
            info=comm.info,
            touch=touch,
            us=3.7,
        )

    gated, slope = raise_half(0)
    gated_par, slope_par = raise_half(1)
    gated_far = comm.far(gated_par)
    comm.advance(call)
    comm.reduce_down(call, dy, dy_far, gated, gated_far)
    third = comm.third
    raised, raised_par, up_sum = call(
        raise_back_body,
        [wide, wide, shape((1, FF), F32)],
        [dy, slope, slope_par, *third],
        info=comm.info,
        us=4.8,
    )
    raised_far = comm.far(raised_par)
    grad_hidden, branch, sums_two = call(
        hidden_back_body,
        [act_f, act, shape((8, D), F32)],
        [dy, hidden, vecs, raised, raised_par, *second],
        scratch=[pltpu.VMEM((rows, D), F32)],
        us=6.6,
    )
    branch_far = comm.far(branch)

    def attend_back(part, weight, *touch):
        return call(
            functools.partial(attend_back_body, slots),
            [triple, shape((8, HALF), F32)],
            [part, branch, weight],
            info=visible,
            scratch=[pltpu.VMEM((rows, HALF), LOW)],
            touch=touch,
            us=8.2,
        )

    triple_par, sums_par = attend_back(qkv_par, comm.first[1])
    triple_far = comm.far(triple_par)
    comm.pump(call, 0)
    comm.reduce_up(call, normed_two, normed_two_far, raised, raised_far)
    triple_own, sums_own = attend_back(qkv_own, comm.first[0], branch_far)
    comm.pump(call, 0)
    comm.reduce_qkv(
        call, normed_one, normed_one_far, triple_own, triple_far, branch, branch_far, o_own, o_far
    )
    comm.pump(call, 1)
    grad_tokens, block = call(
        functools.partial(token_back_body, share),
        [act, shape((D, 128), F32)],
        [
            tokens, grad_hidden, vecs, sums_two, dy_sum, up_sum, sums_own, sums_par,
            triple_own, triple_par, *comm.first,
        ],
        info=comm.info,
        scratch=[pltpu.VMEM((rows, D), F32), pltpu.VMEM((128, D), F32)],
        us=6.5,
    )
    (output,) = call(
        mix_body, [act], [hidden, vecs, gated, gated_par, *third], us=4.1, last=True
    )
    comm.pump(call, 0)
    comm.reduce_block(call, block)
    g_down_t, g_up, g_out_t, g_qkv, g_vec = comm.results(call)
    (
        g_gain_one, g_shift_one, g_gain_two, g_shift_two, g_bias_out, g_bias_down, g_query, g_value,
    ) = [g_vec[:, i] for i in range(8)]
    return (
        output.reshape(seqs, slots, D),
        grad_tokens.reshape(seqs, slots, D),
        g_qkv,
        g_out_t.T,
        g_up,
        g_down_t.T,
        g_gain_one, g_shift_one, g_query, g_value, g_bias_out, g_gain_two, g_shift_two,
        g_vec[0, UP_LANE : UP_LANE + 4 * share],
        g_bias_down,
    )


def solution(mesh):
    row, tall, wide, vec = P("dp", None, None), P("dp", None), P(None, "dp"), P("dp")
    in_specs = (row, vec, vec, row, tall, wide, tall, wide) + (vec,) * 9
    out_specs = (row, row, tall, wide, tall, wide) + (vec,) * 9
    body = functools.partial(shards, mesh.shape["dp"])
    return jax.shard_map(
        body, mesh=mesh, in_specs=in_specs, out_specs=out_specs, check_vma=False
    )
```

```python
import functools
import jax
import jax.numpy as jnp
import numpy as np
from jax import lax
from jax.experimental import pallas as pl
from jax.experimental.pallas import tpu as pltpu
from jax.sharding import PartitionSpec as P

HEADS = 12
HEAD_DIM = 64
IMG_LEN = 196
ALWAYS = 152
EPS = 1e-06
D = 768
FF = 3072
HALF = D // 2
WIDE = FF // 2
LOW = jnp.bfloat16
F32 = jnp.float32
STEP = 768
PART = 512
ROWS = 64
MARGIN = 10
PACE = 4
UP_LANE = 32
SCALE = HEAD_DIM ** (-0.5)
CHUNKS = ((4 * HALF + 128, 896), (WIDE, 768), (WIDE, 768))
Z_CODES = (0, 4, 8, 12)
SMEM = pl.BlockSpec(memory_space=pltpu.SMEM)
ANY = pl.BlockSpec(memory_space=pl.ANY)
VMEM = pl.BlockSpec(memory_space=pltpu.VMEM)


def shape(dims, kind=LOW):
    return jax.ShapeDtypeStruct(dims, kind)


class Chain:
    def __init__(self, loose):
        self.last = None
        self.loose = loose
        self.count = 0

    def near(self, array):
        if any(array is a for a in self.loose):
            return array
        return pltpu.with_memory_space_constraint(array, pltpu.VMEM)

    def __call__(
        self, body, outs, ins, *, info=None, touch=(), in_hbm=(), scratch=(), us=8, last=False
    ):
        us *= PACE
        if self.count < len(COSTS):
            us = COSTS[self.count]
        self.count += 1
        head = [] if info is None else [info]
        ins = list(ins)
        count = len(head) + len(ins)
        specs = [SMEM] * len(head) + [ANY if i in in_hbm else VMEM for i in range(len(ins))]
        given = [
            pltpu.with_memory_space_constraint(a, pltpu.HBM) if i in in_hbm else self.near(a)
            for i, a in enumerate(ins)
        ]
        extra = list(touch) + ([] if self.last is None else [self.last])
        total = count + len(extra)

        def run(*refs):
            body(*refs[:count], *refs[total:])

        held = sum(
            int(np.prod(k.shape)) * jnp.dtype(k.dtype).itemsize
            for k in scratch
            if getattr(k, "shape", ())
        )
        size = sum(a.size * a.dtype.itemsize for a in [*ins, *outs])
        results = pl.pallas_call(
            run,
            out_shape=tuple(outs if last else [pltpu.VMEM(o.shape, o.dtype) for o in outs]),
            in_specs=specs + [ANY] * len(extra),
            out_specs=(VMEM,) * len(outs),
            scratch_shapes=list(scratch),
            compiler_params=pltpu.CompilerParams(vmem_limit_bytes=held + MARGIN * 2**20),
            cost_estimate=pl.CostEstimate(
                flops=int(us * 1.1e9), bytes_accessed=size, transcendentals=0
            ),
        )(*head, *given, *extra)
        self.last = min(results, key=lambda r: r.size * r.dtype.itemsize)
        return results


def dot(left, right, left_dim=1, right_dim=0):
    return lax.dot_general(
        left, right, (((left_dim,), (right_dim,)), ((), ())), preferred_element_type=F32
    )


def joined(own, par, axis=1):
    return jnp.concatenate([own[...], par[...]], axis)


def standardize(values):
    center = values - jnp.mean(values, -1, keepdims=True)
    scale = lax.rsqrt(jnp.mean(center * center, -1, keepdims=True) + EPS)
    return center * scale, scale


def row_loop(rows, body, init=0):
    def step(i, carry):
        return body(pl.ds(pl.multiple_of(i * ROWS, ROWS), ROWS), carry)

    return lax.fori_loop(0, rows // ROWS, step, init)


def swap(value, bit):
    pairs = [(i, i ^ bit) for i in range(32)]
    return lax.ppermute(value, "dp", pairs)


def pack_body(info, small, bias_up, *refs):
    weights, (mine, other), (rows, *held, sem) = refs[:4], refs[4:6], refs[6:]
    copies = [pltpu.make_async_copy(w, v, sem) for w, v in zip(weights, held)]
    for copy in copies:
        copy.start()
    w_qkv, w_out, w_up, w_down = held
    rows[...] = jnp.zeros_like(rows)
    share = w_qkv.shape[0]
    rows[: small.shape[0], :share] = small[...].astype(F32)
    rows[...] = rows[...].T
    rows[0:1, UP_LANE : UP_LANE + 4 * share] = bias_up[...].astype(F32)
    block = rows[:share, :].astype(LOW)
    for copy in copies:
        copy.wait()
    for flip, out in enumerate((mine, other)):
        h = info[1] ^ flip

        def half(weight, width, start=0):
            return weight[:, pl.ds(pl.multiple_of(start + h * width, 128), width)]

        for i in range(3):
            out[:, i * HALF : (i + 1) * HALF] = half(w_qkv, HALF, i * D)
        out[:, 3 * HALF : 4 * HALF] = half(w_out, HALF)
        at = CHUNKS[0][0]
        out[:, 4 * HALF : at] = block
        out[:, at : at + WIDE] = half(w_up, WIDE)
        out[:, at + WIDE :] = half(w_down, WIDE)


def unit_body(info, mine, other, unit_one, units, unit_a, unit_b):
    a, b = mine[...].astype(F32), other[...].astype(F32)
    unit = jnp.where(
        info[1] == 0, jnp.concatenate([a, b], 0), jnp.concatenate([b, a], 0)
    ).astype(LOW)
    start = at_a = at_b = 0
    for i, (width, cut) in enumerate(CHUNKS):
        part = unit[:, start : start + width]
        if i == 0:
            unit_one[...] = part
        else:
            units[i - 1] = part
        unit_a[:, at_a : at_a + cut] = part[:, :cut]
        unit_b[:, at_b : at_b + width - cut] = part[:, cut:]
        start, at_a, at_b = start + width, at_a + cut, at_b + width - cut


def own_body(unit_a, far_a, unit_b, far_b, pair_a, pair_b):
    for pair, unit, far in ((pair_a, unit_a, far_a), (pair_b, unit_b, far_b)):
        width = pair.shape[2]
        pair[0] = unit[:, :width]
        pair[1] = far[:, :width]


def pair_body(index, units, far, pair):
    pair[0] = units[index]
    pair[1] = far[...]


def stack_body(cut, *refs):
    pieces, (stack_a, stack_b) = refs[:-2], refs[-2:]
    at = 0
    for piece in pieces:
        for i in range(piece.shape[0] if len(piece.shape) == 3 else 1):
            part = piece.at[i] if len(piece.shape) == 3 else piece
            stack_a[at] = part[:, :cut]
            stack_b[at] = part[:, cut:]
            at += 1


def first_stack_body(cut, index, *refs):
    *pieces, units, stack_a, stack_b, again = refs
    stack_body(cut, *pieces, stack_a, stack_b)
    again[...] = units[index]


def join_body(start_a, start_b, *refs):
    stacks, own, (join_a, join_b) = refs[:4], refs[4:-2], refs[-2:]
    for side, join, start in ((0, join_a, start_a), (1, join_b, start_b)):
        width = join.shape[2]
        parts = own[2 * side : 2 * side + 2]
        for i, part in enumerate(parts):
            join[i] = part[:, start : start + width]
        at = len(parts)
        join[at : at + 3] = stacks[2 * side][...]
        join[at + 3 : at + 6] = stacks[2 * side + 1][...]


def place_body(plan, info, *refs):
    pieces, out, sem = refs[:-2], refs[-2], refs[-1]
    copies = []
    for piece, (codes, source, target, width) in zip(pieces, plan):
        for i, code in enumerate(codes):
            row = pl.multiple_of((info[0] ^ code) * 48, 48)
            copies.append(
                pltpu.make_async_copy(
                    piece.at[i, :, pl.ds(source, width)],
                    out.at[pl.ds(row, 48), pl.ds(target, width)],
                    sem,
                )
            )
    for copy in copies:
        copy.start()
    for copy in copies:
        copy.wait()


ORDER = "up0o1q0tm1b02310210122"
EARLY = "SkJPlmsnhtjfgGFd"
COSTS = ()
KEEP_A = tuple(c ^ y for y in (0, 2) for c in Z_CODES)
KEEP_B = tuple(c ^ x for x in (0, 1) for c in Z_CODES)
SEND_A = tuple(c ^ 1 for c in KEEP_A)
SEND_B = tuple(c ^ 2 for c in KEEP_B)


def spread(chip, grad, send, keep, send_codes, keep_codes):
    for out, codes in ((send, send_codes), (keep, keep_codes)):
        for i, code in enumerate(codes):
            row = pl.multiple_of((chip ^ code) * 48, 48)
            out[i] = grad[pl.ds(row, 48), :].astype(out.dtype)


def add(left, right):
    return (left.astype(F32) + right.astype(F32)).astype(LOW)


def first_sum_body(far_a, keep_a, far_b, keep_b, send_a, own_a, send_b, own_b):
    for far, keep, send, own in ((far_a, keep_a, send_a, own_a), (far_b, keep_b, send_b, own_b)):
        for i in range(4):
            send[i] = add(far[4 + i], keep[4 + i])
            own[i] = add(far[i], keep[i])


def second_sum_body(far_a, keep_a, far_b, keep_b, *outs):
    cut = keep_a.shape[2]
    for i in range(4):
        out = outs[i] if len(outs) == 4 else outs[i % 2].at[i // 2]
        out[:, :cut] = add(far_a[i], keep_a[i])
        out[:, cut:] = add(far_b[i], keep_b[i])


def last_sum_body(info, own, z_one, z_two, z_three, mine, other, total):
    value = own[...].astype(F32)
    for piece in (z_one, z_two, z_three):
        value = value + piece[...].astype(F32)
    total[...] = value
    split_rows(info, total, mine, other)


def split_rows(info, total, mine, other):
    rows = mine.shape[0]
    mine[...] = total[pl.ds(pl.multiple_of(info[1] * rows, 8), rows), :]
    other[...] = total[pl.ds(pl.multiple_of((1 - info[1]) * rows, 8), rows), :]


def merge(info, mine, other, start, width, out, count=1):
    for flip, part in enumerate((mine, other)):
        h = info[1] ^ flip
        for i in range(count):
            at = pl.multiple_of((2 * i + h) * width, 128)
            out[:, pl.ds(at, width)] = part[:, start + i * width : start + (i + 1) * width]


def merge_one_body(info, mine, other, out):
    merge(info, mine, other, 0, WIDE, out)


def merge_qkv_body(info, mine, other, out_qkv, out_out, vec):
    merge(info, mine, other, 0, HALF, out_qkv, 3)
    merge(info, mine, other, 3 * HALF, HALF, out_out)
    vec[...] = mine[:, 4 * HALF :] + other[:, 4 * HALF :]


def near_sum_body(own, far, keep, send):
    keep[...] = add(own[0], far[0])
    send[...] = add(own[1], far[1])


def last_near_body(info, keep, far, mine, other, total):
    total[...] = keep[...].astype(F32) + far[...].astype(F32)
    split_rows(info, total, mine, other)


def block_body(info, block, send, keep):
    spread(info[0], block, send, keep, SEND_A, KEEP_A)


def block_sum_body(far, keep, send, own):
    count = keep.shape[0] // 2
    own[...] = far[:count] + keep[:count]
    send[...] = far[count:] + keep[count:]


def second_sum_block_body(far_a, keep_a, far_b, keep_b, far_v, keep_v, *outs):
    width = keep_a.shape[2] + keep_b.shape[2]
    second_sum_body(far_a, keep_a, far_b, keep_b, *(o.at[:, :width] for o in outs))
    for i, out in enumerate(outs):
        out[:, width:] = (far_v[i] + keep_v[i]).astype(LOW)


def start_body(slots, visible, cot, dy, total):
    rows = cot.shape[0]
    total[...] = jnp.zeros_like(total)
    for s in range(rows // slots):
        live = lax.broadcasted_iota(jnp.int32, (slots, 1), 0) < visible[s]
        part = jnp.where(live, cot[s * slots : (s + 1) * slots, :].astype(F32), 0.0)
        dy[s * slots : (s + 1) * slots, :] = part.astype(LOW)
        total[0:1, :] += jnp.sum(part, 0, keepdims=True)


def qkv_body(info, tokens, own, normed, qkv, vecs):
    vecs[...] = own[:, 4 * HALF :].astype(F32).T[:16, :]

    def norm(at, carry):
        z, _ = standardize(tokens[at, :].astype(F32))
        normed[at, :] = (z * vecs[0:1, :] + vecs[1:2, :]).astype(LOW)
        return carry

    row_loop(tokens.shape[0], norm)
    project_qkv(info, 0, normed, own, vecs, qkv)


def project_qkv(info, flip, normed, weight, vecs, out):
    half = half_of(info, flip, HALF)
    bias = [vecs[6:7, half], jnp.zeros((1, HALF), F32), vecs[7:8, half]]
    value = dot(normed[...], weight[:, : 3 * HALF]) + jnp.concatenate(bias, 1)
    out[...] = value.astype(LOW)


def qkv_far_body(share, info, normed, own, weight, vecs, qkv, bias_up):
    project_qkv(info, 1, normed, weight, vecs, qkv)
    for d in range(D // share):
        row = own[d * share // 16 * 16 : d * share // 16 * 16 + 16, 4 * HALF :].astype(F32)
        at = d * share % 16
        bias_up[0:1, 4 * share * d : 4 * share * (d + 1)] = row[
            at : at + 1, UP_LANE : UP_LANE + 4 * share
        ]


def by_head(block):
    lane = lax.broadcasted_iota(jnp.int32, (1, 128), 1)
    return jnp.concatenate(
        [jnp.where(lane < HEAD_DIM, block, 0), jnp.where(lane >= HEAD_DIM, block, 0)], 0
    )


def scores_of(key, query, live):
    scores = dot(key, query, 1, 1)
    return jnp.concatenate(
        [scores[:ALWAYS], jnp.where(live[ALWAYS:], scores[ALWAYS:], -1e30)], 0
    )


def from_columns(values, slots):
    return jnp.concatenate(
        [values[:HEAD_DIM, :slots], values[HEAD_DIM:, slots:]], 0
    ).T


def blocks_of(slots, rows):
    for s in range(rows // slots):
        for j in range(HALF // 128):
            yield s, j, slice(s * slots, (s + 1) * slots)


def attend_body(slots, visible, qkv, out, logs):
    slot = lax.broadcasted_iota(jnp.int32, (slots, 1), 0)
    for s, j, at in blocks_of(slots, qkv.shape[0]):
        query, key, value = (
            qkv[at, i * HALF + j * 128 : i * HALF + (j + 1) * 128] for i in range(3)
        )
        scores = scores_of(key, by_head(query * SCALE), slot < visible[s])
        top = jnp.max(scores, 0, keepdims=True)
        power = jnp.exp(scores - top)
        total = jnp.sum(power, 0, keepdims=True)
        row = s * (HALF // 128) + j
        logs[row : row + 1, :] = top + jnp.log(total)
        mixed = dot(value.T, (power * (1.0 / total)).astype(LOW))
        out[at, j * 128 : (j + 1) * 128] = from_columns(mixed, slots).astype(LOW)


def hidden_body(tokens, vecs, o_own, o_par, own, par, hidden, normed, standard, scales):
    out_cols = slice(3 * HALF, 4 * HALF)
    hidden[...] = dot(joined(o_own, o_par), joined(own.at[:, out_cols], par.at[:, out_cols]), 1, 1)

    def norm(at, carry):
        value = tokens[at, :].astype(F32) + (hidden[at, :] + vecs[4:5, :])
        hidden[at, :] = value
        z, scale = standardize(value)
        standard[at, :] = z
        scales[at, :] = jnp.broadcast_to(scale, (ROWS, 128))
        normed[at, :] = (z * vecs[2:3, :] + vecs[3:4, :]).astype(LOW)
        return carry

    row_loop(tokens.shape[0], norm)


def turn_body(normed_two, dy, normed_one, out):
    for i, array in enumerate((normed_two, dy, normed_one)):
        out[i * D : (i + 1) * D, :] = array[...].T


GELU_A = 0.7978845608028654
GELU_B = 0.044715


def raise_body(flip, info, normed, bias, weight, gate, slope):
    for i in range(WIDE // PART):
        at = slice(i * PART, (i + 1) * PART)
        start = pl.multiple_of((info[1] ^ flip) * WIDE + i * PART, 128)
        u = dot(normed[...], weight[:, at]) + bias[:, pl.ds(start, PART)]
        square = u * u
        t = jnp.tanh(u * (GELU_A + (GELU_A * GELU_B) * square))
        lift = 0.5 + 0.5 * t
        gated = u * lift
        curve = GELU_A + (3.0 * GELU_A * GELU_B) * square
        slope[:, at] = (lift + (gated * (1.0 - t)) * curve).astype(LOW)
        gate[:, at] = gated.astype(LOW)


def half_of(info, flip, width):
    return pl.ds(pl.multiple_of((info[1] ^ flip) * width, 128), width)


def mix_body(hidden, vecs, a_own, a_par, own, par, out):
    value = dot(joined(a_own, a_par), joined(own, par), 1, 1)
    out[...] = (hidden[...] + (value + vecs[5:6, :])).astype(LOW)


def raise_back_body(info, dy, s_own, s_par, own, par, d_own, d_par, total):
    for i in range(WIDE // PART):
        at = slice(i * PART, (i + 1) * PART)
        for h, (slope, weight, out) in enumerate(((s_own, own, d_own), (s_par, par, d_par))):
            value = (dot(dy[...], weight[:, at]) * slope[:, at].astype(F32)).astype(LOW)
            start = pl.multiple_of((info[1] ^ h) * WIDE + i * PART, 128)
            total[:, pl.ds(start, PART)] = jnp.sum(value.astype(F32), 0, keepdims=True)
            out[:, at] = value


def norm_back(part, z, scale, gain):
    pz = part * z
    mean_e = jnp.mean(part * gain, -1, keepdims=True)
    mean_ez = jnp.mean(pz * gain, -1, keepdims=True)
    return scale * ((part * gain - mean_e) - z * mean_ez), pz


def fold(values):
    return jnp.sum(values.reshape(ROWS // 8, 8, D), 0)


def hidden_back_body(dy, standard, scales, vecs, d_own, d_par, own, par, dh, dp, sums, acc):
    acc[...] = dot(joined(d_own, d_par), joined(own, par), 1, 1)

    def back(at, carry):
        part = acc[at, :]
        value, pz = norm_back(part, standard[at, :], scales[at, 0:1], vecs[2:3, :])
        value = dy[at, :].astype(F32) + value
        dh[at, :] = value
        low = value.astype(LOW)
        dp[at, :] = low
        gain, shift, bias = carry
        return gain + fold(pz), shift + fold(part), bias + fold(low.astype(F32))

    zero = jnp.zeros((8, D), F32)
    totals = row_loop(acc.shape[0], back, (zero, zero, zero))
    for r in range(3):
        sums[r : r + 1, :] = jnp.sum(totals[r], 0, keepdims=True)


def attend_back_body(slots, visible, qkv, logs, dp, out_weight, dqkv, sums, mixed):
    mixed[...] = dot(dp[...], out_weight[:, 3 * HALF : 4 * HALF]).astype(LOW)
    slot = lax.broadcasted_iota(jnp.int32, (slots, 1), 0)
    sums[...] = jnp.zeros_like(sums)
    for s, j, at in blocks_of(slots, qkv.shape[0]):
        cols = [slice(i * HALF + j * 128, i * HALF + (j + 1) * 128) for i in range(3)]
        query, key, value = (qkv[at, c] for c in cols)
        query = by_head(query * SCALE)
        grad = by_head(mixed[at, j * 128 : (j + 1) * 128])
        row = s * (HALF // 128) + j
        soft = jnp.exp(scores_of(key, query, slot < visible[s]) - logs[row : row + 1, :])
        grad_soft = dot(value, grad, 1, 1)
        inner = jnp.sum(soft * grad_soft, 0, keepdims=True)
        grad_scores = (soft * (grad_soft - inner)).astype(LOW)
        grads = (
            from_columns(dot(key.T, grad_scores), slots) * SCALE,
            dot(grad_scores, query),
            dot(soft.astype(LOW), grad),
        )
        for i, value in enumerate(grads):
            low = value.astype(LOW)
            dqkv[at, cols[i]] = low
            if i != 1:
                sums[i : i + 1, j * 128 : (j + 1) * 128] += jnp.sum(
                    low.astype(F32), 0, keepdims=True
                )


def token_back_body(
    share, info, tokens, dh, vecs, sums_two, dy_sum, up_sum, sums_own, sums_par, d_own, d_par, own, par,
    out, block, acc, sums,
):
    cols = slice(0, 3 * HALF)
    acc[...] = dot(joined(d_own, d_par), joined(own.at[:, cols], par.at[:, cols]), 1, 1)

    def back(at, carry):
        part = acc[at, :]
        z, scale = standardize(tokens[at, :].astype(F32))
        value, pz = norm_back(part, z, scale, vecs[0:1, :])
        out[at, :] = (dh[at, :] + value).astype(LOW)
        gain, shift = carry
        return gain + fold(pz), shift + fold(part)

    zero = jnp.zeros((8, D), F32)
    totals = row_loop(acc.shape[0], back, (zero, zero))
    sums[...] = jnp.zeros_like(sums)
    for r in range(2):
        sums[r : r + 1, :] = jnp.sum(totals[r], 0, keepdims=True)
    sums[2:5, :] = sums_two[0:3, :]
    sums[5:6, :] = dy_sum[0:1, :]
    for flip, part in enumerate((sums_own, sums_par)):
        half = half_of(info, flip, HALF)
        sums[6:7, half] = part[0:1, :]
        sums[7:8, half] = part[2:3, :]
    block[...] = sums[...].T
    for d in range(D // share):
        part = up_sum[0:1, 4 * share * d : 4 * share * (d + 1)]
        block[share * d : share * d + 1, UP_LANE : UP_LANE + 4 * share] = part


def outer(left, left_far, right, right_far):
    return dot(joined(left, left_far), joined(right, right_far, 0))


def pair_grads(info, blocks, sends, grad):
    send_a, keep_a, send_b, keep_b = sends
    width = keep_a.shape[2]
    at = 0
    for block in blocks:
        value = block().astype(LOW)
        count = value.shape[1]
        grad[:, :count] = value
        split = min(max(width - at, 0), count)
        if split:
            cols = slice(at, at + split)
            part = grad.at[:, :split]
            spread(info[0], part, send_a.at[:, :, cols], keep_a.at[:, :, cols], SEND_A, KEEP_A)
        if split < count:
            cols = slice(at + split - width, at + count - width)
            part = grad.at[:, split:count]
            spread(info[0], part, send_b.at[:, :, cols], keep_b.at[:, :, cols], SEND_B, KEEP_B)
        at += count


def steps_of(left, left_far, right, right_far):
    for at in range(0, right.shape[1], STEP):
        at = slice(at, min(at + STEP, right.shape[1]))
        yield functools.partial(outer, left, left_far, right.at[:, at], right_far.at[:, at])


def grad_body(index, info, near, far, right, right_far, *rest):
    left = [b.at[index * D : (index + 1) * D, :] for b in (near, far)]
    pair_grads(info, steps_of(*left, right, right_far), rest[:4], rest[4])


def qkv_grad_body(info, near, far, dqkv, dqkv_far, dp, dp_far, mixed, mixed_far, *rest):
    def out():
        return dot(joined(dp, dp_far, 0), joined(mixed, mixed_far, 0), 0, 0)

    left = [b.at[2 * D : 3 * D, :] for b in (near, far)]
    pair_grads(info, [*steps_of(*left, dqkv, dqkv_far), out], rest[:4], rest[4])


def pick(flag, left, right):
    return jnp.where(flag, left, right)


def half_major(matrix):
    rows = matrix.shape[0]
    return matrix.reshape(rows, 3, 2, HALF).transpose(0, 2, 1, 3).reshape(rows, 3 * D)


def third_major(matrix):
    rows = matrix.shape[0]
    return matrix.reshape(rows, 2, 3, HALF).transpose(0, 2, 1, 3).reshape(rows, 3 * D)


class WholeComm:
    touch = ()

    def __init__(self, count):
        self.info = jnp.zeros((2,), jnp.int32)

    def order(self, low, high):
        return low, high

    def weights(self, call, small, bias_up, w_qkv, w_out, w_up, w_down):
        def gather(value):
            return lax.all_gather(value, "dp", axis=0, tiled=True)

        def half(matrix, h):
            width = matrix.shape[1] // 2
            return matrix[:, h * width : (h + 1) * width]

        block = jnp.pad(small.T, ((0, 0), (0, 128 - small.shape[0])))
        block = gather(block.at[0, UP_LANE : UP_LANE + bias_up.shape[1]].set(bias_up[0]))
        qkv, out, up = (gather(w) for w in (half_major(w_qkv), w_out, w_up))
        self.first = [jnp.concatenate([half(qkv, h), half(out, h), block], 1) for h in range(2)]
        self.held = {1: [half(up, h) for h in range(2)]}
        down = gather(w_down)
        self.held[2] = [half(down, h) for h in range(2)]

    def step(self, call):
        pass

    def advance(self, call):
        pass

    def gather_step(self, call, step):
        pass

    def pump(self, call, index, *touch):
        pass

    def reduce(self, value):
        return lax.psum_scatter(value, "dp", scatter_dimension=0, tiled=True)

    def far(self, array):
        return array

    def reduce_down(self, call, near, far, gated, gated_far):
        self.down = self.reduce(dot(near[D : 2 * D], jnp.concatenate([gated, gated_far], 1)))

    def reduce_up(self, call, near, far, raised, raised_far):
        self.up = self.reduce(dot(near[:D], jnp.concatenate([raised, raised_far], 1)))

    def reduce_qkv(self, call, near, far, triple, triple_far, dp, dp_far, mixed, mixed_far):
        triple = jnp.concatenate([triple, triple_far], 1)
        self.qkv = third_major(self.reduce(dot(near[2 * D :], triple)))
        mixed = jnp.concatenate([mixed, mixed_far], 1)
        self.out = self.reduce(dot(dp, mixed, 0, 0))

    def reduce_block(self, call, block):
        self.vec = self.reduce(block)

    def results(self, call):
        return self.down, self.up, self.out, self.qkv, self.vec


class GridComm:
    def __init__(self):
        index = lax.axis_index("dp")
        self.info = jnp.stack([index >> 1, index & 1]).astype(jnp.int32)
        self.is_first = (index & 1) == 0
        self.jobs = []

    def order(self, low, high):
        return pick(self.is_first, low, high), pick(self.is_first, high, low)

    def weights(self, call, small, bias_up, w_qkv, w_out, w_up, w_down):
        rows = w_qkv.shape[0]
        total = sum(width for width, _ in CHUNKS)
        total_a = sum(cut for _, cut in CHUNKS)
        parts = (w_qkv, w_out, w_up, w_down)
        mine, other = call(
            pack_body,
            [shape((rows, total))] * 2,
            [small, bias_up, *parts],
            info=self.info,
            in_hbm=(2, 3, 4, 5),
            scratch=[pltpu.VMEM((128, 128), F32)]
            + [pltpu.VMEM(w.shape, LOW) for w in parts]
            + [pltpu.SemaphoreType.DMA],
        )
        wide = CHUNKS[1][0]
        unit, self.units, unit_a, unit_b = call(
            unit_body,
            [
                shape((48, CHUNKS[0][0])), shape((2, 48, wide)),
                shape((48, total_a)), shape((48, total - total_a)),
            ],
            [mine, swap(other, 1)],
            info=self.info,
        )
        self.own = [unit_a, swap(unit_a, 4), unit_b, swap(unit_b, 2)]
        self.lines = [swap(unit, bit) for bit in (8, 16, 24)]
        self.plan = self.schedule(call)

    def advance(self, call):
        next(self.plan)

    def pair(self, call, index, far):
        (pair,) = call(
            functools.partial(pair_body, index - 1), [shape(self.units.shape)], [self.units, far]
        )
        return [far, swap(pair, 8)]

    def schedule(self, call):
        width, cut = CHUNKS[0]
        pair_a, pair_b = call(
            own_body, [shape((2, 48, cut)), shape((2, 48, width - cut))], self.own
        )
        pairs = [pair_a, swap(pair_a, 2), pair_b, swap(pair_b, 4)]
        yield
        a, b, again = call(
            functools.partial(first_stack_body, cut, 0),
            [shape((3, 48, cut)), shape((3, 48, width - cut)), shape(self.units.shape[1:])],
            [*self.lines, self.units],
            touch=(pairs[1], pairs[3]),
        )
        stacked = [a, swap(a, 4), b, swap(b, 2)]
        far_one = swap(again, 16)
        joined = self.join(call, 0, stacked)
        line_one = self.pair(call, 1, far_one)
        (own,) = self.finish(call, 0, joined, pairs)
        self.first = [own, swap(own, 1)]
        self.line = {1: line_one}
        self.held = {}
        yield

    def gather_step(self, call, step):
        index = 1 if step in "SJf" else 2
        if step == "P":
            self.line[2] = self.pair(call, 2, self.line[2])
        elif step == "S":
            width, cut = CHUNKS[1]
            a, b, again = call(
                functools.partial(first_stack_body, cut, 1),
                [shape((3, 48, cut)), shape((3, 48, width - cut)), shape(self.units.shape[1:])],
                [*self.line[1], self.units],
            )
            self.held[1] = [a, swap(a, 4), b, swap(b, 2)]
            self.line[2] = swap(again, 16)
        elif step == "s":
            self.held[2] = self.stack(call, 2, self.line[2])
        elif step in "Jj":
            self.held[index] = self.join(call, index, self.held[index])
        else:
            (own,) = self.finish(call, index, self.held[index])
            self.held[index] = [own, swap(own, 1)]

    def starts(self, index):
        return (
            sum(c for _, c in CHUNKS[:index]),
            sum(w - c for w, c in CHUNKS[:index]),
        )

    def stack(self, call, index, line, touch=()):
        width, cut = CHUNKS[index]
        a, b = call(
            functools.partial(stack_body, cut),
            [shape((3, 48, cut)), shape((3, 48, width - cut))],
            line,
            touch=touch,
        )
        return a, swap(a, 4), b, swap(b, 2)

    def join(self, call, index, stacked, touch=()):
        width, cut = CHUNKS[index]
        count = 6 if index == 0 else 8
        a, b = call(
            functools.partial(join_body, *self.starts(index)),
            [shape((count, 48, cut)), shape((count, 48, width - cut))],
            [*stacked] + ([] if index == 0 else self.own),
            touch=touch,
        )
        return a, swap(a, 2), b, swap(b, 4)

    def finish(self, call, index, joined, pairs=()):
        width, cut = CHUNKS[index]
        z = (8, 4, 12) if index else Z_CODES[1:]
        codes_a = z + tuple(c ^ 2 for c in z)
        codes_b = z + tuple(c ^ 1 for c in z)
        if index:
            codes_a, codes_b = (0, 2) + codes_a, (0, 1) + codes_b
        plan = []
        for codes_a, codes_b in [(codes_a, codes_b)] + ([((0, 2), (0, 1))] if pairs else []):
            plan += [
                (codes_a, 0, 0, cut),
                (tuple(c ^ 1 for c in codes_a), 0, 0, cut),
                (codes_b, 0, cut, width - cut),
                (tuple(c ^ 2 for c in codes_b), 0, cut, width - cut),
            ]
        return call(
            functools.partial(place_body, plan),
            [shape((D, width))],
            [*joined, *pairs],
            info=self.info,
            scratch=[pltpu.SemaphoreType.DMA],
        )

    def pieces(self, width_a, width_b):
        return [shape((8, 48, w)) for w in (width_a, width_a, width_b, width_b)]

    def job(self, call, name, parts, body, outs, direct):
        send_a, keep_a, send_b, keep_b = parts
        width_a, width_b = keep_a.shape[2], keep_b.shape[2]
        width = width_a + width_b
        far_a, far_b = swap(send_a, 2), swap(send_b, 4)
        yield
        send_a, keep_a, send_b, keep_b = call(
            first_sum_body,
            [shape((4, 48, w)) for w in (width_a, width_a, width_b, width_b)],
            [far_a, keep_a, far_b, keep_b],
            touch=self.touch,
        )
        far_a, far_b = swap(send_a, 4), swap(send_b, 2)
        yield
        if direct:
            width += 128
            own, *lines = call(
                second_sum_block_body,
                [shape((48, width))] * 4,
                [far_a, keep_a, far_b, keep_b, *self.block],
            )
            lines = [swap(line, bit) for line, bit in zip(lines, (8, 16, 24))]
            yield
            last_body, lines = last_sum_body, [own, *lines]
        else:
            own, send = call(
                second_sum_body, [shape((2, 48, width))] * 2, [far_a, keep_a, far_b, keep_b]
            )
            far = swap(send, 8)
            yield
            own, send = call(near_sum_body, [shape((48, width))] * 2, [own, far])
            far = swap(send, 16)
            yield
            last_body, lines = last_near_body, [own, far]
        mine, other = call(
            last_body,
            [shape((24, width), F32)] * 2,
            lines,
            info=self.info,
            scratch=[pltpu.VMEM((48, width), F32)],
        )
        other = swap(other, 1)
        yield
        self.outs[name] = call(body, outs, [mine, other], info=self.info, last=True)

    def begin(self, job):
        next(job)
        self.jobs.append(job)

    def pump(self, call, index, *touch):
        self.touch = touch
        return next(self.jobs[index], self) is not self

    def block_job(self, call, block):
        send, keep = call(
            block_body, [shape((8, 48, 128), F32)] * 2, [block], info=self.info
        )
        far = swap(send, 2)
        yield
        send, keep = call(block_sum_body, [shape((4, 48, 128), F32)] * 2, [far, keep])
        self.block = [swap(send, 4), keep]
        yield

    def results(self, call):
        (down,), (up,), (qkv, out, vec) = [self.outs[k] for k in ("down", "up", "qkv")]
        return down, up, out, qkv, vec

    def far(self, array):
        return swap(array, 1)

    def reduce_down(self, call, *args):
        self.outs = {}
        parts = call(
            functools.partial(grad_body, 1),
            self.pieces(768, 768),
            args,
            info=self.info,
            scratch=[pltpu.VMEM((D, STEP), LOW)],
            us=6,
        )
        self.begin(self.job(call, "down", parts, merge_one_body, [shape((24, FF), F32)], False))

    def reduce_up(self, call, *args):
        parts = call(
            functools.partial(grad_body, 0),
            self.pieces(768, 768),
            args,
            info=self.info,
            scratch=[pltpu.VMEM((D, STEP), LOW)],
            us=6,
        )
        self.begin(self.job(call, "up", parts, merge_one_body, [shape((24, FF), F32)], False))

    def reduce_qkv(self, call, *args):
        parts = call(
            qkv_grad_body,
            self.pieces(768, 768),
            args,
            info=self.info,
            scratch=[pltpu.VMEM((D, STEP), LOW)],
            us=6,
        )
        outs = [shape((24, 3 * D), F32), shape((24, D), F32), shape((24, 128), F32)]
        self.begin(self.job(call, "qkv", parts, merge_qkv_body, outs, True))

    def reduce_block(self, call, block):
        self.begin(self.block_job(call, block))


def shards(count, tokens, lengths, source, cotangent, w_qkv, w_out, w_up, w_down, *small):
    (
        gain_one, shift_one, bias_query, bias_value, bias_out, gain_two, shift_two,
        bias_up, bias_down,
    ) = small
    seqs, slots = tokens.shape[:2]
    rows = seqs * slots
    share = gain_one.shape[0]
    comm = GridComm() if count == 32 else WholeComm(count)
    visible = jnp.where(source == 1, lengths, IMG_LEN)
    tokens = tokens.reshape(rows, D)
    cotangent = cotangent.reshape(rows, D)
    small = jnp.stack(
        [gain_one, shift_one, gain_two, shift_two, bias_out, bias_down, bias_query, bias_value]
    )
    bias_up = bias_up[None]
    call = Chain([tokens, cotangent, small, bias_up])

    act = shape((rows, D))
    act_f = shape((rows, D), F32)
    half = shape((rows, HALF))
    triple = shape((rows, 3 * HALF))
    wide = shape((rows, WIDE))

    def attend(part, *touch):
        return call(
            functools.partial(attend_body, slots),
            [half, shape((8, 2 * slots), F32)],
            [part],
            info=visible,
            us=4.3,
            touch=touch,
        )

    comm.weights(call, small, bias_up, w_qkv, w_out.T, w_up, w_down.T)
    comm.advance(call)
    dy, dy_sum = call(
        functools.partial(start_body, slots),
        [act, shape((8, D), F32)],
        [cotangent],
        info=visible,
    )
    comm.advance(call)
    for step in EARLY:
        if step == "k":
            normed_one, qkv_own, vecs = call(
                qkv_body,
                [act, triple, shape((16, D), F32)],
                [tokens, comm.first[0]],
                info=comm.info,
                us=4.3,
            )
        elif step == "l":
            o_own, logs_own = attend(qkv_own)
        elif step == "m":
            qkv_par, bias_up = call(
                functools.partial(qkv_far_body, share),
                [triple, shape((1, FF), F32)],
                [normed_one, comm.first[0], comm.first[1], vecs],
                info=comm.info,
                us=2.5,
            )
        elif step == "n":
            o_par, logs_par = attend(qkv_par)
            o_far = comm.far(o_par)
        elif step == "h":
            hidden, normed_two, standard, scales = call(
                hidden_body,
                [act_f, act, act_f, shape((rows, 128), F32)],
                [tokens, vecs, o_own, o_par, *comm.first],
                us=4,
            )
        elif step == "t":
            (near,) = call(
                turn_body, [shape((3 * D, rows))], [normed_two, dy, normed_one], touch=(o_far,), us=3
            )
            far = comm.far(near)
        elif step in "gG":
            flip = 0 if step == "g" else 1
            values = call(
                functools.partial(raise_body, flip),
                [wide] * 2,
                [normed_two, bias_up, comm.held[1][flip]],
                info=comm.info,
                us=3.7,
            )
            if step == "g":
                gated, slope = values
            else:
                gated_par, slope_par = values
                gated_far = comm.far(gated_par)
        elif step == "d":
            comm.reduce_down(call, near, far, gated, gated_far)
        else:
            comm.gather_step(call, step)
    second = comm.held[1]
    third = comm.held[2]
    raised, raised_par, up_sum = call(
        raise_back_body,
        [wide, wide, shape((1, FF), F32)],
        [dy, slope, slope_par, *third],
        info=comm.info,
        us=4.8,
    )
    raised_far = comm.far(raised_par)
    grad_hidden, branch, sums_two = call(
        hidden_back_body,
        [act_f, act, shape((8, D), F32)],
        [dy, standard, scales, vecs, raised, raised_par, *second],
        scratch=[pltpu.VMEM((rows, D), F32)],
        us=6.6,
    )
    branch_far = comm.far(branch)

    def attend_back(part, logs, weight, *touch):
        return call(
            functools.partial(attend_back_body, slots),
            [triple, shape((8, HALF), F32)],
            [part, logs, branch, weight],
            info=visible,
            scratch=[pltpu.VMEM((rows, HALF), LOW)],
            touch=touch,
            us=8.2,
        )

    sums = [branch_far]
    for step in ORDER:
        if step == "p":
            triple_par, sums_par = attend_back(qkv_par, logs_par, comm.first[1])
            triple_far = comm.far(triple_par)
        elif step == "o":
            triple_own, sums_own = attend_back(qkv_own, logs_own, comm.first[0])
        elif step == "u":
            comm.reduce_up(call, near, far, raised, raised_far)
        elif step == "q":
            comm.reduce_qkv(
                call, near, far, triple_own, triple_far, branch, branch_far, o_own, o_far
            )
        elif step == "t":
            grad_tokens, block = call(
                functools.partial(token_back_body, share),
                [act, shape((D, 128), F32)],
                [
                    tokens, grad_hidden, vecs, sums_two, dy_sum, up_sum, sums_own, sums_par,
                    triple_own, triple_par, *comm.first,
                ],
                info=comm.info,
                scratch=[pltpu.VMEM((rows, D), F32), pltpu.VMEM((128, D), F32)],
                us=6.5,
            )
        elif step == "b":
            comm.reduce_block(call, block)
        elif step == "m":
            (output,) = call(
                mix_body, [act], [hidden, vecs, gated, gated_par, *third], us=4.1, last=True
            )
        else:
            comm.pump(call, int(step), *sums)
            sums = []
    g_down_t, g_up, g_out_t, g_qkv, g_vec = comm.results(call)
    (
        g_gain_one, g_shift_one, g_gain_two, g_shift_two, g_bias_out, g_bias_down, g_query, g_value,
    ) = [g_vec[:, i] for i in range(8)]
    return (
        output.reshape(seqs, slots, D),
        grad_tokens.reshape(seqs, slots, D),
        g_qkv,
        g_out_t.T,
        g_up,
        g_down_t.T,
        g_gain_one, g_shift_one, g_query, g_value, g_bias_out, g_gain_two, g_shift_two,
        g_vec[0, UP_LANE : UP_LANE + 4 * share],
        g_bias_down,
    )


def solution(mesh):
    row, tall, wide, vec = P("dp", None, None), P("dp", None), P(None, "dp"), P("dp")
    in_specs = (row, vec, vec, row, tall, wide, tall, wide) + (vec,) * 9
    out_specs = (row, row, tall, wide, tall, wide) + (vec,) * 9
    body = functools.partial(shards, mesh.shape["dp"])
    return jax.shard_map(
        body, mesh=mesh, in_specs=in_specs, out_specs=out_specs, check_vma=False
    )
```

```python
import functools
import jax
import jax.numpy as jnp
import numpy as np
from jax import lax
from jax.experimental import pallas as pl
from jax.experimental.pallas import tpu as pltpu
from jax.sharding import PartitionSpec as P

HEADS = 12
HEAD_DIM = 64
IMG_LEN = 196
ALWAYS = 152
EPS = 1e-06
D = 768
FF = 3072
HALF = D // 2
WIDE = FF // 2
LOW = jnp.bfloat16
F32 = jnp.float32
STEP = 768
PART = 512
ROWS = 128
MARGIN = 10
PACE = 4
UP_LANE = 32
SCALE = HEAD_DIM ** (-0.5)
CHUNKS = ((4 * HALF + 128, 896), (WIDE, 768), (WIDE, 768))
Z_CODES = (0, 4, 8, 12)
SMEM = pl.BlockSpec(memory_space=pltpu.SMEM)
ANY = pl.BlockSpec(memory_space=pl.ANY)
VMEM = pl.BlockSpec(memory_space=pltpu.VMEM)


def shape(dims, kind=LOW):
    return jax.ShapeDtypeStruct(dims, kind)


class Chain:
    def __init__(self, loose):
        self.last = None
        self.loose = loose
        self.count = 0

    def near(self, array):
        if any(array is a for a in self.loose):
            return array
        return pltpu.with_memory_space_constraint(array, pltpu.VMEM)

    def __call__(
        self, body, outs, ins, *, info=None, touch=(), in_hbm=(), scratch=(), us=8, last=False
    ):
        us *= PACE
        if self.count < len(COSTS):
            us *= COSTS[self.count]
        self.count += 1
        head = [] if info is None else [info]
        ins = list(ins)
        count = len(head) + len(ins)
        specs = [SMEM] * len(head) + [ANY if i in in_hbm else VMEM for i in range(len(ins))]
        given = [
            pltpu.with_memory_space_constraint(a, pltpu.HBM) if i in in_hbm else self.near(a)
            for i, a in enumerate(ins)
        ]
        extra = list(touch) + ([] if self.last is None else [self.last])
        total = count + len(extra)

        def run(*refs):
            body(*refs[:count], *refs[total:])

        held = sum(
            int(np.prod(k.shape)) * jnp.dtype(k.dtype).itemsize
            for k in scratch
            if getattr(k, "shape", ())
        )
        size = sum(a.size * a.dtype.itemsize for a in [*ins, *outs])
        results = pl.pallas_call(
            run,
            out_shape=tuple(outs if last else [pltpu.VMEM(o.shape, o.dtype) for o in outs]),
            in_specs=specs + [ANY] * len(extra),
            out_specs=(VMEM,) * len(outs),
            scratch_shapes=list(scratch),
            compiler_params=pltpu.CompilerParams(vmem_limit_bytes=held + MARGIN * 2**20),
            cost_estimate=pl.CostEstimate(
                flops=int(us * 1.1e9), bytes_accessed=size, transcendentals=0
            ),
        )(*head, *given, *extra)
        self.last = min(results, key=lambda r: r.size * r.dtype.itemsize)
        return results


def dot(left, right, left_dim=1, right_dim=0):
    return lax.dot_general(
        left, right, (((left_dim,), (right_dim,)), ((), ())), preferred_element_type=F32
    )


def joined(own, par, axis=1):
    return jnp.concatenate([own[...], par[...]], axis)


def standardize(values):
    center = values - jnp.mean(values, -1, keepdims=True)
    scale = lax.rsqrt(jnp.mean(center * center, -1, keepdims=True) + EPS)
    return center * scale, scale


def row_loop(rows, body, init=0):
    def step(i, carry):
        return body(pl.ds(pl.multiple_of(i * ROWS, ROWS), ROWS), carry)

    return lax.fori_loop(0, rows // ROWS, step, init)


def swap(value, bit):
    pairs = [(i, i ^ bit) for i in range(32)]
    return lax.ppermute(value, "dp", pairs)


def pack_body(info, small, bias_up, *refs):
    weights, (mine, other), (rows, *held, sem) = refs[:4], refs[4:6], refs[6:]
    copies = [pltpu.make_async_copy(w, v, sem) for w, v in zip(weights, held)]
    for copy in copies:
        copy.start()
    w_qkv, w_out, w_up, w_down = held
    rows[...] = jnp.zeros_like(rows)
    share = w_qkv.shape[0]
    rows[: small.shape[0], :share] = small[...].astype(F32)
    rows[...] = rows[...].T
    rows[0:1, UP_LANE : UP_LANE + 4 * share] = bias_up[...].astype(F32)
    block = rows[:share, :].astype(LOW)
    for copy in copies:
        copy.wait()
    for flip, out in enumerate((mine, other)):
        h = info[1] ^ flip

        def half(weight, width, start=0):
            return weight[:, pl.ds(pl.multiple_of(start + h * width, 128), width)]

        for i in range(3):
            out[:, i * HALF : (i + 1) * HALF] = half(w_qkv, HALF, i * D)
        out[:, 3 * HALF : 4 * HALF] = half(w_out, HALF)
        at = CHUNKS[0][0]
        out[:, 4 * HALF : at] = block
        out[:, at : at + WIDE] = half(w_up, WIDE)
        out[:, at + WIDE :] = half(w_down, WIDE)


def unit_body(info, mine, other, unit_one, units, unit_a, unit_b):
    a, b = mine[...].astype(F32), other[...].astype(F32)
    unit = jnp.where(
        info[1] == 0, jnp.concatenate([a, b], 0), jnp.concatenate([b, a], 0)
    ).astype(LOW)
    start = at_a = at_b = 0
    for i, (width, cut) in enumerate(CHUNKS):
        part = unit[:, start : start + width]
        if i == 0:
            unit_one[...] = part
        else:
            units[i - 1] = part
        unit_a[:, at_a : at_a + cut] = part[:, :cut]
        unit_b[:, at_b : at_b + width - cut] = part[:, cut:]
        start, at_a, at_b = start + width, at_a + cut, at_b + width - cut


def own_body(unit_a, far_a, unit_b, far_b, pair_a, pair_b):
    for pair, unit, far in ((pair_a, unit_a, far_a), (pair_b, unit_b, far_b)):
        width = pair.shape[2]
        pair[0] = unit[:, :width]
        pair[1] = far[:, :width]


def pair_body(index, units, far, pair):
    pair[0] = units[index]
    pair[1] = far[...]


def stack_body(cut, *refs):
    pieces, (stack_a, stack_b) = refs[:-2], refs[-2:]
    at = 0
    for piece in pieces:
        for i in range(piece.shape[0] if len(piece.shape) == 3 else 1):
            part = piece.at[i] if len(piece.shape) == 3 else piece
            stack_a[at] = part[:, :cut]
            stack_b[at] = part[:, cut:]
            at += 1


def first_stack_body(cut, index, *refs):
    *pieces, units, stack_a, stack_b, again = refs
    stack_body(cut, *pieces, stack_a, stack_b)
    again[...] = units[index]


def join_body(start_a, start_b, *refs):
    stacks, own, (join_a, join_b) = refs[:4], refs[4:-2], refs[-2:]
    for side, join, start in ((0, join_a, start_a), (1, join_b, start_b)):
        width = join.shape[2]
        parts = own[2 * side : 2 * side + 2]
        for i, part in enumerate(parts):
            join[i] = part[:, start : start + width]
        at = len(parts)
        join[at : at + 3] = stacks[2 * side][...]
        join[at + 3 : at + 6] = stacks[2 * side + 1][...]


def place_body(plan, info, *refs):
    pieces, out, sem = refs[:-2], refs[-2], refs[-1]
    copies = []
    for piece, (codes, source, target, width) in zip(pieces, plan):
        for i, code in enumerate(codes):
            row = pl.multiple_of((info[0] ^ code) * 48, 48)
            copies.append(
                pltpu.make_async_copy(
                    piece.at[i, :, pl.ds(source, width)],
                    out.at[pl.ds(row, 48), pl.ds(target, width)],
                    sem,
                )
            )
    for copy in copies:
        copy.start()
    for copy in copies:
        copy.wait()


ORDER = "up0o1q0tm1b02310210122"
EARLY = "SkJPlmsnhftjgGFd"
COSTS = ()
KEEP_A = tuple(c ^ y for y in (0, 2) for c in Z_CODES)
KEEP_B = tuple(c ^ x for x in (0, 1) for c in Z_CODES)
SEND_A = tuple(c ^ 1 for c in KEEP_A)
SEND_B = tuple(c ^ 2 for c in KEEP_B)


def spread(chip, grad, send, keep, send_codes, keep_codes):
    for out, codes in ((send, send_codes), (keep, keep_codes)):
        for i, code in enumerate(codes):
            row = pl.multiple_of((chip ^ code) * 48, 48)
            out[i] = grad[pl.ds(row, 48), :].astype(out.dtype)


def add(left, right):
    return (left.astype(F32) + right.astype(F32)).astype(LOW)


def first_sum_body(far_a, keep_a, far_b, keep_b, send_a, own_a, send_b, own_b):
    for far, keep, send, own in ((far_a, keep_a, send_a, own_a), (far_b, keep_b, send_b, own_b)):
        for i in range(4):
            send[i] = add(far[4 + i], keep[4 + i])
            own[i] = add(far[i], keep[i])


def second_sum_body(far_a, keep_a, far_b, keep_b, *outs):
    cut = keep_a.shape[2]
    for i in range(4):
        out = outs[i] if len(outs) == 4 else outs[i % 2].at[i // 2]
        out[:, :cut] = add(far_a[i], keep_a[i])
        out[:, cut:] = add(far_b[i], keep_b[i])


def last_sum_body(info, own, z_one, z_two, z_three, mine, other, total):
    value = own[...].astype(F32)
    for piece in (z_one, z_two, z_three):
        value = value + piece[...].astype(F32)
    total[...] = value
    split_rows(info, total, mine, other)


def split_rows(info, total, mine, other):
    rows = mine.shape[0]
    mine[...] = total[pl.ds(pl.multiple_of(info[1] * rows, 8), rows), :]
    other[...] = total[pl.ds(pl.multiple_of((1 - info[1]) * rows, 8), rows), :]


def merge(info, mine, other, start, width, out, count=1):
    for flip, part in enumerate((mine, other)):
        h = info[1] ^ flip
        for i in range(count):
            at = pl.multiple_of((2 * i + h) * width, 128)
            out[:, pl.ds(at, width)] = part[:, start + i * width : start + (i + 1) * width]


def merge_one_body(info, mine, other, out):
    merge(info, mine, other, 0, WIDE, out)


def merge_qkv_body(info, mine, other, out_qkv, out_out, vec):
    merge(info, mine, other, 0, HALF, out_qkv, 3)
    merge(info, mine, other, 3 * HALF, HALF, out_out)
    vec[...] = mine[:, 4 * HALF :] + other[:, 4 * HALF :]


def near_sum_body(own, far, keep, send):
    keep[...] = add(own[0], far[0])
    send[...] = add(own[1], far[1])


def last_near_body(info, keep, far, mine, other, total):
    total[...] = keep[...].astype(F32) + far[...].astype(F32)
    split_rows(info, total, mine, other)


def block_body(info, block, send, keep):
    spread(info[0], block, send, keep, SEND_A, KEEP_A)


def block_sum_body(far, keep, send, own):
    count = keep.shape[0] // 2
    own[...] = far[:count] + keep[:count]
    send[...] = far[count:] + keep[count:]


def second_sum_block_body(far_a, keep_a, far_b, keep_b, far_v, keep_v, *outs):
    width = keep_a.shape[2] + keep_b.shape[2]
    second_sum_body(far_a, keep_a, far_b, keep_b, *(o.at[:, :width] for o in outs))
    for i, out in enumerate(outs):
        out[:, width:] = (far_v[i] + keep_v[i]).astype(LOW)


def start_body(slots, visible, cot, dy, total):
    rows = cot.shape[0]
    total[...] = jnp.zeros_like(total)
    for s in range(rows // slots):
        live = lax.broadcasted_iota(jnp.int32, (slots, 1), 0) < visible[s]
        part = jnp.where(live, cot[s * slots : (s + 1) * slots, :].astype(F32), 0.0)
        dy[s * slots : (s + 1) * slots, :] = part.astype(LOW)
        total[0:1, :] += jnp.sum(part, 0, keepdims=True)


def qkv_body(info, tokens, own, normed, qkv, vecs):
    vecs[...] = own[:, 4 * HALF :].astype(F32).T[:16, :]

    def norm(at, carry):
        z, _ = standardize(tokens[at, :].astype(F32))
        normed[at, :] = (z * vecs[0:1, :] + vecs[1:2, :]).astype(LOW)
        return carry

    row_loop(tokens.shape[0], norm)
    project_qkv(info, 0, normed, own, vecs, qkv)


def project_qkv(info, flip, normed, weight, vecs, out):
    half = half_of(info, flip, HALF)
    bias = [vecs[6:7, half], jnp.zeros((1, HALF), F32), vecs[7:8, half]]
    value = dot(normed[...], weight[:, : 3 * HALF]) + jnp.concatenate(bias, 1)
    out[...] = value.astype(LOW)


def qkv_far_body(share, info, normed, own, weight, vecs, qkv, bias_up):
    project_qkv(info, 1, normed, weight, vecs, qkv)
    for d in range(D // share):
        row = own[d * share // 16 * 16 : d * share // 16 * 16 + 16, 4 * HALF :].astype(F32)
        at = d * share % 16
        bias_up[0:1, 4 * share * d : 4 * share * (d + 1)] = row[
            at : at + 1, UP_LANE : UP_LANE + 4 * share
        ]


def by_head(block):
    lane = lax.broadcasted_iota(jnp.int32, (1, 128), 1)
    return jnp.concatenate(
        [jnp.where(lane < HEAD_DIM, block, 0), jnp.where(lane >= HEAD_DIM, block, 0)], 0
    )


def scores_of(key, query, live):
    scores = dot(key, query, 1, 1)
    return jnp.concatenate(
        [scores[:ALWAYS], jnp.where(live[ALWAYS:], scores[ALWAYS:], -1e30)], 0
    )


def from_columns(values, slots):
    return jnp.concatenate(
        [values[:HEAD_DIM, :slots], values[HEAD_DIM:, slots:]], 0
    ).T


def blocks_of(slots, rows):
    for s in range(rows // slots):
        for j in range(HALF // 128):
            yield s, j, slice(s * slots, (s + 1) * slots)


def attend_body(slots, visible, qkv, out, logs):
    slot = lax.broadcasted_iota(jnp.int32, (slots, 1), 0)
    for s, j, at in blocks_of(slots, qkv.shape[0]):
        query, key, value = (
            qkv[at, i * HALF + j * 128 : i * HALF + (j + 1) * 128] for i in range(3)
        )
        scores = scores_of(key, by_head(query * SCALE), slot < visible[s])
        top = jnp.max(scores, 0, keepdims=True)
        power = jnp.exp(scores - top)
        total = jnp.sum(power, 0, keepdims=True)
        row = s * (HALF // 128) + j
        logs[row : row + 1, :] = top + jnp.log(total)
        mixed = dot(value.T, (power * (1.0 / total)).astype(LOW))
        out[at, j * 128 : (j + 1) * 128] = from_columns(mixed, slots).astype(LOW)


def hidden_body(tokens, vecs, o_own, o_par, own, par, hidden, normed, standard, scales):
    out_cols = slice(3 * HALF, 4 * HALF)
    hidden[...] = dot(joined(o_own, o_par), joined(own.at[:, out_cols], par.at[:, out_cols]), 1, 1)

    def norm(at, carry):
        value = tokens[at, :].astype(F32) + (hidden[at, :] + vecs[4:5, :])
        hidden[at, :] = value
        z, scale = standardize(value)
        standard[at, :] = z
        scales[at, :] = jnp.broadcast_to(scale, (ROWS, 128))
        normed[at, :] = (z * vecs[2:3, :] + vecs[3:4, :]).astype(LOW)
        return carry

    row_loop(tokens.shape[0], norm)


def turn_body(normed_two, dy, normed_one, out):
    for i, array in enumerate((normed_two, dy, normed_one)):
        out[i * D : (i + 1) * D, :] = array[...].T


GELU_A = 0.7978845608028654
GELU_B = 0.044715


def raise_body(flip, info, normed, bias, weight, gate, slope):
    for i in range(WIDE // PART):
        at = slice(i * PART, (i + 1) * PART)
        start = pl.multiple_of((info[1] ^ flip) * WIDE + i * PART, 128)
        u = dot(normed[...], weight[:, at]) + bias[:, pl.ds(start, PART)]
        square = u * u
        t = jnp.tanh(u * (GELU_A + (GELU_A * GELU_B) * square))
        lift = 0.5 + 0.5 * t
        gated = u * lift
        curve = GELU_A + (3.0 * GELU_A * GELU_B) * square
        slope[:, at] = (lift + (gated * (1.0 - t)) * curve).astype(LOW)
        gate[:, at] = gated.astype(LOW)


def half_of(info, flip, width):
    return pl.ds(pl.multiple_of((info[1] ^ flip) * width, 128), width)


def mix_body(hidden, vecs, a_own, a_par, own, par, out):
    value = dot(joined(a_own, a_par), joined(own, par), 1, 1)
    out[...] = (hidden[...] + (value + vecs[5:6, :])).astype(LOW)


def raise_back_body(info, dy, s_own, s_par, own, par, d_own, d_par, total):
    for i in range(WIDE // PART):
        at = slice(i * PART, (i + 1) * PART)
        for h, (slope, weight, out) in enumerate(((s_own, own, d_own), (s_par, par, d_par))):
            value = (dot(dy[...], weight[:, at]) * slope[:, at].astype(F32)).astype(LOW)
            start = pl.multiple_of((info[1] ^ h) * WIDE + i * PART, 128)
            total[:, pl.ds(start, PART)] = jnp.sum(value.astype(F32), 0, keepdims=True)
            out[:, at] = value


def norm_back(part, z, scale, gain):
    pz = part * z
    mean_e = jnp.mean(part * gain, -1, keepdims=True)
    mean_ez = jnp.mean(pz * gain, -1, keepdims=True)
    return scale * ((part * gain - mean_e) - z * mean_ez), pz


def fold(values):
    return jnp.sum(values.reshape(ROWS // 8, 8, D), 0)


def hidden_back_body(dy, standard, scales, vecs, d_own, d_par, own, par, dh, dp, sums, acc):
    acc[...] = dot(joined(d_own, d_par), joined(own, par), 1, 1)

    def back(at, carry):
        part = acc[at, :]
        value, pz = norm_back(part, standard[at, :], scales[at, 0:1], vecs[2:3, :])
        value = dy[at, :].astype(F32) + value
        dh[at, :] = value
        low = value.astype(LOW)
        dp[at, :] = low
        gain, shift, bias = carry
        return gain + fold(pz), shift + fold(part), bias + fold(low.astype(F32))

    zero = jnp.zeros((8, D), F32)
    totals = row_loop(acc.shape[0], back, (zero, zero, zero))
    for r in range(3):
        sums[r : r + 1, :] = jnp.sum(totals[r], 0, keepdims=True)


def attend_back_body(slots, visible, qkv, logs, dp, out_weight, dqkv, sums, mixed):
    mixed[...] = dot(dp[...], out_weight[:, 3 * HALF : 4 * HALF]).astype(LOW)
    slot = lax.broadcasted_iota(jnp.int32, (slots, 1), 0)
    sums[...] = jnp.zeros_like(sums)
    for s, j, at in blocks_of(slots, qkv.shape[0]):
        cols = [slice(i * HALF + j * 128, i * HALF + (j + 1) * 128) for i in range(3)]
        query, key, value = (qkv[at, c] for c in cols)
        query = by_head(query * SCALE)
        grad = by_head(mixed[at, j * 128 : (j + 1) * 128])
        row = s * (HALF // 128) + j
        soft = jnp.exp(scores_of(key, query, slot < visible[s]) - logs[row : row + 1, :])
        grad_soft = dot(value, grad, 1, 1)
        inner = jnp.sum(soft * grad_soft, 0, keepdims=True)
        grad_scores = (soft * (grad_soft - inner)).astype(LOW)
        grads = (
            from_columns(dot(key.T, grad_scores), slots) * SCALE,
            dot(grad_scores, query),
            dot(soft.astype(LOW), grad),
        )
        for i, value in enumerate(grads):
            low = value.astype(LOW)
            dqkv[at, cols[i]] = low
            if i != 1:
                sums[i : i + 1, j * 128 : (j + 1) * 128] += jnp.sum(
                    low.astype(F32), 0, keepdims=True
                )


def token_back_body(
    share, info, tokens, dh, vecs, sums_two, dy_sum, up_sum, sums_own, sums_par, d_own, d_par, own, par,
    out, block, acc, sums,
):
    cols = slice(0, 3 * HALF)
    acc[...] = dot(joined(d_own, d_par), joined(own.at[:, cols], par.at[:, cols]), 1, 1)

    def back(at, carry):
        part = acc[at, :]
        z, scale = standardize(tokens[at, :].astype(F32))
        value, pz = norm_back(part, z, scale, vecs[0:1, :])
        out[at, :] = (dh[at, :] + value).astype(LOW)
        gain, shift = carry
        return gain + fold(pz), shift + fold(part)

    zero = jnp.zeros((8, D), F32)
    totals = row_loop(acc.shape[0], back, (zero, zero))
    sums[...] = jnp.zeros_like(sums)
    for r in range(2):
        sums[r : r + 1, :] = jnp.sum(totals[r], 0, keepdims=True)
    sums[2:5, :] = sums_two[0:3, :]
    sums[5:6, :] = dy_sum[0:1, :]
    for flip, part in enumerate((sums_own, sums_par)):
        half = half_of(info, flip, HALF)
        sums[6:7, half] = part[0:1, :]
        sums[7:8, half] = part[2:3, :]
    block[...] = sums[...].T
    for d in range(D // share):
        part = up_sum[0:1, 4 * share * d : 4 * share * (d + 1)]
        block[share * d : share * d + 1, UP_LANE : UP_LANE + 4 * share] = part


def outer(left, left_far, right, right_far):
    return dot(joined(left, left_far), joined(right, right_far, 0))


def pair_grads(info, blocks, sends, grad):
    send_a, keep_a, send_b, keep_b = sends
    width = keep_a.shape[2]
    at = 0
    for block in blocks:
        value = block().astype(LOW)
        count = value.shape[1]
        grad[:, :count] = value
        split = min(max(width - at, 0), count)
        if split:
            cols = slice(at, at + split)
            part = grad.at[:, :split]
            spread(info[0], part, send_a.at[:, :, cols], keep_a.at[:, :, cols], SEND_A, KEEP_A)
        if split < count:
            cols = slice(at + split - width, at + count - width)
            part = grad.at[:, split:count]
            spread(info[0], part, send_b.at[:, :, cols], keep_b.at[:, :, cols], SEND_B, KEEP_B)
        at += count


def steps_of(left, left_far, right, right_far):
    for at in range(0, right.shape[1], STEP):
        at = slice(at, min(at + STEP, right.shape[1]))
        yield functools.partial(outer, left, left_far, right.at[:, at], right_far.at[:, at])


def grad_body(index, info, near, far, right, right_far, *rest):
    left = [b.at[index * D : (index + 1) * D, :] for b in (near, far)]
    pair_grads(info, steps_of(*left, right, right_far), rest[:4], rest[4])


def qkv_grad_body(info, near, far, dqkv, dqkv_far, dp, dp_far, mixed, mixed_far, *rest):
    def out():
        return dot(joined(dp, dp_far, 0), joined(mixed, mixed_far, 0), 0, 0)

    left = [b.at[2 * D : 3 * D, :] for b in (near, far)]
    pair_grads(info, [*steps_of(*left, dqkv, dqkv_far), out], rest[:4], rest[4])


def pick(flag, left, right):
    return jnp.where(flag, left, right)


def half_major(matrix):
    rows = matrix.shape[0]
    return matrix.reshape(rows, 3, 2, HALF).transpose(0, 2, 1, 3).reshape(rows, 3 * D)


def third_major(matrix):
    rows = matrix.shape[0]
    return matrix.reshape(rows, 2, 3, HALF).transpose(0, 2, 1, 3).reshape(rows, 3 * D)


class WholeComm:
    touch = ()

    def __init__(self, count):
        self.info = jnp.zeros((2,), jnp.int32)

    def order(self, low, high):
        return low, high

    def weights(self, call, small, bias_up, w_qkv, w_out, w_up, w_down):
        def gather(value):
            return lax.all_gather(value, "dp", axis=0, tiled=True)

        def half(matrix, h):
            width = matrix.shape[1] // 2
            return matrix[:, h * width : (h + 1) * width]

        block = jnp.pad(small.T, ((0, 0), (0, 128 - small.shape[0])))
        block = gather(block.at[0, UP_LANE : UP_LANE + bias_up.shape[1]].set(bias_up[0]))
        qkv, out, up = (gather(w) for w in (half_major(w_qkv), w_out, w_up))
        self.first = [jnp.concatenate([half(qkv, h), half(out, h), block], 1) for h in range(2)]
        self.held = {1: [half(up, h) for h in range(2)]}
        down = gather(w_down)
        self.held[2] = [half(down, h) for h in range(2)]

    def step(self, call):
        pass

    def advance(self, call):
        pass

    def gather_step(self, call, step):
        pass

    def pump(self, call, index, *touch):
        pass

    def reduce(self, value):
        return lax.psum_scatter(value, "dp", scatter_dimension=0, tiled=True)

    def far(self, array):
        return array

    def reduce_down(self, call, near, far, gated, gated_far):
        self.down = self.reduce(dot(near[D : 2 * D], jnp.concatenate([gated, gated_far], 1)))

    def reduce_up(self, call, near, far, raised, raised_far):
        self.up = self.reduce(dot(near[:D], jnp.concatenate([raised, raised_far], 1)))

    def reduce_qkv(self, call, near, far, triple, triple_far, dp, dp_far, mixed, mixed_far):
        triple = jnp.concatenate([triple, triple_far], 1)
        self.qkv = third_major(self.reduce(dot(near[2 * D :], triple)))
        mixed = jnp.concatenate([mixed, mixed_far], 1)
        self.out = self.reduce(dot(dp, mixed, 0, 0))

    def reduce_block(self, call, block):
        self.vec = self.reduce(block)

    def results(self, call):
        return self.down, self.up, self.out, self.qkv, self.vec


class GridComm:
    def __init__(self):
        index = lax.axis_index("dp")
        self.info = jnp.stack([index >> 1, index & 1]).astype(jnp.int32)
        self.is_first = (index & 1) == 0
        self.jobs = []

    def order(self, low, high):
        return pick(self.is_first, low, high), pick(self.is_first, high, low)

    def weights(self, call, small, bias_up, w_qkv, w_out, w_up, w_down):
        rows = w_qkv.shape[0]
        total = sum(width for width, _ in CHUNKS)
        total_a = sum(cut for _, cut in CHUNKS)
        parts = (w_qkv, w_out, w_up, w_down)
        mine, other = call(
            pack_body,
            [shape((rows, total))] * 2,
            [small, bias_up, *parts],
            info=self.info,
            in_hbm=(2, 3, 4, 5),
            scratch=[pltpu.VMEM((128, 128), F32)]
            + [pltpu.VMEM(w.shape, LOW) for w in parts]
            + [pltpu.SemaphoreType.DMA],
        )
        wide = CHUNKS[1][0]
        unit, self.units, unit_a, unit_b = call(
            unit_body,
            [
                shape((48, CHUNKS[0][0])), shape((2, 48, wide)),
                shape((48, total_a)), shape((48, total - total_a)),
            ],
            [mine, swap(other, 1)],
            info=self.info,
        )
        self.own = [unit_a, swap(unit_a, 4), unit_b, swap(unit_b, 2)]
        self.lines = [swap(unit, bit) for bit in (8, 16, 24)]
        self.plan = self.schedule(call)

    def advance(self, call):
        next(self.plan)

    def pair(self, call, index, far):
        (pair,) = call(
            functools.partial(pair_body, index - 1), [shape(self.units.shape)], [self.units, far]
        )
        return [far, swap(pair, 8)]

    def schedule(self, call):
        width, cut = CHUNKS[0]
        pair_a, pair_b = call(
            own_body, [shape((2, 48, cut)), shape((2, 48, width - cut))], self.own
        )
        pairs = [pair_a, swap(pair_a, 2), pair_b, swap(pair_b, 4)]
        yield
        a, b, again = call(
            functools.partial(first_stack_body, cut, 0),
            [shape((3, 48, cut)), shape((3, 48, width - cut)), shape(self.units.shape[1:])],
            [*self.lines, self.units],
            touch=(pairs[1], pairs[3]),
        )
        stacked = [a, swap(a, 4), b, swap(b, 2)]
        far_one = swap(again, 16)
        joined = self.join(call, 0, stacked)
        line_one = self.pair(call, 1, far_one)
        (own,) = self.finish(call, 0, joined, pairs)
        self.first = [own, swap(own, 1)]
        self.line = {1: line_one}
        self.held = {}
        yield

    def gather_step(self, call, step):
        index = 1 if step in "SJf" else 2
        if step == "P":
            self.line[2] = self.pair(call, 2, self.line[2])
        elif step == "S":
            width, cut = CHUNKS[1]
            a, b, again = call(
                functools.partial(first_stack_body, cut, 1),
                [shape((3, 48, cut)), shape((3, 48, width - cut)), shape(self.units.shape[1:])],
                [*self.line[1], self.units],
            )
            self.held[1] = [a, swap(a, 4), b, swap(b, 2)]
            self.line[2] = swap(again, 16)
        elif step == "s":
            self.held[2] = self.stack(call, 2, self.line[2])
        elif step in "Jj":
            self.held[index] = self.join(call, index, self.held[index])
        else:
            (own,) = self.finish(call, index, self.held[index])
            self.held[index] = [own, swap(own, 1)]

    def starts(self, index):
        return (
            sum(c for _, c in CHUNKS[:index]),
            sum(w - c for w, c in CHUNKS[:index]),
        )

    def stack(self, call, index, line, touch=()):
        width, cut = CHUNKS[index]
        a, b = call(
            functools.partial(stack_body, cut),
            [shape((3, 48, cut)), shape((3, 48, width - cut))],
            line,
            touch=touch,
        )
        return a, swap(a, 4), b, swap(b, 2)

    def join(self, call, index, stacked, touch=()):
        width, cut = CHUNKS[index]
        count = 6 if index == 0 else 8
        a, b = call(
            functools.partial(join_body, *self.starts(index)),
            [shape((count, 48, cut)), shape((count, 48, width - cut))],
            [*stacked] + ([] if index == 0 else self.own),
            touch=touch,
        )
        return a, swap(a, 2), b, swap(b, 4)

    def finish(self, call, index, joined, pairs=()):
        width, cut = CHUNKS[index]
        z = (8, 4, 12) if index else Z_CODES[1:]
        codes_a = z + tuple(c ^ 2 for c in z)
        codes_b = z + tuple(c ^ 1 for c in z)
        if index:
            codes_a, codes_b = (0, 2) + codes_a, (0, 1) + codes_b
        plan = []
        for codes_a, codes_b in [(codes_a, codes_b)] + ([((0, 2), (0, 1))] if pairs else []):
            plan += [
                (codes_a, 0, 0, cut),
                (tuple(c ^ 1 for c in codes_a), 0, 0, cut),
                (codes_b, 0, cut, width - cut),
                (tuple(c ^ 2 for c in codes_b), 0, cut, width - cut),
            ]
        return call(
            functools.partial(place_body, plan),
            [shape((D, width))],
            [*joined, *pairs],
            info=self.info,
            scratch=[pltpu.SemaphoreType.DMA],
        )

    def pieces(self, width_a, width_b):
        return [shape((8, 48, w)) for w in (width_a, width_a, width_b, width_b)]

    def job(self, call, name, parts, body, outs, direct):
        send_a, keep_a, send_b, keep_b = parts
        width_a, width_b = keep_a.shape[2], keep_b.shape[2]
        width = width_a + width_b
        far_a, far_b = swap(send_a, 2), swap(send_b, 4)
        yield
        send_a, keep_a, send_b, keep_b = call(
            first_sum_body,
            [shape((4, 48, w)) for w in (width_a, width_a, width_b, width_b)],
            [far_a, keep_a, far_b, keep_b],
            touch=self.touch,
        )
        far_a, far_b = swap(send_a, 4), swap(send_b, 2)
        yield
        if direct:
            width += 128
            own, *lines = call(
                second_sum_block_body,
                [shape((48, width))] * 4,
                [far_a, keep_a, far_b, keep_b, *self.block],
            )
            lines = [swap(line, bit) for line, bit in zip(lines, (8, 16, 24))]
            yield
            last_body, lines = last_sum_body, [own, *lines]
        else:
            own, send = call(
                second_sum_body, [shape((2, 48, width))] * 2, [far_a, keep_a, far_b, keep_b]
            )
            far = swap(send, 8)
            yield
            own, send = call(near_sum_body, [shape((48, width))] * 2, [own, far])
            far = swap(send, 16)
            yield
            last_body, lines = last_near_body, [own, far]
        mine, other = call(
            last_body,
            [shape((24, width), F32)] * 2,
            lines,
            info=self.info,
            scratch=[pltpu.VMEM((48, width), F32)],
        )
        other = swap(other, 1)
        yield
        self.outs[name] = call(body, outs, [mine, other], info=self.info, last=True)

    def begin(self, job):
        next(job)
        self.jobs.append(job)

    def pump(self, call, index, *touch):
        self.touch = touch
        return next(self.jobs[index], self) is not self

    def block_job(self, call, block):
        send, keep = call(
            block_body, [shape((8, 48, 128), F32)] * 2, [block], info=self.info
        )
        far = swap(send, 2)
        yield
        send, keep = call(block_sum_body, [shape((4, 48, 128), F32)] * 2, [far, keep])
        self.block = [swap(send, 4), keep]
        yield

    def results(self, call):
        (down,), (up,), (qkv, out, vec) = [self.outs[k] for k in ("down", "up", "qkv")]
        return down, up, out, qkv, vec

    def far(self, array):
        return swap(array, 1)

    def reduce_down(self, call, *args):
        self.outs = {}
        parts = call(
            functools.partial(grad_body, 1),
            self.pieces(768, 768),
            args,
            info=self.info,
            scratch=[pltpu.VMEM((D, STEP), LOW)],
            us=6,
        )
        self.begin(self.job(call, "down", parts, merge_one_body, [shape((24, FF), F32)], False))

    def reduce_up(self, call, *args):
        parts = call(
            functools.partial(grad_body, 0),
            self.pieces(768, 768),
            args,
            info=self.info,
            scratch=[pltpu.VMEM((D, STEP), LOW)],
            us=6,
        )
        self.begin(self.job(call, "up", parts, merge_one_body, [shape((24, FF), F32)], False))

    def reduce_qkv(self, call, *args):
        parts = call(
            qkv_grad_body,
            self.pieces(768, 768),
            args,
            info=self.info,
            scratch=[pltpu.VMEM((D, STEP), LOW)],
            us=6,
        )
        outs = [shape((24, 3 * D), F32), shape((24, D), F32), shape((24, 128), F32)]
        self.begin(self.job(call, "qkv", parts, merge_qkv_body, outs, True))

    def reduce_block(self, call, block):
        self.begin(self.block_job(call, block))


def shards(count, tokens, lengths, source, cotangent, w_qkv, w_out, w_up, w_down, *small):
    (
        gain_one, shift_one, bias_query, bias_value, bias_out, gain_two, shift_two,
        bias_up, bias_down,
    ) = small
    seqs, slots = tokens.shape[:2]
    rows = seqs * slots
    share = gain_one.shape[0]
    comm = GridComm() if count == 32 else WholeComm(count)
    visible = jnp.where(source == 1, lengths, IMG_LEN)
    tokens = tokens.reshape(rows, D)
    cotangent = cotangent.reshape(rows, D)
    small = jnp.stack(
        [gain_one, shift_one, gain_two, shift_two, bias_out, bias_down, bias_query, bias_value]
    )
    bias_up = bias_up[None]
    call = Chain([tokens, cotangent, small, bias_up])

    act = shape((rows, D))
    act_f = shape((rows, D), F32)
    half = shape((rows, HALF))
    triple = shape((rows, 3 * HALF))
    wide = shape((rows, WIDE))

    def attend(part, *touch):
        return call(
            functools.partial(attend_body, slots),
            [half, shape((8, 2 * slots), F32)],
            [part],
            info=visible,
            us=4.3,
            touch=touch,
        )

    comm.weights(call, small, bias_up, w_qkv, w_out.T, w_up, w_down.T)
    comm.advance(call)
    dy, dy_sum = call(
        functools.partial(start_body, slots),
        [act, shape((8, D), F32)],
        [cotangent],
        info=visible,
    )
    comm.advance(call)
    for step in EARLY:
        if step == "k":
            normed_one, qkv_own, vecs = call(
                qkv_body,
                [act, triple, shape((16, D), F32)],
                [tokens, comm.first[0]],
                info=comm.info,
                us=4.3,
            )
        elif step == "l":
            o_own, logs_own = attend(qkv_own)
        elif step == "m":
            qkv_par, bias_up = call(
                functools.partial(qkv_far_body, share),
                [triple, shape((1, FF), F32)],
                [normed_one, comm.first[0], comm.first[1], vecs],
                info=comm.info,
                us=2.5,
            )
        elif step == "n":
            o_par, logs_par = attend(qkv_par)
            o_far = comm.far(o_par)
        elif step == "h":
            hidden, normed_two, standard, scales = call(
                hidden_body,
                [act_f, act, act_f, shape((rows, 128), F32)],
                [tokens, vecs, o_own, o_par, *comm.first],
                us=4,
            )
        elif step == "t":
            (near,) = call(
                turn_body, [shape((3 * D, rows))], [normed_two, dy, normed_one], touch=(o_far,), us=3
            )
            far = comm.far(near)
        elif step in "gG":
            flip = 0 if step == "g" else 1
            values = call(
                functools.partial(raise_body, flip),
                [wide] * 2,
                [normed_two, bias_up, comm.held[1][flip]],
                info=comm.info,
                us=3.7,
            )
            if step == "g":
                gated, slope = values
            else:
                gated_par, slope_par = values
                gated_far = comm.far(gated_par)
        elif step == "d":
            comm.reduce_down(call, near, far, gated, gated_far)
        else:
            comm.gather_step(call, step)
    second = comm.held[1]
    third = comm.held[2]
    raised, raised_par, up_sum = call(
        raise_back_body,
        [wide, wide, shape((1, FF), F32)],
        [dy, slope, slope_par, *third],
        info=comm.info,
        us=4.8,
    )
    raised_far = comm.far(raised_par)
    grad_hidden, branch, sums_two = call(
        hidden_back_body,
        [act_f, act, shape((8, D), F32)],
        [dy, standard, scales, vecs, raised, raised_par, *second],
        scratch=[pltpu.VMEM((rows, D), F32)],
        us=6.6,
    )
    branch_far = comm.far(branch)

    def attend_back(part, logs, weight, *touch):
        return call(
            functools.partial(attend_back_body, slots),
            [triple, shape((8, HALF), F32)],
            [part, logs, branch, weight],
            info=visible,
            scratch=[pltpu.VMEM((rows, HALF), LOW)],
            touch=touch,
            us=8.2,
        )

    sums = [branch_far]
    for step in ORDER:
        if step == "p":
            triple_par, sums_par = attend_back(qkv_par, logs_par, comm.first[1])
            triple_far = comm.far(triple_par)
        elif step == "o":
            triple_own, sums_own = attend_back(qkv_own, logs_own, comm.first[0])
        elif step == "u":
            comm.reduce_up(call, near, far, raised, raised_far)
        elif step == "q":
            comm.reduce_qkv(
                call, near, far, triple_own, triple_far, branch, branch_far, o_own, o_far
            )
        elif step == "t":
            grad_tokens, block = call(
                functools.partial(token_back_body, share),
                [act, shape((D, 128), F32)],
                [
                    tokens, grad_hidden, vecs, sums_two, dy_sum, up_sum, sums_own, sums_par,
                    triple_own, triple_par, *comm.first,
                ],
                info=comm.info,
                scratch=[pltpu.VMEM((rows, D), F32), pltpu.VMEM((128, D), F32)],
                us=6.5,
            )
        elif step == "b":
            comm.reduce_block(call, block)
        elif step == "m":
            (output,) = call(
                mix_body, [act], [hidden, vecs, gated, gated_par, *third], us=4.1, last=True
            )
        else:
            comm.pump(call, int(step), *sums)
            sums = []
    g_down_t, g_up, g_out_t, g_qkv, g_vec = comm.results(call)
    (
        g_gain_one, g_shift_one, g_gain_two, g_shift_two, g_bias_out, g_bias_down, g_query, g_value,
    ) = [g_vec[:, i] for i in range(8)]
    return (
        output.reshape(seqs, slots, D),
        grad_tokens.reshape(seqs, slots, D),
        g_qkv,
        g_out_t.T,
        g_up,
        g_down_t.T,
        g_gain_one, g_shift_one, g_query, g_value, g_bias_out, g_gain_two, g_shift_two,
        g_vec[0, UP_LANE : UP_LANE + 4 * share],
        g_bias_down,
    )


def solution(mesh):
    row, tall, wide, vec = P("dp", None, None), P("dp", None), P(None, "dp"), P("dp")
    in_specs = (row, vec, vec, row, tall, wide, tall, wide) + (vec,) * 9
    out_specs = (row, row, tall, wide, tall, wide) + (vec,) * 9
    body = functools.partial(shards, mesh.shape["dp"])
    return jax.shard_map(
        body, mesh=mesh, in_specs=in_specs, out_specs=out_specs, check_vma=False
    )
```

```python
import functools
import jax
import jax.numpy as jnp
import numpy as np
from jax import lax
from jax.experimental import pallas as pl
from jax.experimental.pallas import tpu as pltpu
from jax.sharding import PartitionSpec as P

HEADS = 12
HEAD_DIM = 64
IMG_LEN = 196
ALWAYS = 152
EPS = 1e-06
D = 768
FF = 3072
HALF = D // 2
WIDE = FF // 2
LOW = jnp.bfloat16
F32 = jnp.float32
STEP = 768
PART = 512
ROWS = 160
MARGIN = 10
PACE = 4
UP_LANE = 32
SCALE = HEAD_DIM ** (-0.5)
CHUNKS = ((4 * HALF + 128, 896), (WIDE, 768), (WIDE, 768))
Z_CODES = (0, 4, 8, 12)
SMEM = pl.BlockSpec(memory_space=pltpu.SMEM)
ANY = pl.BlockSpec(memory_space=pl.ANY)
VMEM = pl.BlockSpec(memory_space=pltpu.VMEM)


def shape(dims, kind=LOW):
    return jax.ShapeDtypeStruct(dims, kind)


class Chain:
    def __init__(self, loose):
        self.last = None
        self.loose = loose
        self.count = 0

    def near(self, array):
        if any(array is a for a in self.loose):
            return array
        return pltpu.with_memory_space_constraint(array, pltpu.VMEM)

    def __call__(
        self, body, outs, ins, *, info=None, touch=(), in_hbm=(), scratch=(), us=8, last=False
    ):
        us *= PACE
        if self.count < len(COSTS):
            us *= COSTS[self.count]
        self.count += 1
        head = [] if info is None else [info]
        ins = list(ins)
        count = len(head) + len(ins)
        specs = [SMEM] * len(head) + [ANY if i in in_hbm else VMEM for i in range(len(ins))]
        given = [
            pltpu.with_memory_space_constraint(a, pltpu.HBM) if i in in_hbm else self.near(a)
            for i, a in enumerate(ins)
        ]
        extra = list(touch) + ([] if self.last is None else [self.last])
        total = count + len(extra)

        def run(*refs):
            body(*refs[:count], *refs[total:])

        held = sum(
            int(np.prod(k.shape)) * jnp.dtype(k.dtype).itemsize
            for k in scratch
            if getattr(k, "shape", ())
        )
        size = sum(a.size * a.dtype.itemsize for a in [*ins, *outs])
        results = pl.pallas_call(
            run,
            out_shape=tuple(outs if last else [pltpu.VMEM(o.shape, o.dtype) for o in outs]),
            in_specs=specs + [ANY] * len(extra),
            out_specs=(VMEM,) * len(outs),
            scratch_shapes=list(scratch),
            compiler_params=pltpu.CompilerParams(vmem_limit_bytes=held + MARGIN * 2**20),
            cost_estimate=pl.CostEstimate(
                flops=int(us * 1.1e9), bytes_accessed=size, transcendentals=0
            ),
        )(*head, *given, *extra)
        self.last = min(results, key=lambda r: r.size * r.dtype.itemsize)
        return results


def dot(left, right, left_dim=1, right_dim=0):
    return lax.dot_general(
        left, right, (((left_dim,), (right_dim,)), ((), ())), preferred_element_type=F32
    )


def joined(own, par, axis=1):
    return jnp.concatenate([own[...], par[...]], axis)


def standardize(values):
    center = values - jnp.mean(values, -1, keepdims=True)
    scale = lax.rsqrt(jnp.mean(center * center, -1, keepdims=True) + EPS)
    return center * scale, scale


def row_loop(rows, body, init=0):
    def step(i, carry):
        return body(pl.ds(pl.multiple_of(i * ROWS, ROWS), ROWS), carry)

    return lax.fori_loop(0, rows // ROWS, step, init)


def swap(value, bit):
    pairs = [(i, i ^ bit) for i in range(32)]
    return lax.ppermute(value, "dp", pairs)


def pack_body(info, small, bias_up, *refs):
    weights, (mine, other), (rows, *held, sem) = refs[:4], refs[4:6], refs[6:]
    copies = [pltpu.make_async_copy(w, v, sem) for w, v in zip(weights, held)]
    for copy in copies:
        copy.start()
    w_qkv, w_out, w_up, w_down = held
    rows[...] = jnp.zeros_like(rows)
    share = w_qkv.shape[0]
    rows[: small.shape[0], :share] = small[...].astype(F32)
    rows[...] = rows[...].T
    rows[0:1, UP_LANE : UP_LANE + 4 * share] = bias_up[...].astype(F32)
    block = rows[:share, :].astype(LOW)
    for copy in copies:
        copy.wait()
    for flip, out in enumerate((mine, other)):
        h = info[1] ^ flip

        def half(weight, width, start=0):
            return weight[:, pl.ds(pl.multiple_of(start + h * width, 128), width)]

        for i in range(3):
            out[:, i * HALF : (i + 1) * HALF] = half(w_qkv, HALF, i * D)
        out[:, 3 * HALF : 4 * HALF] = half(w_out, HALF)
        at = CHUNKS[0][0]
        out[:, 4 * HALF : at] = block
        out[:, at : at + WIDE] = half(w_up, WIDE)
        out[:, at + WIDE :] = half(w_down, WIDE)


def unit_body(info, mine, other, unit_one, units, unit_a, unit_b):
    a, b = mine[...].astype(F32), other[...].astype(F32)
    unit = jnp.where(
        info[1] == 0, jnp.concatenate([a, b], 0), jnp.concatenate([b, a], 0)
    ).astype(LOW)
    start = at_a = at_b = 0
    for i, (width, cut) in enumerate(CHUNKS):
        part = unit[:, start : start + width]
        if i == 0:
            unit_one[...] = part
        else:
            units[i - 1] = part
        unit_a[:, at_a : at_a + cut] = part[:, :cut]
        unit_b[:, at_b : at_b + width - cut] = part[:, cut:]
        start, at_a, at_b = start + width, at_a + cut, at_b + width - cut


def own_body(unit_a, far_a, unit_b, far_b, pair_a, pair_b):
    for pair, unit, far in ((pair_a, unit_a, far_a), (pair_b, unit_b, far_b)):
        width = pair.shape[2]
        pair[0] = unit[:, :width]
        pair[1] = far[:, :width]


def pair_body(index, units, far, pair):
    pair[0] = units[index]
    pair[1] = far[...]


def stack_body(cut, *refs):
    pieces, (stack_a, stack_b) = refs[:-2], refs[-2:]
    at = 0
    for piece in pieces:
        for i in range(piece.shape[0] if len(piece.shape) == 3 else 1):
            part = piece.at[i] if len(piece.shape) == 3 else piece
            stack_a[at] = part[:, :cut]
            stack_b[at] = part[:, cut:]
            at += 1


def first_stack_body(cut, index, *refs):
    *pieces, units, stack_a, stack_b, again = refs
    stack_body(cut, *pieces, stack_a, stack_b)
    again[...] = units[index]


def join_body(start_a, start_b, *refs):
    stacks, own, (join_a, join_b) = refs[:4], refs[4:-2], refs[-2:]
    for side, join, start in ((0, join_a, start_a), (1, join_b, start_b)):
        width = join.shape[2]
        parts = own[2 * side : 2 * side + 2]
        for i, part in enumerate(parts):
            join[i] = part[:, start : start + width]
        at = len(parts)
        join[at : at + 3] = stacks[2 * side][...]
        join[at + 3 : at + 6] = stacks[2 * side + 1][...]


def place_body(plan, info, *refs):
    pieces, out, sem = refs[:-2], refs[-2], refs[-1]
    copies = []
    for piece, (codes, source, target, width) in zip(pieces, plan):
        for i, code in enumerate(codes):
            row = pl.multiple_of((info[0] ^ code) * 48, 48)
            copies.append(
                pltpu.make_async_copy(
                    piece.at[i, :, pl.ds(source, width)],
                    out.at[pl.ds(row, 48), pl.ds(target, width)],
                    sem,
                )
            )
    for copy in copies:
        copy.start()
    for copy in copies:
        copy.wait()


ORDER = "up0o1q0tm1b02310210122"
EARLY = "SkJPlmsnhftjgGFd"
COSTS = ()
KEEP_A = tuple(c ^ y for y in (0, 2) for c in Z_CODES)
KEEP_B = tuple(c ^ x for x in (0, 1) for c in Z_CODES)
SEND_A = tuple(c ^ 1 for c in KEEP_A)
SEND_B = tuple(c ^ 2 for c in KEEP_B)


def spread(chip, grad, send, keep, send_codes, keep_codes):
    for out, codes in ((send, send_codes), (keep, keep_codes)):
        for i, code in enumerate(codes):
            row = pl.multiple_of((chip ^ code) * 48, 48)
            out[i] = grad[pl.ds(row, 48), :].astype(out.dtype)


def add(left, right):
    return (left.astype(F32) + right.astype(F32)).astype(LOW)


def first_sum_body(far_a, keep_a, far_b, keep_b, send_a, own_a, send_b, own_b):
    for far, keep, send, own in ((far_a, keep_a, send_a, own_a), (far_b, keep_b, send_b, own_b)):
        for i in range(4):
            send[i] = add(far[4 + i], keep[4 + i])
            own[i] = add(far[i], keep[i])


def second_sum_body(far_a, keep_a, far_b, keep_b, *outs):
    cut = keep_a.shape[2]
    for i in range(4):
        out = outs[i] if len(outs) == 4 else outs[i % 2].at[i // 2]
        out[:, :cut] = add(far_a[i], keep_a[i])
        out[:, cut:] = add(far_b[i], keep_b[i])


def last_sum_body(info, own, z_one, z_two, z_three, mine, other, total):
    value = own[...].astype(F32)
    for piece in (z_one, z_two, z_three):
        value = value + piece[...].astype(F32)
    total[...] = value
    split_rows(info, total, mine, other)


def split_rows(info, total, mine, other):
    rows = mine.shape[0]
    mine[...] = total[pl.ds(pl.multiple_of(info[1] * rows, 8), rows), :]
    other[...] = total[pl.ds(pl.multiple_of((1 - info[1]) * rows, 8), rows), :]


def merge(info, mine, other, start, width, out, count=1):
    for flip, part in enumerate((mine, other)):
        h = info[1] ^ flip
        for i in range(count):
            at = pl.multiple_of((2 * i + h) * width, 128)
            out[:, pl.ds(at, width)] = part[:, start + i * width : start + (i + 1) * width]


def merge_one_body(info, mine, other, out):
    merge(info, mine, other, 0, WIDE, out)


def merge_qkv_body(info, mine, other, out_qkv, out_out, vec):
    merge(info, mine, other, 0, HALF, out_qkv, 3)
    merge(info, mine, other, 3 * HALF, HALF, out_out)
    vec[...] = mine[:, 4 * HALF :] + other[:, 4 * HALF :]


def near_sum_body(own, far, keep, send):
    keep[...] = add(own[0], far[0])
    send[...] = add(own[1], far[1])


def last_near_body(info, keep, far, mine, other, total):
    total[...] = keep[...].astype(F32) + far[...].astype(F32)
    split_rows(info, total, mine, other)


def block_body(info, block, send, keep):
    spread(info[0], block, send, keep, SEND_A, KEEP_A)


def block_sum_body(far, keep, send, own):
    count = keep.shape[0] // 2
    own[...] = far[:count] + keep[:count]
    send[...] = far[count:] + keep[count:]


def second_sum_block_body(far_a, keep_a, far_b, keep_b, far_v, keep_v, *outs):
    width = keep_a.shape[2] + keep_b.shape[2]
    second_sum_body(far_a, keep_a, far_b, keep_b, *(o.at[:, :width] for o in outs))
    for i, out in enumerate(outs):
        out[:, width:] = (far_v[i] + keep_v[i]).astype(LOW)


def start_body(slots, visible, cot, dy, total):
    rows = cot.shape[0]
    total[...] = jnp.zeros_like(total)
    for s in range(rows // slots):
        live = lax.broadcasted_iota(jnp.int32, (slots, 1), 0) < visible[s]
        part = jnp.where(live, cot[s * slots : (s + 1) * slots, :].astype(F32), 0.0)
        dy[s * slots : (s + 1) * slots, :] = part.astype(LOW)
        total[0:1, :] += jnp.sum(part, 0, keepdims=True)


def qkv_body(info, tokens, own, normed, qkv, vecs):
    vecs[...] = own[:, 4 * HALF :].astype(F32).T[:16, :]

    def norm(at, carry):
        z, _ = standardize(tokens[at, :].astype(F32))
        normed[at, :] = (z * vecs[0:1, :] + vecs[1:2, :]).astype(LOW)
        return carry

    row_loop(tokens.shape[0], norm)
    project_qkv(info, 0, normed, own, vecs, qkv)


def project_qkv(info, flip, normed, weight, vecs, out):
    half = half_of(info, flip, HALF)
    bias = [vecs[6:7, half], jnp.zeros((1, HALF), F32), vecs[7:8, half]]
    value = dot(normed[...], weight[:, : 3 * HALF]) + jnp.concatenate(bias, 1)
    out[...] = value.astype(LOW)


def qkv_far_body(share, info, normed, own, weight, vecs, qkv, bias_up):
    project_qkv(info, 1, normed, weight, vecs, qkv)
    for d in range(D // share):
        row = own[d * share // 16 * 16 : d * share // 16 * 16 + 16, 4 * HALF :].astype(F32)
        at = d * share % 16
        bias_up[0:1, 4 * share * d : 4 * share * (d + 1)] = row[
            at : at + 1, UP_LANE : UP_LANE + 4 * share
        ]


def by_head(block):
    lane = lax.broadcasted_iota(jnp.int32, (1, 128), 1)
    return jnp.concatenate(
        [jnp.where(lane < HEAD_DIM, block, 0), jnp.where(lane >= HEAD_DIM, block, 0)], 0
    )


def scores_of(key, query, live):
    scores = dot(key, query, 1, 1)
    return jnp.concatenate(
        [scores[:ALWAYS], jnp.where(live[ALWAYS:], scores[ALWAYS:], -1e30)], 0
    )


def from_columns(values, slots):
    return jnp.concatenate(
        [values[:HEAD_DIM, :slots], values[HEAD_DIM:, slots:]], 0
    ).T


def blocks_of(slots, rows):
    for s in range(rows // slots):
        for j in range(HALF // 128):
            yield s, j, slice(s * slots, (s + 1) * slots)


def attend_body(slots, visible, qkv, out, logs):
    slot = lax.broadcasted_iota(jnp.int32, (slots, 1), 0)
    for s, j, at in blocks_of(slots, qkv.shape[0]):
        query, key, value = (
            qkv[at, i * HALF + j * 128 : i * HALF + (j + 1) * 128] for i in range(3)
        )
        scores = scores_of(key, by_head(query * SCALE), slot < visible[s])
        top = jnp.max(scores, 0, keepdims=True)
        power = jnp.exp(scores - top)
        total = jnp.sum(power, 0, keepdims=True)
        row = s * (HALF // 128) + j
        logs[row : row + 1, :] = top + jnp.log(total)
        mixed = dot(value.T, (power * (1.0 / total)).astype(LOW))
        out[at, j * 128 : (j + 1) * 128] = from_columns(mixed, slots).astype(LOW)


def hidden_body(tokens, vecs, o_own, o_par, own, par, hidden, normed, standard, scales):
    out_cols = slice(3 * HALF, 4 * HALF)
    hidden[...] = dot(joined(o_own, o_par), joined(own.at[:, out_cols], par.at[:, out_cols]), 1, 1)

    def norm(at, carry):
        value = tokens[at, :].astype(F32) + (hidden[at, :] + vecs[4:5, :])
        hidden[at, :] = value
        z, scale = standardize(value)
        standard[at, :] = z
        scales[at, :] = jnp.broadcast_to(scale, (ROWS, 128))
        normed[at, :] = (z * vecs[2:3, :] + vecs[3:4, :]).astype(LOW)
        return carry

    row_loop(tokens.shape[0], norm)


def turn_body(normed_two, dy, normed_one, out):
    for i, array in enumerate((normed_two, dy, normed_one)):
        out[i * D : (i + 1) * D, :] = array[...].T


GELU_A = 0.7978845608028654
GELU_B = 0.044715


def raise_body(flip, info, normed, bias, weight, gate, slope):
    for i in range(WIDE // PART):
        at = slice(i * PART, (i + 1) * PART)
        start = pl.multiple_of((info[1] ^ flip) * WIDE + i * PART, 128)
        u = dot(normed[...], weight[:, at]) + bias[:, pl.ds(start, PART)]
        square = u * u
        t = jnp.tanh(u * (GELU_A + (GELU_A * GELU_B) * square))
        lift = 0.5 + 0.5 * t
        gated = u * lift
        curve = GELU_A + (3.0 * GELU_A * GELU_B) * square
        slope[:, at] = (lift + (gated * (1.0 - t)) * curve).astype(LOW)
        gate[:, at] = gated.astype(LOW)


def half_of(info, flip, width):
    return pl.ds(pl.multiple_of((info[1] ^ flip) * width, 128), width)


def mix_body(hidden, vecs, a_own, a_par, own, par, out):
    value = dot(joined(a_own, a_par), joined(own, par), 1, 1)
    out[...] = (hidden[...] + (value + vecs[5:6, :])).astype(LOW)


def raise_back_body(info, dy, s_own, s_par, own, par, d_own, d_par, total):
    for i in range(WIDE // PART):
        at = slice(i * PART, (i + 1) * PART)
        for h, (slope, weight, out) in enumerate(((s_own, own, d_own), (s_par, par, d_par))):
            value = (dot(dy[...], weight[:, at]) * slope[:, at].astype(F32)).astype(LOW)
            start = pl.multiple_of((info[1] ^ h) * WIDE + i * PART, 128)
            total[:, pl.ds(start, PART)] = jnp.sum(value.astype(F32), 0, keepdims=True)
            out[:, at] = value


def norm_back(part, z, scale, gain):
    pz = part * z
    mean_e = jnp.mean(part * gain, -1, keepdims=True)
    mean_ez = jnp.mean(pz * gain, -1, keepdims=True)
    return scale * ((part * gain - mean_e) - z * mean_ez), pz


def fold(values):
    return jnp.sum(values.reshape(ROWS // 8, 8, D), 0)


def hidden_back_body(dy, standard, scales, vecs, d_own, d_par, own, par, dh, dp, sums, acc):
    acc[...] = dot(joined(d_own, d_par), joined(own, par), 1, 1)

    def back(at, carry):
        part = acc[at, :]
        value, pz = norm_back(part, standard[at, :], scales[at, 0:1], vecs[2:3, :])
        value = dy[at, :].astype(F32) + value
        dh[at, :] = value
        low = value.astype(LOW)
        dp[at, :] = low
        gain, shift, bias = carry
        return gain + fold(pz), shift + fold(part), bias + fold(low.astype(F32))

    zero = jnp.zeros((8, D), F32)
    totals = row_loop(acc.shape[0], back, (zero, zero, zero))
    for r in range(3):
        sums[r : r + 1, :] = jnp.sum(totals[r], 0, keepdims=True)


def attend_back_body(slots, visible, qkv, logs, dp, out_weight, dqkv, sums, mixed):
    mixed[...] = dot(dp[...], out_weight[:, 3 * HALF : 4 * HALF]).astype(LOW)
    slot = lax.broadcasted_iota(jnp.int32, (slots, 1), 0)
    sums[...] = jnp.zeros_like(sums)
    for s, j, at in blocks_of(slots, qkv.shape[0]):
        cols = [slice(i * HALF + j * 128, i * HALF + (j + 1) * 128) for i in range(3)]
        query, key, value = (qkv[at, c] for c in cols)
        query = by_head(query * SCALE)
        grad = by_head(mixed[at, j * 128 : (j + 1) * 128])
        row = s * (HALF // 128) + j
        soft = jnp.exp(scores_of(key, query, slot < visible[s]) - logs[row : row + 1, :])
        grad_soft = dot(value, grad, 1, 1)
        inner = jnp.sum(soft * grad_soft, 0, keepdims=True)
        grad_scores = (soft * (grad_soft - inner)).astype(LOW)
        grads = (
            from_columns(dot(key.T, grad_scores), slots) * SCALE,
            dot(grad_scores, query),
            dot(soft.astype(LOW), grad),
        )
        for i, value in enumerate(grads):
            low = value.astype(LOW)
            dqkv[at, cols[i]] = low
            if i != 1:
                sums[i : i + 1, j * 128 : (j + 1) * 128] += jnp.sum(
                    low.astype(F32), 0, keepdims=True
                )


def token_back_body(
    share, info, tokens, dh, vecs, sums_two, dy_sum, up_sum, sums_own, sums_par, d_own, d_par, own, par,
    out, block, acc, sums,
):
    cols = slice(0, 3 * HALF)
    acc[...] = dot(joined(d_own, d_par), joined(own.at[:, cols], par.at[:, cols]), 1, 1)

    def back(at, carry):
        part = acc[at, :]
        z, scale = standardize(tokens[at, :].astype(F32))
        value, pz = norm_back(part, z, scale, vecs[0:1, :])
        out[at, :] = (dh[at, :] + value).astype(LOW)
        gain, shift = carry
        return gain + fold(pz), shift + fold(part)

    zero = jnp.zeros((8, D), F32)
    totals = row_loop(acc.shape[0], back, (zero, zero))
    sums[...] = jnp.zeros_like(sums)
    for r in range(2):
        sums[r : r + 1, :] = jnp.sum(totals[r], 0, keepdims=True)
    sums[2:5, :] = sums_two[0:3, :]
    sums[5:6, :] = dy_sum[0:1, :]
    for flip, part in enumerate((sums_own, sums_par)):
        half = half_of(info, flip, HALF)
        sums[6:7, half] = part[0:1, :]
        sums[7:8, half] = part[2:3, :]
    block[...] = sums[...].T
    for d in range(D // share):
        part = up_sum[0:1, 4 * share * d : 4 * share * (d + 1)]
        block[share * d : share * d + 1, UP_LANE : UP_LANE + 4 * share] = part


def outer(left, left_far, right, right_far):
    return dot(joined(left, left_far), joined(right, right_far, 0))


def pair_grads(info, blocks, sends, grad):
    send_a, keep_a, send_b, keep_b = sends
    width = keep_a.shape[2]
    at = 0
    for block in blocks:
        value = block().astype(LOW)
        count = value.shape[1]
        grad[:, :count] = value
        split = min(max(width - at, 0), count)
        if split:
            cols = slice(at, at + split)
            part = grad.at[:, :split]
            spread(info[0], part, send_a.at[:, :, cols], keep_a.at[:, :, cols], SEND_A, KEEP_A)
        if split < count:
            cols = slice(at + split - width, at + count - width)
            part = grad.at[:, split:count]
            spread(info[0], part, send_b.at[:, :, cols], keep_b.at[:, :, cols], SEND_B, KEEP_B)
        at += count


def steps_of(left, left_far, right, right_far):
    for at in range(0, right.shape[1], STEP):
        at = slice(at, min(at + STEP, right.shape[1]))
        yield functools.partial(outer, left, left_far, right.at[:, at], right_far.at[:, at])


def grad_body(index, info, near, far, right, right_far, *rest):
    left = [b.at[index * D : (index + 1) * D, :] for b in (near, far)]
    pair_grads(info, steps_of(*left, right, right_far), rest[:4], rest[4])


def qkv_grad_body(info, near, far, dqkv, dqkv_far, dp, dp_far, mixed, mixed_far, *rest):
    def out():
        return dot(joined(dp, dp_far, 0), joined(mixed, mixed_far, 0), 0, 0)

    left = [b.at[2 * D : 3 * D, :] for b in (near, far)]
    pair_grads(info, [*steps_of(*left, dqkv, dqkv_far), out], rest[:4], rest[4])


def pick(flag, left, right):
    return jnp.where(flag, left, right)


def half_major(matrix):
    rows = matrix.shape[0]
    return matrix.reshape(rows, 3, 2, HALF).transpose(0, 2, 1, 3).reshape(rows, 3 * D)


def third_major(matrix):
    rows = matrix.shape[0]
    return matrix.reshape(rows, 2, 3, HALF).transpose(0, 2, 1, 3).reshape(rows, 3 * D)


class WholeComm:
    touch = ()

    def __init__(self, count):
        self.info = jnp.zeros((2,), jnp.int32)

    def order(self, low, high):
        return low, high

    def weights(self, call, small, bias_up, w_qkv, w_out, w_up, w_down):
        def gather(value):
            return lax.all_gather(value, "dp", axis=0, tiled=True)

        def half(matrix, h):
            width = matrix.shape[1] // 2
            return matrix[:, h * width : (h + 1) * width]

        block = jnp.pad(small.T, ((0, 0), (0, 128 - small.shape[0])))
        block = gather(block.at[0, UP_LANE : UP_LANE + bias_up.shape[1]].set(bias_up[0]))
        qkv, out, up = (gather(w) for w in (half_major(w_qkv), w_out, w_up))
        self.first = [jnp.concatenate([half(qkv, h), half(out, h), block], 1) for h in range(2)]
        self.held = {1: [half(up, h) for h in range(2)]}
        down = gather(w_down)
        self.held[2] = [half(down, h) for h in range(2)]

    def step(self, call):
        pass

    def advance(self, call):
        pass

    def gather_step(self, call, step):
        pass

    def pump(self, call, index, *touch):
        pass

    def reduce(self, value):
        return lax.psum_scatter(value, "dp", scatter_dimension=0, tiled=True)

    def far(self, array):
        return array

    def reduce_down(self, call, near, far, gated, gated_far):
        self.down = self.reduce(dot(near[D : 2 * D], jnp.concatenate([gated, gated_far], 1)))

    def reduce_up(self, call, near, far, raised, raised_far):
        self.up = self.reduce(dot(near[:D], jnp.concatenate([raised, raised_far], 1)))

    def reduce_qkv(self, call, near, far, triple, triple_far, dp, dp_far, mixed, mixed_far):
        triple = jnp.concatenate([triple, triple_far], 1)
        self.qkv = third_major(self.reduce(dot(near[2 * D :], triple)))
        mixed = jnp.concatenate([mixed, mixed_far], 1)
        self.out = self.reduce(dot(dp, mixed, 0, 0))

    def reduce_block(self, call, block):
        self.vec = self.reduce(block)

    def results(self, call):
        return self.down, self.up, self.out, self.qkv, self.vec


class GridComm:
    def __init__(self):
        index = lax.axis_index("dp")
        self.info = jnp.stack([index >> 1, index & 1]).astype(jnp.int32)
        self.is_first = (index & 1) == 0
        self.jobs = []

    def order(self, low, high):
        return pick(self.is_first, low, high), pick(self.is_first, high, low)

    def weights(self, call, small, bias_up, w_qkv, w_out, w_up, w_down):
        rows = w_qkv.shape[0]
        total = sum(width for width, _ in CHUNKS)
        total_a = sum(cut for _, cut in CHUNKS)
        parts = (w_qkv, w_out, w_up, w_down)
        mine, other = call(
            pack_body,
            [shape((rows, total))] * 2,
            [small, bias_up, *parts],
            info=self.info,
            in_hbm=(2, 3, 4, 5),
            scratch=[pltpu.VMEM((128, 128), F32)]
            + [pltpu.VMEM(w.shape, LOW) for w in parts]
            + [pltpu.SemaphoreType.DMA],
        )
        wide = CHUNKS[1][0]
        unit, self.units, unit_a, unit_b = call(
            unit_body,
            [
                shape((48, CHUNKS[0][0])), shape((2, 48, wide)),
                shape((48, total_a)), shape((48, total - total_a)),
            ],
            [mine, swap(other, 1)],
            info=self.info,
        )
        self.own = [unit_a, swap(unit_a, 4), unit_b, swap(unit_b, 2)]
        self.lines = [swap(unit, bit) for bit in (8, 16, 24)]
        self.plan = self.schedule(call)

    def advance(self, call):
        next(self.plan)

    def pair(self, call, index, far):
        (pair,) = call(
            functools.partial(pair_body, index - 1), [shape(self.units.shape)], [self.units, far]
        )
        return [far, swap(pair, 8)]

    def schedule(self, call):
        width, cut = CHUNKS[0]
        pair_a, pair_b = call(
            own_body, [shape((2, 48, cut)), shape((2, 48, width - cut))], self.own
        )
        pairs = [pair_a, swap(pair_a, 2), pair_b, swap(pair_b, 4)]
        yield
        a, b, again = call(
            functools.partial(first_stack_body, cut, 0),
            [shape((3, 48, cut)), shape((3, 48, width - cut)), shape(self.units.shape[1:])],
            [*self.lines, self.units],
            touch=(pairs[1], pairs[3]),
        )
        stacked = [a, swap(a, 4), b, swap(b, 2)]
        far_one = swap(again, 16)
        joined = self.join(call, 0, stacked)
        line_one = self.pair(call, 1, far_one)
        (own,) = self.finish(call, 0, joined, pairs)
        self.first = [own, swap(own, 1)]
        self.line = {1: line_one}
        self.held = {}
        yield

    def gather_step(self, call, step):
        index = 1 if step in "SJf" else 2
        if step == "P":
            self.line[2] = self.pair(call, 2, self.line[2])
        elif step == "S":
            width, cut = CHUNKS[1]
            a, b, again = call(
                functools.partial(first_stack_body, cut, 1),
                [shape((3, 48, cut)), shape((3, 48, width - cut)), shape(self.units.shape[1:])],
                [*self.line[1], self.units],
            )
            self.held[1] = [a, swap(a, 4), b, swap(b, 2)]
            self.line[2] = swap(again, 16)
        elif step == "s":
            self.held[2] = self.stack(call, 2, self.line[2])
        elif step in "Jj":
            self.held[index] = self.join(call, index, self.held[index])
        else:
            (own,) = self.finish(call, index, self.held[index])
            self.held[index] = [own, swap(own, 1)]

    def starts(self, index):
        return (
            sum(c for _, c in CHUNKS[:index]),
            sum(w - c for w, c in CHUNKS[:index]),
        )

    def stack(self, call, index, line, touch=()):
        width, cut = CHUNKS[index]
        a, b = call(
            functools.partial(stack_body, cut),
            [shape((3, 48, cut)), shape((3, 48, width - cut))],
            line,
            touch=touch,
        )
        return a, swap(a, 4), b, swap(b, 2)

    def join(self, call, index, stacked, touch=()):
        width, cut = CHUNKS[index]
        count = 6 if index == 0 else 8
        a, b = call(
            functools.partial(join_body, *self.starts(index)),
            [shape((count, 48, cut)), shape((count, 48, width - cut))],
            [*stacked] + ([] if index == 0 else self.own),
            touch=touch,
        )
        return a, swap(a, 2), b, swap(b, 4)

    def finish(self, call, index, joined, pairs=()):
        width, cut = CHUNKS[index]
        z = (8, 4, 12) if index else Z_CODES[1:]
        codes_a = z + tuple(c ^ 2 for c in z)
        codes_b = z + tuple(c ^ 1 for c in z)
        if index:
            codes_a, codes_b = (0, 2) + codes_a, (0, 1) + codes_b
        plan = []
        for codes_a, codes_b in [(codes_a, codes_b)] + ([((0, 2), (0, 1))] if pairs else []):
            plan += [
                (codes_a, 0, 0, cut),
                (tuple(c ^ 1 for c in codes_a), 0, 0, cut),
                (codes_b, 0, cut, width - cut),
                (tuple(c ^ 2 for c in codes_b), 0, cut, width - cut),
            ]
        return call(
            functools.partial(place_body, plan),
            [shape((D, width))],
            [*joined, *pairs],
            info=self.info,
            scratch=[pltpu.SemaphoreType.DMA],
        )

    def pieces(self, width_a, width_b):
        return [shape((8, 48, w)) for w in (width_a, width_a, width_b, width_b)]

    def job(self, call, name, parts, body, outs, direct):
        send_a, keep_a, send_b, keep_b = parts
        width_a, width_b = keep_a.shape[2], keep_b.shape[2]
        width = width_a + width_b
        far_a, far_b = swap(send_a, 2), swap(send_b, 4)
        yield
        send_a, keep_a, send_b, keep_b = call(
            first_sum_body,
            [shape((4, 48, w)) for w in (width_a, width_a, width_b, width_b)],
            [far_a, keep_a, far_b, keep_b],
            touch=self.touch,
        )
        far_a, far_b = swap(send_a, 4), swap(send_b, 2)
        yield
        if direct:
            width += 128
            own, *lines = call(
                second_sum_block_body,
                [shape((48, width))] * 4,
                [far_a, keep_a, far_b, keep_b, *self.block],
            )
            lines = [swap(line, bit) for line, bit in zip(lines, (8, 16, 24))]
            yield
            last_body, lines = last_sum_body, [own, *lines]
        else:
            own, send = call(
                second_sum_body, [shape((2, 48, width))] * 2, [far_a, keep_a, far_b, keep_b]
            )
            far = swap(send, 8)
            yield
            own, send = call(near_sum_body, [shape((48, width))] * 2, [own, far])
            far = swap(send, 16)
            yield
            last_body, lines = last_near_body, [own, far]
        mine, other = call(
            last_body,
            [shape((24, width), F32)] * 2,
            lines,
            info=self.info,
            scratch=[pltpu.VMEM((48, width), F32)],
        )
        other = swap(other, 1)
        yield
        self.outs[name] = call(body, outs, [mine, other], info=self.info, last=True)

    def begin(self, job):
        next(job)
        self.jobs.append(job)

    def pump(self, call, index, *touch):
        self.touch = touch
        return next(self.jobs[index], self) is not self

    def block_job(self, call, block):
        send, keep = call(
            block_body, [shape((8, 48, 128), F32)] * 2, [block], info=self.info
        )
        far = swap(send, 2)
        yield
        send, keep = call(block_sum_body, [shape((4, 48, 128), F32)] * 2, [far, keep])
        self.block = [swap(send, 4), keep]
        yield

    def results(self, call):
        (down,), (up,), (qkv, out, vec) = [self.outs[k] for k in ("down", "up", "qkv")]
        return down, up, out, qkv, vec

    def far(self, array):
        return swap(array, 1)

    def reduce_down(self, call, *args):
        self.outs = {}
        parts = call(
            functools.partial(grad_body, 1),
            self.pieces(768, 768),
            args,
            info=self.info,
            scratch=[pltpu.VMEM((D, STEP), LOW)],
            us=6,
        )
        self.begin(self.job(call, "down", parts, merge_one_body, [shape((24, FF), F32)], False))

    def reduce_up(self, call, *args):
        parts = call(
            functools.partial(grad_body, 0),
            self.pieces(768, 768),
            args,
            info=self.info,
            scratch=[pltpu.VMEM((D, STEP), LOW)],
            us=6,
        )
        self.begin(self.job(call, "up", parts, merge_one_body, [shape((24, FF), F32)], False))

    def reduce_qkv(self, call, *args):
        parts = call(
            qkv_grad_body,
            self.pieces(768, 768),
            args,
            info=self.info,
            scratch=[pltpu.VMEM((D, STEP), LOW)],
            us=6,
        )
        outs = [shape((24, 3 * D), F32), shape((24, D), F32), shape((24, 128), F32)]
        self.begin(self.job(call, "qkv", parts, merge_qkv_body, outs, True))

    def reduce_block(self, call, block):
        self.begin(self.block_job(call, block))


def shards(count, tokens, lengths, source, cotangent, w_qkv, w_out, w_up, w_down, *small):
    (
        gain_one, shift_one, bias_query, bias_value, bias_out, gain_two, shift_two,
        bias_up, bias_down,
    ) = small
    seqs, slots = tokens.shape[:2]
    rows = seqs * slots
    share = gain_one.shape[0]
    comm = GridComm() if count == 32 else WholeComm(count)
    visible = jnp.where(source == 1, lengths, IMG_LEN)
    tokens = tokens.reshape(rows, D)
    cotangent = cotangent.reshape(rows, D)
    small = jnp.stack(
        [gain_one, shift_one, gain_two, shift_two, bias_out, bias_down, bias_query, bias_value]
    )
    bias_up = bias_up[None]
    call = Chain([tokens, cotangent, small, bias_up])

    act = shape((rows, D))
    act_f = shape((rows, D), F32)
    half = shape((rows, HALF))
    triple = shape((rows, 3 * HALF))
    wide = shape((rows, WIDE))

    def attend(part, *touch):
        return call(
            functools.partial(attend_body, slots),
            [half, shape((8, 2 * slots), F32)],
            [part],
            info=visible,
            us=4.3,
            touch=touch,
        )

    comm.weights(call, small, bias_up, w_qkv, w_out.T, w_up, w_down.T)
    comm.advance(call)
    dy, dy_sum = call(
        functools.partial(start_body, slots),
        [act, shape((8, D), F32)],
        [cotangent],
        info=visible,
    )
    comm.advance(call)
    for step in EARLY:
        if step == "k":
            normed_one, qkv_own, vecs = call(
                qkv_body,
                [act, triple, shape((16, D), F32)],
                [tokens, comm.first[0]],
                info=comm.info,
                us=4.3,
            )
        elif step == "l":
            o_own, logs_own = attend(qkv_own)
        elif step == "m":
            qkv_par, bias_up = call(
                functools.partial(qkv_far_body, share),
                [triple, shape((1, FF), F32)],
                [normed_one, comm.first[0], comm.first[1], vecs],
                info=comm.info,
                us=2.5,
            )
        elif step == "n":
            o_par, logs_par = attend(qkv_par)
            o_far = comm.far(o_par)
        elif step == "h":
            hidden, normed_two, standard, scales = call(
                hidden_body,
                [act_f, act, act_f, shape((rows, 128), F32)],
                [tokens, vecs, o_own, o_par, *comm.first],
                us=4,
            )
        elif step == "t":
            (near,) = call(
                turn_body, [shape((3 * D, rows))], [normed_two, dy, normed_one], touch=(o_far,), us=3
            )
            far = comm.far(near)
        elif step in "gG":
            flip = 0 if step == "g" else 1
            values = call(
                functools.partial(raise_body, flip),
                [wide] * 2,
                [normed_two, bias_up, comm.held[1][flip]],
                info=comm.info,
                us=3.7,
            )
            if step == "g":
                gated, slope = values
            else:
                gated_par, slope_par = values
                gated_far = comm.far(gated_par)
        elif step == "d":
            comm.reduce_down(call, near, far, gated, gated_far)
        else:
            comm.gather_step(call, step)
    second = comm.held[1]
    third = comm.held[2]
    raised, raised_par, up_sum = call(
        raise_back_body,
        [wide, wide, shape((1, FF), F32)],
        [dy, slope, slope_par, *third],
        info=comm.info,
        us=4.8,
    )
    raised_far = comm.far(raised_par)
    grad_hidden, branch, sums_two = call(
        hidden_back_body,
        [act_f, act, shape((8, D), F32)],
        [dy, standard, scales, vecs, raised, raised_par, *second],
        scratch=[pltpu.VMEM((rows, D), F32)],
        us=6.6,
    )
    branch_far = comm.far(branch)

    def attend_back(part, logs, weight, *touch):
        return call(
            functools.partial(attend_back_body, slots),
            [triple, shape((8, HALF), F32)],
            [part, logs, branch, weight],
            info=visible,
            scratch=[pltpu.VMEM((rows, HALF), LOW)],
            touch=touch,
            us=8.2,
        )

    sums = [branch_far]
    for step in ORDER:
        if step == "p":
            triple_par, sums_par = attend_back(qkv_par, logs_par, comm.first[1])
            triple_far = comm.far(triple_par)
        elif step == "o":
            triple_own, sums_own = attend_back(qkv_own, logs_own, comm.first[0])
        elif step == "u":
            comm.reduce_up(call, near, far, raised, raised_far)
        elif step == "q":
            comm.reduce_qkv(
                call, near, far, triple_own, triple_far, branch, branch_far, o_own, o_far
            )
        elif step == "t":
            grad_tokens, block = call(
                functools.partial(token_back_body, share),
                [act, shape((D, 128), F32)],
                [
                    tokens, grad_hidden, vecs, sums_two, dy_sum, up_sum, sums_own, sums_par,
                    triple_own, triple_par, *comm.first,
                ],
                info=comm.info,
                scratch=[pltpu.VMEM((rows, D), F32), pltpu.VMEM((128, D), F32)],
                us=6.5,
            )
        elif step == "b":
            comm.reduce_block(call, block)
        elif step == "m":
            (output,) = call(
                mix_body, [act], [hidden, vecs, gated, gated_par, *third], us=4.1, last=True
            )
        else:
            comm.pump(call, int(step), *sums)
            sums = []
    g_down_t, g_up, g_out_t, g_qkv, g_vec = comm.results(call)
    (
        g_gain_one, g_shift_one, g_gain_two, g_shift_two, g_bias_out, g_bias_down, g_query, g_value,
    ) = [g_vec[:, i] for i in range(8)]
    return (
        output.reshape(seqs, slots, D),
        grad_tokens.reshape(seqs, slots, D),
        g_qkv,
        g_out_t.T,
        g_up,
        g_down_t.T,
        g_gain_one, g_shift_one, g_query, g_value, g_bias_out, g_gain_two, g_shift_two,
        g_vec[0, UP_LANE : UP_LANE + 4 * share],
        g_bias_down,
    )


def solution(mesh):
    row, tall, wide, vec = P("dp", None, None), P("dp", None), P(None, "dp"), P("dp")
    in_specs = (row, vec, vec, row, tall, wide, tall, wide) + (vec,) * 9
    out_specs = (row, row, tall, wide, tall, wide) + (vec,) * 9
    body = functools.partial(shards, mesh.shape["dp"])
    return jax.shard_map(
        body, mesh=mesh, in_specs=in_specs, out_specs=out_specs, check_vma=False
    )
```
